32 devices in a mesh: dp: 4 (over z), ctx: 2 (over x), tensor: 4 (over y, core).
Axes of the slice: x: 2, y: 2, z: 4, core: 2. Of those that a mesh axis runs over, the one named last changes fastest.
Arguments:
- tokens_in: bfloat16 [4096, 2048], P(('dp', 'ctx')), may hold values from -6 to 6
- cotangent: bfloat16 [4096, 2048], P(('dp', 'ctx')), may hold values from -6 to 6
- seq_lengths: int32 [4, 2], P('dp'), may hold values from 256 to 768, as said below
- block_order: int32 [4, 2, 2], P('dp'), may hold values from 0 to 3, as said below
- gain_one: float32 [2048], replicated, may hold values from 0.5 to 1.5
- down_q: bfloat16 [2048, 1024], P(('dp', 'ctx')), may hold values from -0.125 to 0.125
- gain_q: float32 [1024], replicated, may hold values from 0.5 to 1.5
- up_q: bfloat16 [1024, 4096], P(('dp', 'ctx'), 'tensor'), may hold values from -0.1875 to 0.1875
- key_w: bfloat16 [2048, 256], P(('dp', 'ctx')), may hold values from -0.125 to 0.125
- value_w: bfloat16 [2048, 256], P(('dp', 'ctx')), may hold values from -0.125 to 0.125
- out_w: bfloat16 [2048, 4096], P(('dp', 'ctx'), 'tensor'), may hold values from -0.5 to 0.5
- gain_two: float32 [2048], replicated, may hold values from 0.5 to 1.5
- gate_w: bfloat16 [2048, 5632], P(('dp', 'ctx'), 'tensor'), may hold values from -0.125 to 0.125
- up_w: bfloat16 [2048, 5632], P(('dp', 'ctx'), 'tensor'), may hold values from -0.125 to 0.125
- down_w: bfloat16 [2048, 5632], P(('dp', 'ctx'), 'tensor'), may hold values from -0.078125 to 0.078125
Outputs:
- out_tokens: bfloat16 [4096, 2048], P(('dp', 'ctx'))
- grad_tokens: float32 [4096, 2048], P(('dp', 'ctx'))
- grad_gain_one: float32 [2048], P(('dp', 'ctx'))
- grad_down_q: float32 [2048, 1024], P(('dp', 'ctx'))
- grad_gain_q: float32 [1024], P(('dp', 'ctx'))
- grad_up_q: float32 [1024, 4096], P(('dp', 'ctx'), 'tensor')
- grad_key_w: float32 [2048, 256], P(('dp', 'ctx'))
- grad_value_w: float32 [2048, 256], P(('dp', 'ctx'))
- grad_out_w: float32 [2048, 4096], P(('dp', 'ctx'), 'tensor')
- grad_gain_two: float32 [2048], P(('dp', 'ctx'))
- grad_gate_w: float32 [2048, 5632], P(('dp', 'ctx'), 'tensor')
- grad_up_w: float32 [2048, 5632], P(('dp', 'ctx'), 'tensor')
- grad_down_w: float32 [2048, 5632], P(('dp', 'ctx'), 'tensor')
The draws below stay inside these ranges and needn't reach their ends.
Inputs may be any that keep to these rules, and one draw needn't show every extreme that they name: `seq_lengths`: row g holds the lengths of group g's first and second sequence; they add up to 1024. block_order[g, r] holds r and 3 - r, in either order.
All inputs are finite; a program needn't handle non-finite values.
Results may differ from the reference program's by a relative error of at most 0.017.
Values may be sent and summed in bfloat16 or wider, within the bound.
No kernel may reach another device: no remote copies, remote signals or barrier semaphores. Data moves between devices by JAX's collectives and lax.ppermute only.
A program may use at most 192 MiB of HBM per device.

```python
import jax
import jax.numpy as jnp
from jax import lax

D = 2048
QL = 1024
H = 16
HD = 256
FF = 5632
TOK_DEV = 512
GROUP = 1024
TOKENS = 4096
QH = 4096
N_DP = 4
N_CTX = 2


def draw_seq_lengths(key, part):
    key = jax.random.fold_in(key, 11)
    pick_key = jax.random.fold_in(key, 5)
    first = jax.random.randint(key, (N_DP, 1), GROUP // 4, GROUP - GROUP // 4 + 1)
    chosen = jax.random.randint(pick_key, (), 0, N_DP)
    rows = jnp.arange(N_DP, dtype=jnp.int32)[:, None]
    first = jnp.where(rows == chosen, GROUP // 4, first)
    return jnp.concatenate([first, GROUP - first], axis=1).astype(jnp.int32)


def draw_block_order(key, part):
    key = jax.random.fold_in(key, 23)
    flips = jax.random.randint(key, (N_DP, N_CTX, 1), 0, 2)
    early = jnp.broadcast_to(jnp.arange(N_CTX, dtype=jnp.int32)[None, :, None], (N_DP, N_CTX, 1))
    late = 2 * N_CTX - 1 - early
    first = jnp.where(flips == 1, late, early)
    latter = jnp.where(flips == 1, early, late)
    return jnp.concatenate([first, latter], axis=2).astype(jnp.int32)


def levels(key, extent, pieces, smallest, top_value):
    level, own = 1.0, jax.random.fold_in(key, 6)
    for axis_at, blocks in pieces:
        steps = jnp.exp(jax.random.uniform(jax.random.fold_in(own, axis_at), (blocks,), jnp.float32, smallest / len(pieces), top_value / len(pieces)))
        level = level * jnp.repeat(steps, extent[axis_at] // blocks).reshape([-1 if axis == axis_at else 1 for axis in range(len(extent))])
    return level


def scatter_about(own_key, shape, deviation, reach, split=(), kind=jnp.bfloat16):
    drawn = jax.random.normal(own_key, shape, jnp.float32) * deviation
    if len(split) > 0:
        drawn = levels(own_key, shape, split, -0.22, 0.18) * drawn
    return jnp.clip(drawn, min=-reach, max=reach).astype(kind)


def setup_inputs(seed: int = 0) -> dict:
    seeds = jax.random.split(jax.random.key(seed), 16)
    tokens_in = scatter_about(seeds[0], (TOKENS, D), 1.0, 6.0, ((0, 8),))
    cotangent = scatter_about(seeds[1], (TOKENS, D), 1.0, 6.0, ((0, 8),))
    seq_lengths = draw_seq_lengths(jax.random.fold_in(seeds[15], 71), 0)
    block_order = draw_block_order(jax.random.fold_in(seeds[15], 71), 0)
    gain_one = jnp.clip(1.0 + 0.1 * jax.random.normal(seeds[4], (D,), jnp.float32), 0.5, 1.5)
    down_q = scatter_about(seeds[5], (D, QL), D ** -0.5, 0.125, ((0, 8),))
    gain_q = jnp.clip(1.0 + 0.1 * jax.random.normal(seeds[6], (QL,), jnp.float32), 0.5, 1.5)
    up_q = scatter_about(seeds[7], (QL, QH), QL ** -0.5, 0.1875, ((0, 8), (1, 4)))
    key_w = scatter_about(seeds[8], (D, HD), D ** -0.5, 0.125, ((0, 8),))
    value_w = scatter_about(seeds[9], (D, HD), D ** -0.5, 0.125, ((0, 8),))
    out_w = scatter_about(seeds[10], (D, QH), (QH // 32) ** -0.5, 0.5, ((0, 8), (1, 4)))
    gain_two = jnp.clip(1.0 + 0.1 * jax.random.normal(seeds[11], (D,), jnp.float32), 0.5, 1.5)
    gate_w = scatter_about(seeds[12], (D, FF), D ** -0.5, 0.125, ((0, 8), (1, 4)))
    up_w = scatter_about(seeds[13], (D, FF), D ** -0.5, 0.125, ((0, 8), (1, 4)))
    down_w = scatter_about(seeds[14], (D, FF), FF ** -0.5, 0.078125, ((0, 8), (1, 4)))
    return {"tokens_in": tokens_in, "cotangent": cotangent, "seq_lengths": seq_lengths, "block_order": block_order, "gain_one": gain_one, "down_q": down_q, "gain_q": gain_q, "up_q": up_q, "key_w": key_w, "value_w": value_w, "out_w": out_w, "gain_two": gain_two, "gate_w": gate_w, "up_w": up_w, "down_w": down_w}


@jax.custom_vjp
def low(v):
    return lax.optimization_barrier(v.astype(jnp.bfloat16)).astype(jnp.float32)

@jax.custom_vjp
def low_back(v):
    return v

def low_keep(v):
    return (low(v), None)

def low_pass(kept, grad):
    return (grad,)

def back_keep(v):
    return (v, None)

def back_low(kept, grad):
    return (low(grad),)
low.defvjp(low_keep, low_pass)
low_back.defvjp(back_keep, back_low)
EPSILON = 1e-06
PRECISE = lax.Precision.HIGHEST

def product(left, right):
    return jnp.dot(left, right, precision=PRECISE, preferred_element_type=jnp.float32)

def rms_scale(array, gain):
    return array * lax.rsqrt(lax.optimization_barrier(jnp.mean(array * array, axis=-1, keepdims=True)) + EPSILON) * gain

def rotate(array, places):
    half = array.shape[-1] // 2
    freqs = 10000.0 ** (-jnp.arange(half, dtype=jnp.float32) / half)
    angles = places[:, None] * freqs[None, :]
    cosine = jnp.cos(angles)
    sine = jnp.sin(angles)
    first = array[..., :half]
    latter = array[..., half:]
    return jnp.concatenate([first * cosine - latter * sine, latter * cosine + first * sine], axis=-1)

def layout(order, lengths):
    block_rows = TOK_DEV // 2
    places = (order[:, :, None] * block_rows + jnp.arange(block_rows, dtype=jnp.int32)[None, None, :]).reshape(-1)
    second = (places >= lengths[0]).astype(jnp.int32)
    in_sequence = places - second * lengths[0]
    return (places, second, in_sequence)

def group_forward(token_rows, order, lengths, weights):
    gain_one, down_q, gain_q, up_q, key_w, value_w, out_w, gain_two, gate_w, up_w, down_w = weights
    places, second, in_sequence = layout(order, lengths)
    angle_pos = in_sequence.astype(jnp.float32)
    normed = low(rms_scale(token_rows, gain_one))
    latent = low_back(product(normed, down_q))
    query_in = low(rms_scale(latent, gain_q))
    query_pre = low_back(product(query_in, up_q))
    query = query_pre.reshape(-1, H, HD).transpose(1, 0, 2)
    query = low(rotate(query, angle_pos))
    keys = low(rotate(low_back(product(normed, key_w)), angle_pos))
    values = low(low_back(product(normed, value_w)))
    allowed = (second[:, None] == second[None, :]) & (places[None, :] <= places[:, None])

    def one_head(q_head):
        scores = low_back(product(q_head, keys.T) * HD ** (-0.5))
        scores = jnp.where(allowed, scores, -1e+30)
        soft = jax.nn.softmax(scores, axis=-1)
        return product(low(soft), values)
    mixed_heads = lax.map(jax.checkpoint(one_head), query)
    attended = low(low_back(mixed_heads.transpose(1, 0, 2).reshape(-1, H * HD)))
    branch = low_back(product(attended, out_w.T))
    middle = token_rows + branch
    normed_two = low(rms_scale(middle, gain_two))
    gate_pre = low_back(product(normed_two, gate_w))
    up_pre = low_back(product(normed_two, up_w))
    hidden = low(jax.nn.silu(gate_pre) * up_pre)
    return middle + product(hidden, down_w.T)

def reference(tokens_in, cotangent, seq_lengths, block_order, gain_one, down_q, gain_q, up_q, key_w, value_w, out_w, gain_two, gate_w, up_w, down_w):
    weights = tuple((w.astype(jnp.float32) for w in (gain_one, down_q, gain_q, up_q, key_w, value_w, out_w, gain_two, gate_w, up_w, down_w)))
    token_rows = tokens_in.astype(jnp.float32).reshape(N_DP, GROUP, D)
    grad_rows = cotangent.astype(jnp.float32).reshape(N_DP, GROUP, D)

    def forward_all(all_rows, all_weights):

        def one_group(item):
            return jax.checkpoint(group_forward)(item[0], item[1], item[2], all_weights)
        return lax.map(one_group, (all_rows, block_order, seq_lengths))
    outputs, pullback = jax.vjp(forward_all, token_rows, weights)
    grad_in, grad_weights = pullback(grad_rows)
    return (outputs.reshape(TOKENS, D).astype(jnp.bfloat16), grad_in.reshape(TOKENS, D), grad_weights[0], grad_weights[1], grad_weights[2], grad_weights[3], grad_weights[4], grad_weights[5], grad_weights[6], grad_weights[7], grad_weights[8], grad_weights[9], grad_weights[10])
```

```python
import jax
import jax.numpy as jnp
from jax import lax
from jax.experimental import pallas as pl
from jax.experimental.pallas import tpu as pltpu
from jax.sharding import PartitionSpec as P

HD = 256


EPSILON = 1e-06

AXES = ("dp", "ctx", "tensor")
BF = jnp.bfloat16
F32 = jnp.float32


def dot(left, right):
    return jnp.dot(left, right, preferred_element_type=F32)


def times_trans(left, right):
    return lax.dot_general(left, right, (((1,), (1,)), ((), ())), preferred_element_type=F32)


def trans_times(left, right):
    return lax.dot_general(left, right, (((0,), (0,)), ((), ())), preferred_element_type=F32)


def rms_parts(array):
    inverse = lax.rsqrt(jnp.mean(array * array, axis=-1, keepdims=True) + EPSILON)
    return (array * inverse, inverse)


def rms_back(grad_out, plain, inverse, gain):
    grad_plain = grad_out * gain
    grad_in = inverse * (grad_plain - plain * jnp.mean(grad_plain * plain, axis=-1, keepdims=True))
    return (grad_in, jnp.sum(grad_out * plain, axis=0))


def angles_of(places, half):
    freqs = 10000.0 ** (-jnp.arange(half, dtype=F32) / half)
    angles = places[:, None] * freqs[None, :]
    return (jnp.cos(angles), jnp.sin(angles))


def turn(array, cosine, sine):
    half = array.shape[-1] // 2
    first = array[..., :half]
    latter = array[..., half:]
    return jnp.concatenate(
        [first * cosine - latter * sine, latter * cosine + first * sine], axis=-1
    )


def routes(move):
    pairs = []
    for z in range(4):
        for x in range(2):
            for y in range(2):
                for c in range(2):
                    to = move(z, x, y, c)
                    if to is not None:
                        tz, tx, ty, tc = to
                        pairs.append(
                            (((z * 2 + x) * 2 + y) * 2 + c, ((tz * 2 + tx) * 2 + ty) * 2 + tc)
                        )
    return pairs


OVER_X = routes(lambda z, x, y, c: (z, 1 - x, y, c))
OVER_Y = routes(lambda z, x, y, c: (z, x, 1 - y, c))
OVER_XY = routes(lambda z, x, y, c: (z, 1 - x, 1 - y, c))
OVER_C = routes(lambda z, x, y, c: (z, x, y, 1 - c))
TRANSPOSE = routes(lambda z, x, y, c: (z, c, y, x))
Z_ONE = routes(lambda z, x, y, c: (z ^ 1, x, y, c))
Z_TWO = routes(lambda z, x, y, c: (z ^ 2, x, y, c))
Z_THREE = routes(lambda z, x, y, c: (z ^ 3, x, y, c))
Z_INNER = routes(lambda z, x, y, c: (3 - z, x, y, c) if z in (1, 2) else None)
Z_OUTWARD = routes(lambda z, x, y, c: ({1: 0, 2: 3}[z], x, y, c) if z in (1, 2) else None)
Z_INWARD = routes(lambda z, x, y, c: ({0: 1, 3: 2}[z], x, y, c) if z in (0, 3) else None)


def send(array, pairs):
    return lax.ppermute(array, AXES, pairs)


def gather_z(array, inner):
    one = send(array, Z_ONE)
    two = send(array, Z_TWO)
    middle = send(array, Z_INNER)
    passed = send(two, Z_OUTWARD)
    three = jnp.where(inner, middle, passed)
    return [array, one, two, three]


def reduce_z(slabs):
    own, one, two, three = slabs
    passed = send(three, Z_INWARD)
    got_one = send(one, Z_ONE)
    got_three = send(three, Z_INNER)
    got_two = send((two.astype(F32) + passed.astype(F32)).astype(BF), Z_TWO)
    return own.astype(F32) + got_one.astype(F32) + got_two.astype(F32) + got_three.astype(F32)


def extract_columns(array, block, picks):
    rows = array.shape[0]
    count = picks.shape[0]

    def body(picks_ref, in_ref, out_ref):
        out_ref[...] = in_ref[...]

    return pl.pallas_call(
        body,
        grid_spec=pltpu.PrefetchScalarGridSpec(
            num_scalar_prefetch=1,
            grid=(count,),
            in_specs=[pl.BlockSpec((rows, block), lambda i, picks_ref: (0, picks_ref[i]))],
            out_specs=pl.BlockSpec((rows, block), lambda i, picks_ref: (0, i)),
        ),
        out_shape=jax.ShapeDtypeStruct((rows, count * block), array.dtype),
        cost_estimate=pl.CostEstimate(
            flops=0, bytes_accessed=2 * rows * count * block * 2, transcendentals=0
        ),
    )(picks, array)


def assemble_rows(blocks, picks):
    rows, columns = blocks[0].shape
    count = len(blocks)

    def body(picks_ref, *refs):
        ins = refs[:count]
        out_ref = refs[count]
        sems = refs[count + 1]
        copies = []
        for i in range(count):
            start = pl.multiple_of(picks_ref[i] * rows, rows)
            copy = pltpu.make_async_copy(ins[i], out_ref.at[pl.ds(start, rows)], sems.at[i])
            copy.start()
            copies.append(copy)
        for copy in copies:
            copy.wait()

    return pl.pallas_call(
        body,
        grid_spec=pltpu.PrefetchScalarGridSpec(
            num_scalar_prefetch=1,
            grid=(1,),
            in_specs=[pl.BlockSpec(memory_space=pl.ANY)] * count,
            out_specs=pl.BlockSpec((count * rows, columns), lambda i, picks_ref: (0, 0)),
            scratch_shapes=[pltpu.SemaphoreType.DMA((count,))],
        ),
        out_shape=jax.ShapeDtypeStruct((count * rows, columns), blocks[0].dtype),
        compiler_params=pltpu.CompilerParams(vmem_limit_bytes=40 * 1024 * 1024),
        cost_estimate=pl.CostEstimate(
            flops=0, bytes_accessed=4 * rows * count * columns, transcendentals=0
        ),
    )(picks, *blocks)


def rows_at(array, start, count):
    return lax.dynamic_slice_in_dim(array, start, count, axis=0)


def both(own, other, index):
    return jnp.where(
        index == 0, jnp.concatenate([own, other], 0), jnp.concatenate([other, own], 0)
    )


def both_columns(own, other, index):
    return jnp.where(
        index == 0, jnp.concatenate([own, other], 1), jnp.concatenate([other, own], 1)
    )


def plane_reduce(partial, quarter):
    part = partial.shape[0] // 4
    low = partial.astype(BF)

    def piece(flip):
        return rows_at(low, (quarter ^ flip) * part, part)

    got_x = send(piece(2), OVER_X)
    got_y = send(piece(1), OVER_Y)
    got_xy = send(piece(3), OVER_XY)
    return (
        rows_at(partial, quarter * part, part).astype(F32)
        + got_x.astype(F32)
        + got_y.astype(F32)
        + got_xy.astype(F32)
    )


def plane_gather(part, quarter_picks):
    got_x = send(part, OVER_X)
    got_y = send(part, OVER_Y)
    got_xy = send(part, OVER_XY)
    return assemble_rows([part, got_y, got_x, got_xy], quarter_picks)


def fast_device(
    tokens_in,
    cotangent,
    seq_lengths,
    block_order,
    gain_one,
    down_q,
    gain_q,
    up_q,
    key_w,
    value_w,
    out_w,
    gain_two,
    gate_w,
    up_w,
    down_w,
):
    z = lax.axis_index("dp")
    x = lax.axis_index("ctx")
    t = lax.axis_index("tensor")
    y = t // 2
    c = t % 2
    inner = (z == 1) | (z == 2)
    quarter = x * 2 + y
    ks = jnp.arange(4, dtype=jnp.int32)
    z_order = z ^ ks
    own_blocks = z_order * 2 + c
    other_blocks = z_order * 2 + (1 - c)
    all_blocks = jnp.concatenate([own_blocks, other_blocks])
    x_blocks = z_order * 2 + x
    x_all_blocks = jnp.concatenate([x_blocks, z_order * 2 + (1 - x)])
    quarter_picks = quarter ^ ks
    rows = tokens_in.shape[0]
    half = rows // 2
    part = rows // 4
    latent_width = down_q.shape[1]

    first_w = jnp.concatenate([down_q, key_w, value_w], axis=1)
    wide = first_w.shape[1]
    side = wide // 2
    mine = lax.dynamic_slice_in_dim(first_w, c * side, side, axis=1)
    tok_half = rows_at(tokens_in, c * half, half)
    tok_got = send(tok_half, OVER_X)
    mine_all = gather_z(mine, inner)
    over_all = [send(w, OVER_X) for w in mine_all]
    tok_other = both(tok_got, send(tok_got, OVER_C), c)
    tokens = both(tokens_in, tok_other, x)
    own_side = jnp.concatenate(mine_all + over_all, axis=0)
    other_side = send(own_side, OVER_C)
    first_all = both_columns(own_side, other_side, c)
    first_all = assemble_rows(
        [first_all[i * 256 : (i + 1) * 256] for i in range(8)], x_all_blocks
    )

    upq_t = send(up_q, TRANSPOSE)
    upq_all = gather_z(upq_t, inner)
    cols = up_q.shape[1] // 2

    def head_side(blocks):
        keep = [lax.dynamic_slice_in_dim(w, c * cols, cols, axis=1) for w in blocks]
        give = [lax.dynamic_slice_in_dim(w, (1 - c) * cols, cols, axis=1) for w in blocks]
        got = [send(w, OVER_C) for w in give]
        return assemble_rows(keep + got, all_blocks)

    up_q_all = head_side(upq_all)
    out_t = send(out_w, TRANSPOSE)
    out_all = head_side(gather_z(out_t, inner))

    def ffn_weight(w):
        own = gather_z(send(w, TRANSPOSE), inner)
        got = [send(v, OVER_C) for v in own]
        return assemble_rows(own + got, all_blocks)

    gate_all = ffn_weight(gate_w)
    up_all = ffn_weight(up_w)
    down_all = ffn_weight(down_w)

    cot_got = send(rows_at(cotangent, c * half, half), OVER_X)
    cot_other = both(cot_got, send(cot_got, OVER_C), c)
    cot = both(cotangent, cot_other, x)

    block_rows = rows // 2
    places = (
        block_order[0][:, :, None] * block_rows
        + jnp.arange(block_rows, dtype=jnp.int32)[None, None, :]
    ).reshape(-1)
    second = (places >= seq_lengths[0, 0]).astype(jnp.int32)
    pos = (places - second * seq_lengths[0, 0]).astype(F32)
    allowed = (second[:, None] == second[None, :]) & (places[None, :] <= places[:, None])
    cosine, sine = angles_of(pos, HD // 2)
    scale = HD ** (-0.5)

    plain_one, inverse_one = rms_parts(tokens.astype(F32))
    normed = (plain_one * gain_one).astype(BF)
    lat = dot(normed, first_all)
    latent = lat[:, :latent_width]
    plain_q, inverse_q = rms_parts(latent)
    query_in = (plain_q * gain_q).astype(BF)
    keys = turn(lat[:, latent_width : latent_width + HD], cosine, sine).astype(BF)
    values = lat[:, latent_width + HD :].astype(BF)
    query_pre = dot(query_in, up_q_all)
    heads = cols // HD
    queries = []
    softs = []
    mixed = []
    for h in range(heads):
        q = turn(query_pre[:, h * HD : (h + 1) * HD], cosine, sine).astype(BF)
        scores = jnp.where(allowed, times_trans(q, keys) * scale, -1e30)
        largest = jnp.max(scores, axis=-1, keepdims=True)
        exponent = jnp.exp(scores - largest)
        soft = exponent / jnp.sum(exponent, axis=-1, keepdims=True)
        queries.append(q)
        softs.append(soft)
        mixed.append(dot(soft.astype(BF), values).astype(BF))
    attended = jnp.concatenate(mixed, axis=1)
    give = times_trans(rows_at(attended, (1 - c) * rows, rows), out_all).astype(BF)
    keep = times_trans(rows_at(attended, c * rows, rows), out_all)
    branch = keep + send(give, OVER_C).astype(F32)
    own_row = c * rows + quarter * part
    middle = rows_at(tokens, own_row, part).astype(F32) + plane_reduce(branch, quarter)

    plain_two, inverse_two = rms_parts(middle)
    normed_two = plane_gather((plain_two * gain_two).astype(BF), quarter_picks)
    gate_pre = dot(normed_two, gate_all)
    up_pre = dot(normed_two, up_all)
    sigma = jax.nn.sigmoid(gate_pre)
    silu = gate_pre * sigma
    hidden = (silu * up_pre).astype(BF)
    cot_c = rows_at(cot, c * rows, rows)
    grad_hidden = dot(cot_c, down_all)
    grad_gate = (grad_hidden * up_pre * sigma * (1.0 + gate_pre * (1.0 - sigma))).astype(BF)
    grad_up = (grad_hidden * silu).astype(BF)
    grad_norm_two = plane_reduce(
        times_trans(grad_gate, gate_all) + times_trans(grad_up, up_all), quarter
    )
    out_part = middle + plane_reduce(times_trans(hidden, down_all), quarter)
    out_c = plane_gather(out_part.astype(BF), quarter_picks)
    result = jnp.where(x == c, out_c, send(out_c, OVER_C))

    def with_other(array):
        return jnp.concatenate([array, send(array, OVER_C)], axis=0)

    def own_half(array):
        mine_cols = extract_columns(array, 256, own_blocks)
        give_cols = extract_columns(array, 256, other_blocks)
        return jnp.concatenate([mine_cols, send(give_cols, OVER_C)], axis=0)

    def slabs_of(grad):
        low = grad.astype(BF)
        n = low.shape[0] // 4
        return [low[i * n : (i + 1) * n] for i in range(4)]

    def home(grad):
        return send(reduce_z(slabs_of(grad)).astype(BF), TRANSPOSE).astype(F32)

    cot_own = jnp.concatenate(
        [
            extract_columns(cot_c, 256, own_blocks),
            extract_columns(rows_at(cot, (1 - c) * rows, rows), 256, own_blocks),
        ],
        axis=0,
    )
    grad_down_w = home(trans_times(cot_own, with_other(hidden)))
    normed_two_own = own_half(normed_two)
    grad_gate_w = home(trans_times(normed_two_own, with_other(grad_gate)))
    grad_up_w = home(trans_times(normed_two_own, with_other(grad_up)))

    cot_mine = rows_at(cot, own_row, part).astype(F32)
    grad_mid, gain_two_part = rms_back(grad_norm_two, plain_two, inverse_two, gain_two)
    grad_branch_c = plane_gather((cot_mine + grad_mid).astype(BF), quarter_picks)
    grad_branch = both(grad_branch_c, send(grad_branch_c, OVER_C), c)
    grad_attended = dot(grad_branch, out_all).astype(BF)
    key_acc = 0.0
    value_acc = 0.0
    grad_queries = []
    for h in range(heads):
        grad_head = grad_attended[:, h * HD : (h + 1) * HD]
        soft = softs[h]
        grad_soft = times_trans(grad_head, values)
        summed = jnp.sum(soft * grad_soft, axis=-1, keepdims=True)
        grad_scores = (soft * (grad_soft - summed)).astype(BF)
        grad_q = dot(grad_scores, keys) * scale
        key_acc = key_acc + trans_times(grad_scores, queries[h]) * scale
        value_acc = value_acc + trans_times(soft.astype(BF), grad_head)
        grad_queries.append(turn(grad_q, cosine, -sine).astype(BF))
    grad_query_pre = jnp.concatenate(grad_queries, axis=1)
    grad_qin = times_trans(grad_query_pre, up_q_all)
    low_three = jnp.concatenate([grad_qin, key_acc, value_acc], axis=1).astype(BF)
    got_three = send(rows_at(low_three, (1 - c) * rows, rows), OVER_C)
    three = rows_at(low_three, c * rows, rows).astype(F32) + got_three.astype(F32)
    three = plane_reduce(three, quarter)
    plain_q_mine = rows_at(plain_q, own_row, part)
    inverse_q_mine = rows_at(inverse_q, own_row, part)
    grad_latent, gain_q_part = rms_back(
        three[:, :latent_width], plain_q_mine, inverse_q_mine, gain_q
    )
    grad_key_pre = turn(
        three[:, latent_width : latent_width + HD],
        rows_at(cosine, own_row, part),
        -rows_at(sine, own_row, part),
    )
    low_lat = jnp.concatenate(
        [grad_latent, grad_key_pre, three[:, latent_width + HD :]], axis=1
    ).astype(BF)
    low_lat_c = plane_gather(low_lat, quarter_picks)
    grad_lat = both(low_lat_c, send(low_lat_c, OVER_C), c)

    grad_lat_x = rows_at(grad_lat, x * rows, rows)
    grad_norm_one = times_trans(grad_lat_x, first_all)
    grad_in, gain_one_part = rms_back(
        grad_norm_one, rows_at(plain_one, x * rows, rows), rows_at(inverse_one, x * rows, rows), gain_one
    )
    grad_tokens = rows_at(grad_branch, x * rows, rows).astype(F32) + grad_in

    attended_all = both_columns(attended, send(attended, OVER_C), c)
    grad_out_w = home(trans_times(extract_columns(grad_branch, 256, own_blocks), attended_all))
    query_pre_all = both_columns(grad_query_pre, send(grad_query_pre, OVER_C), c)
    grad_up_q = home(trans_times(extract_columns(query_in, 128, own_blocks), query_pre_all))
    lane = wide // 4
    grad_lat_t = lax.dynamic_slice_in_dim(grad_lat, t * lane, lane, axis=1)
    first_quarter = reduce_z(
        slabs_of(trans_times(extract_columns(normed, 256, x_blocks), grad_lat_t))
    ).astype(BF)
    first_half = both_columns(first_quarter, send(first_quarter, OVER_C), c)
    grad_first = both_columns(first_half, send(first_half, OVER_Y), y).astype(F32)

    gains = lax.psum(
        jnp.concatenate([gain_two_part, gain_q_part, gain_one_part * 0.25]), AXES
    )
    dev = z * 2 + x
    d = gain_one.shape[0]
    grad_gain_two = lax.dynamic_slice_in_dim(gains, dev * (d // 8), d // 8)
    grad_gain_q = lax.dynamic_slice_in_dim(
        gains, d + dev * (latent_width // 8), latent_width // 8
    )
    grad_gain_one = lax.dynamic_slice_in_dim(
        gains, d + latent_width + dev * (d // 8), d // 8
    )

    return (
        result,
        grad_tokens,
        grad_gain_one,
        grad_first[:, :latent_width],
        grad_gain_q,
        grad_up_q,
        grad_first[:, latent_width : latent_width + HD],
        grad_first[:, latent_width + HD :],
        grad_out_w,
        grad_gain_two,
        grad_gate_w,
        grad_up_w,
        grad_down_w,
    )


def rotate(array, places):
    half = array.shape[-1] // 2
    freqs = 10000.0 ** (-jnp.arange(half, dtype=jnp.float32) / half)
    angles = places[:, None] * freqs[None, :]
    cosine = jnp.cos(angles)
    sine = jnp.sin(angles)
    first = array[..., :half]
    latter = array[..., half:]
    return jnp.concatenate(
        [first * cosine - latter * sine, latter * cosine + first * sine], axis=-1
    )


def forward(token_rows, attention_w, ffn_w, gains, own_pos, allowed):
    gain_one, gain_q, gain_two = gains
    down_q, up_q, key_w, value_w, out_w = attention_w
    gate_w, up_w, down_w = ffn_w
    row_count = token_rows.shape[0]
    heads = up_q.shape[1] // HD
    scale = HD ** (-0.5)
    plain_one, inverse_one = rms_parts(token_rows)
    normed = (plain_one * gain_one).astype(jnp.bfloat16)
    latent = jnp.dot(normed, down_q, preferred_element_type=jnp.float32)
    plain_q, inverse_q = rms_parts(latent)
    query_in = (plain_q * gain_q).astype(jnp.bfloat16)
    query_pre = jnp.dot(query_in, up_q, preferred_element_type=jnp.float32)
    query = rotate(query_pre.reshape(row_count, heads, HD).transpose(1, 0, 2), own_pos).astype(
        jnp.bfloat16
    )
    keys = rotate(jnp.dot(normed, key_w, preferred_element_type=jnp.float32), own_pos).astype(
        jnp.bfloat16
    )
    values = jnp.dot(normed, value_w, preferred_element_type=jnp.float32).astype(jnp.bfloat16)
    keys_all, values_all = (
        lax.all_gather(keys, "ctx", axis=0, tiled=True),
        lax.all_gather(values, "ctx", axis=0, tiled=True),
    )

    def one_head(q_head):
        scores = jnp.where(allowed, times_trans(q_head, keys_all) * scale, -1e30)
        largest = jnp.max(scores, axis=-1, keepdims=True)
        exponent = jnp.exp(scores - largest)
        totals = jnp.sum(exponent, axis=-1, keepdims=True)
        soft = (exponent / totals).astype(jnp.bfloat16)
        return (
            jnp.dot(soft, values_all, preferred_element_type=jnp.float32),
            (largest + jnp.log(totals))[:, 0],
        )

    mixed_heads, log_totals = lax.map(one_head, query)
    attended = mixed_heads.transpose(1, 0, 2).reshape(row_count, heads * HD).astype(jnp.bfloat16)
    branch = lax.psum(times_trans(attended, out_w), "tensor")
    middle = token_rows + branch
    plain_two, inverse_two = rms_parts(middle)
    normed_two = (plain_two * gain_two).astype(jnp.bfloat16)
    gate_pre = jnp.dot(normed_two, gate_w, preferred_element_type=jnp.float32)
    up_pre = jnp.dot(normed_two, up_w, preferred_element_type=jnp.float32)
    hidden = (jax.nn.silu(gate_pre) * up_pre).astype(jnp.bfloat16)
    result = middle + lax.psum(times_trans(hidden, down_w).astype(jnp.bfloat16), "tensor").astype(
        jnp.float32
    )
    kept_values = (
        plain_one,
        inverse_one,
        normed,
        plain_q,
        inverse_q,
        query_in,
        query,
        keys_all,
        values_all,
        log_totals,
        attended,
        plain_two,
        inverse_two,
        normed_two,
        gate_pre,
        up_pre,
        hidden,
    )
    return (result, kept_values)


def backward(cotangent, attention_w, ffn_w, gains, own_pos, allowed, kept_values):
    gain_one, gain_q, gain_two = gains
    down_q, up_q, key_w, value_w, out_w = attention_w
    gate_w, up_w, down_w = ffn_w
    (
        plain_one,
        inverse_one,
        normed,
        plain_q,
        inverse_q,
        query_in,
        query,
        keys_all,
        values_all,
        log_totals,
        attended,
        plain_two,
        inverse_two,
        normed_two,
        gate_pre,
        up_pre,
        hidden,
    ) = kept_values
    row_count = cotangent.shape[0]
    heads = query.shape[0]
    scale = HD ** (-0.5)
    grad_down = trans_times(cotangent, hidden)
    grad_hidden = jnp.dot(cotangent, down_w, preferred_element_type=jnp.float32)
    sigma = jax.nn.sigmoid(gate_pre)
    grad_gate = (grad_hidden * up_pre * sigma * (1.0 + gate_pre * (1.0 - sigma))).astype(
        jnp.bfloat16
    )
    grad_up = (grad_hidden * gate_pre * sigma).astype(jnp.bfloat16)
    grad_gate_w = trans_times(normed_two, grad_gate)
    grad_up_w = trans_times(normed_two, grad_up)
    grad_norm_two = lax.psum(times_trans(grad_gate, gate_w) + times_trans(grad_up, up_w), "tensor")
    grad_mid_part, grad_gain_two = rms_back(grad_norm_two, plain_two, inverse_two, gain_two)
    ffn_grads = (
        lax.psum_scatter(grad_gate_w, ("dp", "ctx"), scatter_dimension=0, tiled=True),
        lax.psum_scatter(grad_up_w, ("dp", "ctx"), scatter_dimension=0, tiled=True),
        lax.psum_scatter(grad_down, ("dp", "ctx"), scatter_dimension=0, tiled=True),
        lax.psum_scatter(grad_gain_two, ("dp", "ctx"), scatter_dimension=0, tiled=True),
    )
    grad_middle = cotangent.astype(jnp.float32) + grad_mid_part
    grad_branch = grad_middle.astype(jnp.bfloat16)
    grad_out_w = trans_times(grad_branch, attended)
    grad_attended = jnp.dot(grad_branch, out_w, preferred_element_type=jnp.float32).astype(
        jnp.bfloat16
    )
    grad_heads = grad_attended.reshape(row_count, heads, HD).transpose(1, 0, 2)

    def head_back(carry, item):
        key_acc, value_acc = carry
        q_head, grad_head, lse_head = item
        scores = jnp.where(allowed, times_trans(q_head, keys_all) * scale, -1e30)
        soft = jnp.exp(scores - lse_head[:, None])
        grad_soft = times_trans(grad_head, values_all)
        inner = jnp.sum(soft * grad_soft, axis=-1, keepdims=True)
        grad_scores = (soft * (grad_soft - inner)).astype(jnp.bfloat16)
        grad_q = jnp.dot(grad_scores, keys_all, preferred_element_type=jnp.float32) * scale
        key_acc = key_acc + trans_times(grad_scores, q_head) * scale
        value_acc = value_acc + trans_times(soft.astype(jnp.bfloat16), grad_head)
        return ((key_acc, value_acc), grad_q)

    empty = jnp.zeros(keys_all.shape, jnp.float32)
    (key_total, value_total), grad_query = lax.scan(
        head_back, (empty, empty), (query, grad_heads, log_totals)
    )
    key_own, value_own = (
        lax.psum_scatter(key_total, "ctx", scatter_dimension=0, tiled=True),
        lax.psum_scatter(value_total, "ctx", scatter_dimension=0, tiled=True),
    )
    grad_query_pre = (
        rotate(grad_query, -own_pos)
        .transpose(1, 0, 2)
        .reshape(row_count, heads * HD)
        .astype(jnp.bfloat16)
    )
    grad_up_q = trans_times(query_in, grad_query_pre)
    grad_qin_part = times_trans(grad_query_pre, up_q)
    grad_qin, grad_keys_rot, grad_values = lax.psum((grad_qin_part, key_own, value_own), "tensor")
    grad_key_pre = rotate(grad_keys_rot, -own_pos).astype(jnp.bfloat16)
    grad_value_low = grad_values.astype(jnp.bfloat16)
    grad_latent, grad_gain_q = rms_back(grad_qin, plain_q, inverse_q, gain_q)
    grad_latent_low = grad_latent.astype(jnp.bfloat16)
    grad_down_q = trans_times(normed, grad_latent_low)
    grad_key_w = trans_times(normed, grad_key_pre)
    grad_value_w = trans_times(normed, grad_value_low)
    grad_norm_one = (
        times_trans(grad_latent_low, down_q)
        + times_trans(grad_key_pre, key_w)
        + times_trans(grad_value_low, value_w)
    )
    grad_in_part, grad_gain_one = rms_back(grad_norm_one, plain_one, inverse_one, gain_one)
    grad_tokens = grad_middle + grad_in_part
    attention_grads = (
        lax.psum_scatter(grad_gain_one, ("dp", "ctx"), scatter_dimension=0, tiled=True),
        lax.psum_scatter(grad_down_q, ("dp", "ctx"), scatter_dimension=0, tiled=True),
        lax.psum_scatter(grad_gain_q, ("dp", "ctx"), scatter_dimension=0, tiled=True),
        lax.psum_scatter(grad_up_q, ("dp", "ctx"), scatter_dimension=0, tiled=True),
        lax.psum_scatter(grad_key_w, ("dp", "ctx"), scatter_dimension=0, tiled=True),
        lax.psum_scatter(grad_value_w, ("dp", "ctx"), scatter_dimension=0, tiled=True),
        lax.psum_scatter(grad_out_w, ("dp", "ctx"), scatter_dimension=0, tiled=True),
    )
    return (grad_tokens, attention_grads, ffn_grads)


def per_device(
    tokens_in,
    cotangent,
    seq_lengths,
    block_order,
    gain_one,
    down_q,
    gain_q,
    up_q,
    key_w,
    value_w,
    out_w,
    gain_two,
    gate_w,
    up_w,
    down_w,
):
    token_rows = tokens_in.astype(jnp.float32)
    row_count = tokens_in.shape[0]
    block_rows = row_count // 2
    places = (
        block_order[0][:, :, None] * block_rows
        + jnp.arange(block_rows, dtype=jnp.int32)[None, None, :]
    ).reshape(-1)
    second = (places >= seq_lengths[0, 0]).astype(jnp.int32)
    in_sequence = places - second * seq_lengths[0, 0]
    start = lax.axis_index("ctx") * row_count
    own_places = lax.dynamic_slice_in_dim(places, start, row_count)
    own_second = lax.dynamic_slice_in_dim(second, start, row_count)
    own_pos = lax.dynamic_slice_in_dim(in_sequence, start, row_count).astype(jnp.float32)
    allowed = (own_second[:, None] == second[None, :]) & (places[None, :] <= own_places[:, None])
    gains = (gain_one, gain_q, gain_two)
    attention_w = (
        lax.all_gather(down_q, ("dp", "ctx"), axis=0, tiled=True),
        lax.all_gather(up_q, ("dp", "ctx"), axis=0, tiled=True),
        lax.all_gather(key_w, ("dp", "ctx"), axis=0, tiled=True),
        lax.all_gather(value_w, ("dp", "ctx"), axis=0, tiled=True),
        lax.all_gather(out_w, ("dp", "ctx"), axis=0, tiled=True),
    )
    ffn_w = (
        lax.all_gather(gate_w, ("dp", "ctx"), axis=0, tiled=True),
        lax.all_gather(up_w, ("dp", "ctx"), axis=0, tiled=True),
        lax.all_gather(down_w, ("dp", "ctx"), axis=0, tiled=True),
    )
    result, kept_values = forward(token_rows, attention_w, ffn_w, gains, own_pos, allowed)
    attention_w = (
        lax.all_gather(down_q, ("dp", "ctx"), axis=0, tiled=True),
        lax.all_gather(up_q, ("dp", "ctx"), axis=0, tiled=True),
        lax.all_gather(key_w, ("dp", "ctx"), axis=0, tiled=True),
        lax.all_gather(value_w, ("dp", "ctx"), axis=0, tiled=True),
        lax.all_gather(out_w, ("dp", "ctx"), axis=0, tiled=True),
    )
    ffn_w = (
        lax.all_gather(gate_w, ("dp", "ctx"), axis=0, tiled=True),
        lax.all_gather(up_w, ("dp", "ctx"), axis=0, tiled=True),
        lax.all_gather(down_w, ("dp", "ctx"), axis=0, tiled=True),
    )
    unused, kept_values = forward(token_rows, attention_w, ffn_w, gains, own_pos, allowed)
    grad_tokens, attention_grads, ffn_grads = backward(
        cotangent, attention_w, ffn_w, gains, own_pos, allowed, kept_values
    )
    grad_gain_one, grad_down_q, grad_gain_q, grad_up_q, grad_key_w, grad_value_w, grad_out_w = (
        attention_grads
    )
    grad_gate_w, grad_up_w, grad_down_w, grad_gain_two = ffn_grads
    return (
        result.astype(jnp.bfloat16),
        grad_tokens,
        grad_gain_one,
        grad_down_q,
        grad_gain_q,
        grad_up_q,
        grad_key_w,
        grad_value_w,
        grad_out_w,
        grad_gain_two,
        grad_gate_w,
        grad_up_w,
        grad_down_w,
    )


def solution(mesh):
    fast = dict(mesh.shape) == {"dp": 4, "ctx": 2, "tensor": 4}
    return jax.shard_map(
        fast_device if fast else per_device,
        mesh=mesh,
        in_specs=(
            P(("dp", "ctx"), None),
            P(("dp", "ctx"), None),
            P("dp", None),
            P("dp", None, None),
            P(),
            P(("dp", "ctx"), None),
            P(),
            P(("dp", "ctx"), "tensor"),
            P(("dp", "ctx"), None),
            P(("dp", "ctx"), None),
            P(("dp", "ctx"), "tensor"),
            P(),
            P(("dp", "ctx"), "tensor"),
            P(("dp", "ctx"), "tensor"),
            P(("dp", "ctx"), "tensor"),
        ),
        out_specs=(
            P(("dp", "ctx"), None),
            P(("dp", "ctx"), None),
            P(("dp", "ctx")),
            P(("dp", "ctx"), None),
            P(("dp", "ctx")),
            P(("dp", "ctx"), "tensor"),
            P(("dp", "ctx"), None),
            P(("dp", "ctx"), None),
            P(("dp", "ctx"), "tensor"),
            P(("dp", "ctx")),
            P(("dp", "ctx"), "tensor"),
            P(("dp", "ctx"), "tensor"),
            P(("dp", "ctx"), "tensor"),
        ),
        check_vma=False,
    )
```

```python
import jax
import jax.numpy as jnp
from jax import lax
from jax.experimental import pallas as pl
from jax.experimental.pallas import tpu as pltpu
from jax.sharding import PartitionSpec as P

HD = 256


EPSILON = 1e-06

AXES = ("dp", "ctx", "tensor")
BF = jnp.bfloat16
F32 = jnp.float32


def dot(left, right):
    return jnp.dot(left, right, preferred_element_type=F32)


def times_trans(left, right):
    return lax.dot_general(left, right, (((1,), (1,)), ((), ())), preferred_element_type=F32)


def trans_times(left, right):
    return lax.dot_general(left, right, (((0,), (0,)), ((), ())), preferred_element_type=F32)


def rms_parts(array):
    inverse = lax.rsqrt(jnp.mean(array * array, axis=-1, keepdims=True) + EPSILON)
    return (array * inverse, inverse)


def rms_back(grad_out, plain, inverse, gain):
    grad_plain = grad_out * gain
    grad_in = inverse * (grad_plain - plain * jnp.mean(grad_plain * plain, axis=-1, keepdims=True))
    return (grad_in, jnp.sum(grad_out * plain, axis=0))


def angles_of(places, half):
    freqs = 10000.0 ** (-jnp.arange(half, dtype=F32) / half)
    angles = places[:, None] * freqs[None, :]
    return (jnp.cos(angles), jnp.sin(angles))


def turn(array, cosine, sine):
    half = array.shape[-1] // 2
    first = array[..., :half]
    latter = array[..., half:]
    return jnp.concatenate(
        [first * cosine - latter * sine, latter * cosine + first * sine], axis=-1
    )


def routes(move):
    pairs = []
    for z in range(4):
        for x in range(2):
            for y in range(2):
                for c in range(2):
                    to = move(z, x, y, c)
                    if to is not None:
                        tz, tx, ty, tc = to
                        pairs.append(
                            (((z * 2 + x) * 2 + y) * 2 + c, ((tz * 2 + tx) * 2 + ty) * 2 + tc)
                        )
    return pairs


OVER_X = routes(lambda z, x, y, c: (z, 1 - x, y, c))
OVER_Y = routes(lambda z, x, y, c: (z, x, 1 - y, c))
OVER_XY = routes(lambda z, x, y, c: (z, 1 - x, 1 - y, c))
OVER_YC = routes(lambda z, x, y, c: (z, x, 1 - y, 1 - c))
OVER_C = routes(lambda z, x, y, c: (z, x, y, 1 - c))
TRANSPOSE = routes(lambda z, x, y, c: (z, c, y, x) if x != c else None)
Z_ONE = routes(lambda z, x, y, c: (z ^ 1, x, y, c))
Z_TWO = routes(lambda z, x, y, c: (z ^ 2, x, y, c))
Z_THREE = routes(lambda z, x, y, c: (z ^ 3, x, y, c))


def send(array, pairs):
    return lax.ppermute(array, AXES, pairs)


def transpose(array, stays):
    return jnp.where(stays, array, send(array, TRANSPOSE))


def after(array, *others):
    return lax.optimization_barrier((array, *others))[0]


def stage(*arrays):
    return lax.optimization_barrier(arrays)


def gather_z(array):
    return lax.all_gather(array, "dp", axis=0, tiled=True)


def reduce_z(slabs):
    return lax.psum_scatter(slabs, "dp", scatter_dimension=0, tiled=True)


def trade_z(slabs):
    n = slabs.shape[0] // 4
    return [slabs[:n]] + [
        send(slabs[k * n : (k + 1) * n], pairs)
        for k, pairs in ((1, Z_ONE), (2, Z_TWO), (3, Z_THREE))
    ]


WHOLE = pl.BlockSpec(memory_space=pltpu.VMEM)
HELD = pl.BlockSpec(memory_space=pl.ANY)
ROOMY = pltpu.CompilerParams(vmem_limit_bytes=56 * 1024 * 1024)


def cost(macs, moved, share=1):
    return pl.CostEstimate(
        flops=2 * macs // share // 1, bytes_accessed=moved // share // 1, transcendentals=0
    )


def place_copies(plan, numbers, buffers, shape, dtype):
    def body(numbers_ref, *refs):
        ins, out_ref, sem = refs[:-2], refs[-2], refs[-1]
        listed = plan(numbers_ref, ins, out_ref)
        for i, (condition, source, target) in enumerate(listed):
            copy = pltpu.make_async_copy(source, target, sem.at[i])
            if condition is None:
                copy.start()
            else:
                pl.when(condition)(copy.start)
        for i, (condition, source, target) in enumerate(listed):
            copy = pltpu.make_async_copy(source, target, sem.at[i])
            if condition is None:
                copy.wait()
            else:
                pl.when(condition)(copy.wait)

    moved = 2
    for extent in shape:
        moved *= extent
    return pl.pallas_call(
        body,
        grid_spec=pltpu.PrefetchScalarGridSpec(
            num_scalar_prefetch=1,
            grid=(1,),
            in_specs=[HELD] * len(buffers),
            out_specs=pl.BlockSpec(shape, lambda i, numbers_ref: (0, 0)),
            scratch_shapes=[pltpu.SemaphoreType.DMA((40,))],
        ),
        out_shape=jax.ShapeDtypeStruct(shape, dtype),
        compiler_params=ROOMY,
        cost_estimate=cost(0, 2 * moved),
    )(numbers, *buffers)


def attention_forward(query_pre, cosine, sine, keys, values, row_info, key_places):
    rows, width = query_pre.shape
    heads = width // HD
    chunk = 256
    half = HD // 2
    scale = HD ** (-0.5)

    def body(pre_ref, cos_ref, sin_ref, k_ref, v_ref, info_ref, place_ref, q_ref, o_ref, lse_ref):
        for i in range(rows // chunk):
            at = slice(i * chunk, (i + 1) * chunk)
            first, latter = pre_ref[at, :half], pre_ref[at, half:]
            co, si = cos_ref[at], sin_ref[at]
            q = jnp.concatenate([first * co - latter * si, latter * co + first * si], 1).astype(BF)
            q_ref[at] = q
            scores = times_trans(q, k_ref[...]) * scale
            allowed = (place_ref[...] <= info_ref[at, 0:1]) & (place_ref[...] >= info_ref[at, 1:2])
            scores = jnp.where(allowed, scores, -1e30)
            largest = jnp.max(scores, axis=-1, keepdims=True)
            exponent = jnp.exp(scores - largest)
            totals = jnp.sum(exponent, axis=-1, keepdims=True)
            soft = (exponent * (1.0 / totals)).astype(BF)
            o_ref[at] = dot(soft, v_ref[...]).astype(BF)
            lse_ref[0, at] = largest + jnp.log(totals)

    full = lambda h: (0, 0)
    by_head = lambda h: (0, h)
    return pl.pallas_call(
        body,
        grid=(heads,),
        in_specs=[
            pl.BlockSpec((rows, HD), by_head),
            pl.BlockSpec((rows, half), full),
            pl.BlockSpec((rows, half), full),
            pl.BlockSpec((rows, HD), full),
            pl.BlockSpec((rows, HD), full),
            pl.BlockSpec((rows, 2), full),
            pl.BlockSpec((1, rows), full),
        ],
        out_specs=[
            pl.BlockSpec((rows, HD), by_head),
            pl.BlockSpec((rows, HD), by_head),
            pl.BlockSpec((1, rows, 1), lambda h: (h, 0, 0)),
        ],
        out_shape=[
            jax.ShapeDtypeStruct((rows, width), BF),
            jax.ShapeDtypeStruct((rows, width), BF),
            jax.ShapeDtypeStruct((heads, rows, 1), F32),
        ],
        compiler_params=ROOMY,
        cost_estimate=cost(4 * rows * rows * width, 6 * rows * width),
    )(query_pre, cosine, sine, keys, values, row_info, key_places)


def attention_backward(query, grad_out, lse, cosine, sine, keys, values, row_info, key_places):
    rows, width = query.shape
    heads = width // HD
    chunk = 256
    half = HD // 2
    scale = HD ** (-0.5)

    def body(
        q_ref, do_ref, lse_ref, cos_ref, sin_ref, k_ref, v_ref, info_ref, place_ref, dq_ref, dk_ref, dv_ref
    ):
        @pl.when(pl.program_id(0) == 0)
        def clear():
            dk_ref[...] = jnp.zeros_like(dk_ref)
            dv_ref[...] = jnp.zeros_like(dv_ref)

        for i in range(rows // chunk):
            at = slice(i * chunk, (i + 1) * chunk)
            q, do = q_ref[at], do_ref[at]
            scores = times_trans(q, k_ref[...]) * scale
            allowed = (place_ref[...] <= info_ref[at, 0:1]) & (place_ref[...] >= info_ref[at, 1:2])
            soft = jnp.exp(jnp.where(allowed, scores, -1e30) - lse_ref[0, at])
            grad_soft = times_trans(do, v_ref[...])
            summed = jnp.sum(soft * grad_soft, axis=-1, keepdims=True)
            grad_scores = (soft * (grad_soft - summed)).astype(BF)
            dq = dot(grad_scores, k_ref[...]) * scale
            first, latter = dq[:, :half], dq[:, half:]
            co, si = cos_ref[at], sin_ref[at]
            dq_ref[at] = jnp.concatenate(
                [first * co + latter * si, latter * co - first * si], 1
            ).astype(BF)
            dk_ref[...] += trans_times(grad_scores, q) * scale
            dv_ref[...] += trans_times(soft.astype(BF), do)

    full = lambda h: (0, 0)
    by_head = lambda h: (0, h)
    return pl.pallas_call(
        body,
        grid=(heads,),
        in_specs=[
            pl.BlockSpec((rows, HD), by_head),
            pl.BlockSpec((rows, HD), by_head),
            pl.BlockSpec((1, rows, 1), lambda h: (h, 0, 0)),
            pl.BlockSpec((rows, half), full),
            pl.BlockSpec((rows, half), full),
            pl.BlockSpec((rows, HD), full),
            pl.BlockSpec((rows, HD), full),
            pl.BlockSpec((rows, 2), full),
            pl.BlockSpec((1, rows), full),
        ],
        out_specs=[
            pl.BlockSpec((rows, HD), by_head),
            pl.BlockSpec((rows, HD), full),
            pl.BlockSpec((rows, HD), full),
        ],
        out_shape=[
            jax.ShapeDtypeStruct((rows, width), BF),
            jax.ShapeDtypeStruct((rows, HD), F32),
            jax.ShapeDtypeStruct((rows, HD), F32),
        ],
        compiler_params=ROOMY,
        cost_estimate=cost(8 * rows * rows * width, 6 * rows * width),
    )(query, grad_out, lse, cosine, sine, keys, values, row_info, key_places)


def product_of_parts(parts, weight):
    rows = parts[0].shape[0]
    count = len(parts)
    width = weight.shape[1]

    def body(*refs):
        weight_ref, out_ref = refs[count:]
        for i in range(0, count, 4):
            left = jnp.concatenate([refs[j][...] for j in range(i, i + 4)], axis=0)
            out_ref[i * rows : (i + 4) * rows] = dot(left, weight_ref[...]).astype(BF)

    return pl.pallas_call(
        body,
        in_specs=[WHOLE] * (count + 1),
        out_specs=WHOLE,
        out_shape=jax.ShapeDtypeStruct((count * rows, width), BF),
        compiler_params=ROOMY,
        cost_estimate=cost(count * rows * weight.size, 2 * weight.size),
    )(*parts, weight)


def product_pieces(left, weight, extras, got, first_half):
    rows = left.shape[0] // 2
    part = rows // 4
    start = 0 if first_half else rows
    wide = weight.shape[0]
    total = wide + sum(e.shape[1] for e in extras)
    outs = 4 if first_half else 1

    def body(left_ref, weight_ref, *refs):
        extra_refs = refs[: len(extras)]
        got_ref = refs[len(extras)] if got is not None else None
        out_refs = refs[len(refs) - outs :]
        src = slice(start, start + rows)

        def put(value, cols):
            if got_ref is not None:
                value = value + got_ref[:, cols].astype(F32)
            value = value.astype(BF)
            if outs == 1:
                out_refs[0][:, cols] = value
            else:
                for f in range(4):
                    out_refs[f][:, cols] = value[f * part : (f + 1) * part]

        step = 512
        for col in range(0, wide, step):
            put(times_trans(left_ref[src], weight_ref[col : col + step]), slice(col, col + step))
        col = wide
        for extra_ref in extra_refs:
            n = extra_ref.shape[1]
            put(extra_ref[src], slice(col, col + n))
            col += n

    shapes = [jax.ShapeDtypeStruct((part, total), BF)] * 4
    if outs == 1:
        shapes = [jax.ShapeDtypeStruct((rows, total), BF)]
    arrays = [left, weight, *extras] + ([got] if got is not None else [])
    return pl.pallas_call(
        body,
        in_specs=[WHOLE] * len(arrays),
        out_specs=[WHOLE] * outs,
        out_shape=shapes,
        compiler_params=ROOMY,
        cost_estimate=cost(rows * wide * left.shape[1], 2 * weight.size + 4 * rows * total),
    )(*arrays)


def tiles_of(width):
    whole = width // 256
    return whole, width - whole * 256


def ffn_forward(numbers, parts, pairs):
    part, depth = parts[0].shape
    rows = part * len(parts)
    width = pairs[0].shape[1]
    whole, rest = tiles_of(width)

    def body(numbers_ref, *refs):
        part_refs, pair_refs = refs[:4], refs[4:6]
        hid_ref, slope_ref, silu_ref, gate_vm, up_vm, in_vm, sem = refs[6:]
        gate_copies, up_copies = [], []
        for i in range(8):
            to = pl.ds(pl.multiple_of(numbers_ref[i] * 256, 256), 256)
            ref, at = pair_refs[i // 4], (i % 4) * 512
            gate_copies.append(
                pltpu.make_async_copy(ref.at[at : at + 256], gate_vm.at[to], sem.at[i])
            )
            up_copies.append(
                pltpu.make_async_copy(ref.at[at + 256 : at + 512], up_vm.at[to], sem.at[8 + i])
            )
        for copy in gate_copies + up_copies:
            copy.start()
        for f in range(4):
            in_vm[f * part : (f + 1) * part] = part_refs[f][...]
        for copy in gate_copies + up_copies:
            copy.wait()

        def tile(cols):
            gate = dot(in_vm[...], gate_vm[:, cols])
            up = dot(in_vm[...], up_vm[:, cols])
            sigma = jax.nn.sigmoid(gate)
            silu = gate * sigma
            hid_ref[:, cols] = (silu * up).astype(BF)
            slope_ref[:, cols] = up * sigma * (1.0 + gate * (1.0 - sigma))
            silu_ref[:, cols] = silu

        @pl.loop(0, whole)
        def each(i):
            tile(pl.ds(pl.multiple_of(i * 256, 256), 256))

        if rest:
            tile(slice(whole * 256, width))

    return pl.pallas_call(
        body,
        grid_spec=pltpu.PrefetchScalarGridSpec(
            num_scalar_prefetch=1,
            grid=(1,),
            in_specs=[pl.BlockSpec((part, depth), lambda i, n: (0, 0))] * 4 + [HELD] * 2,
            out_specs=[pl.BlockSpec((rows, width), lambda i, n: (0, 0))] * 3,
            scratch_shapes=[
                pltpu.VMEM((depth, width), BF),
                pltpu.VMEM((depth, width), BF),
                pltpu.VMEM((rows, depth), BF),
                pltpu.SemaphoreType.DMA((16,)),
            ],
        ),
        out_shape=[
            jax.ShapeDtypeStruct((rows, width), BF),
            jax.ShapeDtypeStruct((rows, width), F32),
            jax.ShapeDtypeStruct((rows, width), F32),
        ],
        compiler_params=ROOMY,
        cost_estimate=cost(2 * rows * depth * width, 4 * depth * width),
    )(numbers, *parts, *pairs)


def ffn_backward(numbers, cot, slope, silu, pairs, downs):
    rows = slope.shape[0]
    depth = cot.shape[1]
    part = rows // 4
    width = slope.shape[1]
    whole, rest = tiles_of(width)

    def body(numbers_ref, *refs):
        cot_ref, slope_ref, silu_ref = refs[:3]
        pair_refs, down_refs = refs[3:5], refs[5:7]
        gate_out, up_out = refs[7:9]
        piece_refs = refs[9:13]
        down_vm, pair_vm, sem = refs[13:]
        copies, later = [], []
        for i in range(8):
            to = pl.ds(pl.multiple_of(numbers_ref[i] * 256, 256), 256)
            ref, at = down_refs[i // 4], (i % 4) * 256
            copies.append(
                pltpu.make_async_copy(ref.at[at : at + 256], down_vm.at[to], sem.at[i])
            )
            ref, at = pair_refs[i // 4], (i % 4) * 512
            later.append(
                pltpu.make_async_copy(ref.at[at : at + 512], pair_vm.at[i], sem.at[8 + i])
            )
        for copy in copies + later:
            copy.start()
        for copy in copies:
            copy.wait()

        def tile(cols):
            grad = dot(cot_ref[...], down_vm[:, cols])
            gate_out[:, cols] = (grad * slope_ref[:, cols]).astype(BF)
            up_out[:, cols] = (grad * silu_ref[:, cols]).astype(BF)

        @pl.loop(0, whole)
        def each(i):
            tile(pl.ds(pl.multiple_of(i * 256, 256), 256))

        if rest:
            tile(slice(whole * 256, width))
        for copy in later:
            copy.wait()

        @pl.loop(0, 8)
        def block(i):
            cols = pl.ds(pl.multiple_of(numbers_ref[i] * 256, 256), 256)
            value = times_trans(gate_out[...], pair_vm[i, :256]) + times_trans(
                up_out[...], pair_vm[i, 256:]
            )
            value = value.astype(BF)
            for f in range(4):
                piece_refs[f][:, cols] = value[f * part : (f + 1) * part]

    flat = lambda i, n: (0, 0)
    return pl.pallas_call(
        body,
        grid_spec=pltpu.PrefetchScalarGridSpec(
            num_scalar_prefetch=1,
            grid=(1,),
            in_specs=[
                pl.BlockSpec((rows, depth), flat),
                pl.BlockSpec((rows, width), flat),
                pl.BlockSpec((rows, width), flat),
            ]
            + [HELD] * 4,
            out_specs=[pl.BlockSpec((rows, width), flat)] * 2
            + [pl.BlockSpec((part, depth), flat)] * 4,
            scratch_shapes=[
                pltpu.VMEM((depth, width), BF),
                pltpu.VMEM((8, 512, width), BF),
                pltpu.SemaphoreType.DMA((16,)),
            ],
        ),
        out_shape=[jax.ShapeDtypeStruct((rows, width), BF)] * 2
        + [jax.ShapeDtypeStruct((part, depth), BF)] * 4,
        compiler_params=ROOMY,
        cost_estimate=cost(3 * rows * depth * width, 6 * depth * width),
    )(numbers, cot, slope, silu, *pairs, *downs)


def ffn_output(numbers, hidden, downs):
    rows, width = hidden.shape
    part = rows // 4
    depth = 2 * downs[0].shape[0]

    def body(numbers_ref, hid_ref, *refs):
        down_refs, piece_refs = refs[:2], refs[2:6]
        down_vm, sem = refs[6:]
        copies = [
            pltpu.make_async_copy(
                down_refs[i // 4].at[(i % 4) * 256 : (i % 4 + 1) * 256], down_vm.at[i], sem.at[i]
            )
            for i in range(8)
        ]
        for copy in copies:
            copy.start()
        for copy in copies:
            copy.wait()

        @pl.loop(0, 8)
        def block(i):
            cols = pl.ds(pl.multiple_of(numbers_ref[i] * 256, 256), 256)
            value = times_trans(hid_ref[...], down_vm[i]).astype(BF)
            for f in range(4):
                piece_refs[f][:, cols] = value[f * part : (f + 1) * part]

    flat = lambda i, n: (0, 0)
    return pl.pallas_call(
        body,
        grid_spec=pltpu.PrefetchScalarGridSpec(
            num_scalar_prefetch=1,
            grid=(1,),
            in_specs=[pl.BlockSpec((rows, width), flat)] + [HELD] * 2,
            out_specs=[pl.BlockSpec((part, depth), flat)] * 4,
            scratch_shapes=[
                pltpu.VMEM((8, 256, width), BF),
                pltpu.SemaphoreType.DMA((8,)),
            ],
        ),
        out_shape=[jax.ShapeDtypeStruct((part, depth), BF)] * 4,
        compiler_params=ROOMY,
        cost_estimate=cost(rows * depth * width, 2 * depth * width, 4),
    )(numbers, hidden, *downs)


def weight_grads(numbers, terms, width):
    lefts, rights, left_specs, right_specs = [], [], [], []
    shape_of = []
    for left, block, offset, products in terms:
        for array in left:
            lefts.append(array)
            left_specs.append(
                pl.BlockSpec((array.shape[0], block), lambda i, n, offset=offset: (0, n[offset + i]))
            )
        for place, right in products:
            for array, start, count, pick in right:
                rights.append(array)
                if pick is None:
                    right_specs.append(pl.BlockSpec(array.shape, lambda i, n: (0, 0)))
                else:
                    right_specs.append(
                        pl.BlockSpec((array.shape[0], width), lambda i, n, pick=pick: (0, n[pick]))
                    )
        shape_of.append(block)
    height = sum(shape_of)

    def body(numbers_ref, *refs):
        left_refs = refs[: len(lefts)]
        right_refs = refs[len(lefts) : len(lefts) + len(rights)]
        out_ref = refs[-1]
        li, ri, row = 0, 0, 0
        for left, block, offset, products in terms:
            pieces = [left_refs[li + j][...] for j in range(len(left))]
            li += len(left)
            whole = pieces[0] if len(pieces) == 1 else jnp.concatenate(pieces, axis=0)
            for place, right in products:
                value = None
                at = 0
                for array, start, count, pick in right:
                    this = trans_times(
                        whole[at : at + count], right_refs[ri][start : start + count]
                    )
                    value = this if value is None else value + this
                    at += count
                    ri += 1
                value = value.astype(BF)
                n = value.shape[1]
                if place is None:
                    cols = slice(0, n)
                else:
                    cols = pl.ds(pl.multiple_of(numbers_ref[place] * n, n), n)
                out_ref[row : row + block, cols] = value

            row += block

    macs = 4 * height * width * 1024
    return pl.pallas_call(
        body,
        grid_spec=pltpu.PrefetchScalarGridSpec(
            num_scalar_prefetch=1,
            grid=(4,),
            in_specs=left_specs + right_specs,
            out_specs=pl.BlockSpec((height, width), lambda i, n: (i, 0)),
        ),
        out_shape=jax.ShapeDtypeStruct((4 * height, width), BF),
        compiler_params=ROOMY,
        cost_estimate=cost(macs, 4 * height * width * 4, 4),
    )(numbers, *lefts, *rights)


def input_gradient(numbers, grad_lat, first_all, grad_mid, tokens, gain):
    depth = tokens.shape[1]
    wide = grad_lat.shape[1]
    part = 128

    def body(numbers_ref, lat_ref, first_ref, mid_ref, tok_ref, gain_ref, out_ref, grad_vm):
        for col in range(0, depth, 512):
            cols = slice(col, col + 512)
            grad_vm[:, cols] = times_trans(lat_ref[...], first_ref[cols]) * gain_ref[:, cols]
        for i in range(4):
            at = slice(i * part, (i + 1) * part)
            plain = tok_ref[at].astype(F32)
            inverse = lax.rsqrt(jnp.mean(plain * plain, axis=-1, keepdims=True) + EPSILON)
            plain = plain * inverse
            grad = grad_vm[at]
            mean = jnp.mean(grad * plain, axis=-1, keepdims=True)
            to = pl.ds(pl.multiple_of(numbers_ref[9 + i] * part, part), part)
            out_ref[to] = mid_ref[at].astype(F32) + inverse * (grad - plain * mean)

    picked = lambda i, n: (n[8], 0)
    flat = lambda i, n: (0, 0)
    return pl.pallas_call(
        body,
        grid_spec=pltpu.PrefetchScalarGridSpec(
            num_scalar_prefetch=1,
            grid=(1,),
            in_specs=[
                pl.BlockSpec((4 * part, wide), picked),
                pl.BlockSpec((depth, wide), flat),
                pl.BlockSpec((4 * part, depth), picked),
                pl.BlockSpec((4 * part, depth), picked),
                pl.BlockSpec((1, depth), flat),
            ],
            out_specs=pl.BlockSpec((4 * part, depth), flat),
            scratch_shapes=[pltpu.VMEM((4 * part, depth), F32)],
        ),
        out_shape=jax.ShapeDtypeStruct((4 * part, depth), F32),
        compiler_params=ROOMY,
        cost_estimate=cost(4 * part * depth * wide, 2 * depth * wide + 8 * part * depth * 4),
    )(numbers, grad_lat, first_all, grad_mid, tokens, gain.reshape(1, -1))


def first_finish(numbers, quarters, first_w, gain, latent_width):
    rows, lane = quarters[0].shape
    wide = first_w.shape[1]

    def body(numbers_ref, *refs):
        weight_ref, gain_ref, down_ref, key_ref, value_ref, one_ref, all_vm = refs[4:]
        for i in range(4):
            cols = pl.ds(pl.multiple_of(numbers_ref[25 + i] * lane, lane), lane)
            all_vm[:, cols] = refs[i][...].astype(F32)
        down_ref[...] = all_vm[:, :latent_width]
        key_ref[...] = all_vm[:, latent_width : latent_width + HD]
        value_ref[...] = all_vm[:, latent_width + HD :]
        total = jnp.sum(weight_ref[...].astype(F32) * all_vm[...], axis=1, keepdims=True)
        one_ref[...] = total / gain_ref[...]

    flat = lambda i, n: (0, 0)
    extents = [(rows, latent_width), (rows, HD), (rows, wide - latent_width - HD), (rows, 1)]
    *grads, one = pl.pallas_call(
        body,
        grid_spec=pltpu.PrefetchScalarGridSpec(
            num_scalar_prefetch=1,
            grid=(1,),
            in_specs=[pl.BlockSpec((rows, lane), flat)] * 4
            + [pl.BlockSpec((rows, wide), flat), pl.BlockSpec((rows, 1), flat)],
            out_specs=[pl.BlockSpec(e, flat) for e in extents],
            scratch_shapes=[pltpu.VMEM((rows, wide), F32)],
        ),
        out_shape=[jax.ShapeDtypeStruct(e, F32) for e in extents],
        compiler_params=ROOMY,
        cost_estimate=cost(0, 10 * rows * wide),
    )(numbers, *quarters, first_w, gain.reshape(-1, 1))
    return (*grads, one.reshape(-1))


def trade(pieces):
    own, y_piece, x_piece, xy_piece = pieces
    return [own, send(y_piece, OVER_Y), send(x_piece, OVER_X), send(xy_piece, OVER_XY)]


def added(pieces):
    total = pieces[0].astype(F32)
    for piece in pieces[1:]:
        total = total + piece.astype(F32)
    return total


def sum_pieces(pieces):
    return added(trade(pieces))


def spread(part):
    return [part, send(part, OVER_Y), send(part, OVER_X), send(part, OVER_XY)]


def over_core(arrays):
    return [send(array, OVER_C) for array in arrays]


def fast_device(
    tokens_in,
    cotangent,
    seq_lengths,
    block_order,
    gain_one,
    down_q,
    gain_q,
    up_q,
    key_w,
    value_w,
    out_w,
    gain_two,
    gate_w,
    up_w,
    down_w,
):
    z = lax.axis_index("dp")
    x = lax.axis_index("ctx")
    t = lax.axis_index("tensor")
    y = t // 2
    c = t % 2
    stays = x == c
    quarter = x * 2 + y
    rows, depth = tokens_in.shape
    half = rows // 2
    part = rows // 4
    latent_width = down_q.shape[1]
    cols = up_q.shape[1] // 2
    ks = jnp.arange(4, dtype=jnp.int32)
    z_order = z ^ ks
    numbers = jnp.concatenate(
        [
            ks * 2 + c,
            ks * 2 + (1 - c),
            jnp.stack([c ^ x]),
            quarter ^ ks,
            z_order * 2 + x,
            z_order * 2 + (1 - x),
            jnp.stack([c, 1 - c, x, 1 - x, t, t ^ 1, t ^ 2, t ^ 3]),
        ]
    ).astype(jnp.int32)
    at_same, at_quarter, at_x, at_c, at_t = 8, 9, 13, 21, 25

    first_w = jnp.concatenate([down_q, key_w, value_w], axis=1)
    wide = first_w.shape[1]
    side = wide // 4
    mine = lax.dynamic_slice_in_dim(first_w, t * side, side, axis=1)
    attn_t = transpose(jnp.concatenate([up_q, out_w], axis=0), stays)
    tok_got = send(rows_at(tokens_in, t * part, part), OVER_X)
    first_own = stage(mine, send(mine, Z_ONE), send(mine, Z_TWO), send(mine, Z_THREE))
    first_own = jnp.concatenate(first_own, axis=0)
    first_blocks = [first_own] + [send(first_own, p) for p in (OVER_Y, OVER_X, OVER_XY)]
    first_blocks = first_blocks + over_core(first_blocks)

    def first_plan(n, ins, out):
        listed = []
        for i in range(8):
            col = pl.ds(pl.multiple_of(n[at_t + (0, 2, 0, 2, 1, 3, 1, 3)[i]] * side, side), side)
            for k in range(4):
                place = n[at_x + (i % 4 // 2) * 4 + k]
                row = pl.ds(pl.multiple_of(place * 256, 256), 256)
                listed.append((None, ins[i].at[k * 256 : (k + 1) * 256], out.at[row, col]))
        return listed

    pair_t = transpose(after(jnp.concatenate([gate_w, up_w], axis=0), first_own, tok_got), stays)
    first_all = place_copies(first_plan, numbers, first_blocks, (depth, wide), BF)

    def rows_plan(n, ins, out):
        listed = []
        for o in range(2):
            mine_too = (n[at_same] == o)
            for f in range(4):
                q = n[at_quarter + f]
                to = out.at[pl.ds((o * 4 + f) * part, part)]
                here = pl.ds(pl.multiple_of(q * part, part), part)
                listed.append((mine_too, ins[0].at[here], to))
                away = jnp.logical_not(mine_too)
                for j in range(4):
                    listed.append((away & (n[at_t + j] == q), ins[1 + j], to))
        return listed

    def group_rows(array, got):
        got_y = send(got, OVER_Y)
        buffers = [array, got, send(got, OVER_C), got_y, send(got_y, OVER_C)]
        return place_copies(rows_plan, numbers, buffers, (2 * rows, depth), BF)

    tokens = group_rows(tokens_in, tok_got)

    attn_own = gather_z(attn_t)
    attn_rows = attn_t.shape[0]
    upq_rows = up_q.shape[0]
    out_rows = out_w.shape[0]

    def head_plan(start, count):
        def plan(n, ins, out):
            listed = []
            for i in range(8):
                row = pl.ds(pl.multiple_of(n[i] * count, count), count)
                col = pl.ds(pl.multiple_of(n[at_c] * cols, cols), cols)
                at = (i % 4) * attn_rows + start
                listed.append((None, ins[i // 4].at[at : at + count, col], out.at[row]))
            return listed

        return plan


    cot = group_rows(cotangent, send(rows_at(cotangent, t * part, part), OVER_X))

    places = (
        block_order[0][:, :, None] * half + jnp.arange(half, dtype=jnp.int32)[None, None, :]
    ).reshape(2, 4, part)
    places = jnp.stack(
        [
            lax.dynamic_index_in_dim(
                lax.dynamic_index_in_dim(places, c ^ o, 0, False), quarter ^ f, 0, False
            )
            for o in range(2)
            for f in range(4)
        ]
    ).reshape(-1)
    second = (places >= seq_lengths[0, 0]).astype(jnp.int32)
    sequence_start = second * seq_lengths[0, 0]
    cosine, sine = angles_of((places - sequence_start).astype(F32), HD // 2)
    row_info = jnp.stack([places, sequence_start], axis=1)
    key_places = places[None, :]

    token_rows = tokens.astype(F32)
    plain_one, inverse_one = rms_parts(token_rows)
    normed = (plain_one * gain_one).astype(BF)
    lat = dot(normed, first_all)
    pair_own = gather_z(pair_t)
    down_t = transpose(after(down_w, first_all), stays)
    attn_own = after(attn_own, lat)
    attns = [attn_own, send(attn_own, OVER_C)]
    up_q_all = place_copies(
        head_plan(0, upq_rows), numbers, attns, (latent_width, cols), BF
    )
    out_all = place_copies(
        head_plan(upq_rows, out_rows), numbers, attns, (depth, cols), BF
    )
    latent = lat[:, :latent_width]
    plain_q, inverse_q = rms_parts(latent)
    query_in = (plain_q * gain_q).astype(BF)
    keys = turn(lat[:, latent_width : latent_width + HD], cosine, sine).astype(BF)
    values = lat[:, latent_width + HD :].astype(BF)
    query_pre = dot(query_in, up_q_all)
    query, attended, lse = attention_forward(
        query_pre, cosine, sine, keys, values, row_info, key_places
    )
    (give,) = product_pieces(attended, out_all, [], None, False)
    pieces = product_pieces(attended, out_all, [], send(give, OVER_C), True)
    middle, cot = stage(tokens[:part].astype(F32) + sum_pieces(pieces), cot)

    plain_two, inverse_two = rms_parts(middle)
    two_parts = spread((plain_two * gain_two).astype(BF))
    *two_parts, pair_own, down_t = stage(*two_parts, pair_own, down_t)
    down_own = gather_z(down_t)
    pairs = [pair_own, send(pair_own, OVER_C)]
    hidden, slope, silu = ffn_forward(numbers, two_parts, pairs)

    def two(array, other):
        return [(array, 0, rows, None), (other, 0, rows, None)]

    width = down_w.shape[1]
    (hidden_other,) = over_core([hidden])
    down_slabs = weight_grads(
        numbers, [([cot], 256, 0, [(None, two(hidden, hidden_other))])], width
    )
    down_slabs, hidden, down_own = stage(down_slabs, hidden, down_own)
    down_sum = reduce_z(down_slabs)
    downs = [down_own, send(down_own, OVER_C)]
    grad_gate, grad_up, *pieces = ffn_backward(
        numbers, after(cot, down_slabs), slope, silu, pairs, downs
    )

    gate_other, up_other = over_core([grad_gate, grad_up])
    two_all = two_parts + over_core(two_parts)
    pair_slabs = weight_grads(
        numbers,
        [
            (two_all, 256, 0, [(None, two(grad_gate, gate_other))]),
            (two_all, 256, 0, [(None, two(grad_up, up_other))]),
        ],
        width,
    )
    *pieces, pair_slabs, hidden = stage(*trade(pieces), pair_slabs, hidden)
    grad_norm_two = added(pieces)
    pair_sum = reduce_z(after(pair_slabs, down_sum))

    grad_plain = grad_norm_two * gain_two
    grad_mid = cot[:part].astype(F32) + inverse_two * (
        grad_plain - plain_two * jnp.mean(grad_plain * plain_two, axis=-1, keepdims=True)
    )
    mid_parts = spread(grad_mid.astype(BF))
    staged = stage(*mid_parts, *ffn_output(numbers, hidden, downs))
    mid_parts, out_pieces = list(staged[:4]), staged[4:]
    mid_parts = mid_parts + over_core(mid_parts)

    def stack_plan(n, ins, out):
        return [(None, ins[i], out.at[pl.ds(i * part, part)]) for i in range(8)]

    grad_attended = product_of_parts(mid_parts, out_all)
    grad_query_pre, key_acc, value_acc = attention_backward(
        query, grad_attended, lse, cosine, sine, keys, values, row_info, key_places
    )
    staged = stage(*trade(out_pieces), grad_query_pre, key_acc, value_acc)
    out_sum, (grad_query_pre, key_acc, value_acc) = staged[:4], staged[4:]
    extras = [key_acc, value_acc]
    (give,) = product_pieces(grad_query_pre, up_q_all, extras, None, False)
    pieces = product_pieces(grad_query_pre, up_q_all, extras, send(give, OVER_C), True)
    attended_other, query_other = over_core([attended, grad_query_pre])
    *pieces, attended_other, query_other = stage(*pieces, attended_other, query_other)

    def swapped(array):
        return [(array, rows, rows, None), (array, 0, rows, None)]

    attn_slabs = weight_grads(
        numbers,
        [
            (
                [query_in],
                upq_rows,
                0,
                [
                    (at_c, [(grad_query_pre, 0, 2 * rows, None)]),
                    (at_c + 1, swapped(query_other)),
                ],
            ),
            (
                mid_parts,
                out_rows,
                0,
                [
                    (at_c, [(attended, 0, 2 * rows, None)]),
                    (at_c + 1, swapped(attended_other)),
                ],
            ),
        ],
        2 * cols,
    )
    out_part = (middle + added(out_sum)).astype(BF)
    *pieces, attn_slabs, out_part = stage(*trade(pieces), attn_slabs, out_part)
    three = added(pieces)
    attn_sum = reduce_z(after(attn_slabs, pair_sum))

    grad_plain = three[:, :latent_width] * gain_q
    plain_q_mine = plain_q[:part]
    grad_latent = inverse_q[:part] * (
        grad_plain - plain_q_mine * jnp.mean(grad_plain * plain_q_mine, axis=-1, keepdims=True)
    )
    grad_key_pre = turn(
        three[:, latent_width : latent_width + HD], cosine[:part], -sine[:part]
    )
    lat_parts = spread(
        jnp.concatenate(
            [grad_latent, grad_key_pre, three[:, latent_width + HD :]], axis=1
        ).astype(BF)
    )
    down_home = transpose(down_sum, stays)
    grad_branch = place_copies(stack_plan, numbers, mid_parts, (2 * rows, depth), BF)
    pair_home = transpose(pair_sum, stays)
    staged = stage(*lat_parts, down_home, pair_home, grad_branch, out_part)
    lat_parts, (down_home, pair_home, grad_branch, out_part) = list(staged[:4]), staged[4:]
    lat_parts = lat_parts + over_core(lat_parts)

    lane = wide // 4
    first_slabs = weight_grads(
        numbers,
        [([normed], 256, at_x, [(None, [(p, 0, part, at_t) for p in lat_parts])])],
        lane,
    )
    out_parts = spread(out_part)
    out_parts = out_parts + over_core(out_parts)
    grad_lat = place_copies(stack_plan, numbers, lat_parts, (2 * rows, wide), BF)
    grad_tokens = input_gradient(numbers, grad_lat, first_all, grad_branch, tokens, gain_one)

    def out_plan(n, ins, out):
        listed = []
        for f in range(4):
            to = out.at[pl.ds(pl.multiple_of(n[at_quarter + f] * part, part), part)]
            listed.append((n[at_same] == 0, ins[f], to))
            listed.append((n[at_same] == 1, ins[4 + f], to))
        return listed

    attn_home = transpose(attn_sum, stays)
    staged = stage(*trade_z(first_slabs), grad_tokens, attn_home, *out_parts)
    first_quarter = added(staged[:4]).astype(BF)
    grad_tokens, attn_home, *out_parts = staged[4:]
    quarters = [first_quarter] + [send(first_quarter, p) for p in (OVER_C, OVER_Y, OVER_YC)]
    dev = z * 2 + x
    block = depth // 8
    own_one = lax.dynamic_slice_in_dim(gain_one, dev * block, block)
    grad_down_q, grad_key_w, grad_value_w, grad_gain_one = first_finish(
        numbers, quarters, first_w, own_one, latent_width
    )
    result = place_copies(out_plan, numbers, out_parts, (rows, depth), BF)

    grad_down_w = down_home.astype(F32)
    pair_home = pair_home.astype(F32)
    grad_gate_w, grad_up_w = pair_home[:256], pair_home[256:]
    attn_home = attn_home.astype(F32)
    grad_up_q, grad_out_w = attn_home[:upq_rows], attn_home[upq_rows:]

    own_two = lax.dynamic_slice_in_dim(gain_two, dev * block, block)
    own_q = lax.dynamic_slice_in_dim(gain_q, dev * upq_rows, upq_rows)
    two_sum = jnp.sum(gate_w.astype(F32) * grad_gate_w + up_w.astype(F32) * grad_up_w, axis=1)
    q_sum = jnp.sum(up_q.astype(F32) * grad_up_q, axis=1)
    small = jnp.concatenate([two_sum, q_sum]).reshape(3, -1)
    small = small + send(small, OVER_C) + send(small, OVER_Y) + send(small, OVER_YC)
    small = small.reshape(-1)
    grad_gain_two = small[:block] / own_two
    grad_gain_q = small[block:] / own_q

    return (
        result,
        grad_tokens,
        grad_gain_one,
        grad_down_q,
        grad_gain_q,
        grad_up_q,
        grad_key_w,
        grad_value_w,
        grad_out_w,
        grad_gain_two,
        grad_gate_w,
        grad_up_w,
        grad_down_w,
    )


def rows_at(array, start, count):
    return lax.dynamic_slice_in_dim(array, start, count, axis=0)


def rotate(array, places):
    half = array.shape[-1] // 2
    freqs = 10000.0 ** (-jnp.arange(half, dtype=jnp.float32) / half)
    angles = places[:, None] * freqs[None, :]
    cosine = jnp.cos(angles)
    sine = jnp.sin(angles)
    first = array[..., :half]
    latter = array[..., half:]
    return jnp.concatenate(
        [first * cosine - latter * sine, latter * cosine + first * sine], axis=-1
    )


def forward(token_rows, attention_w, ffn_w, gains, own_pos, allowed):
    gain_one, gain_q, gain_two = gains
    down_q, up_q, key_w, value_w, out_w = attention_w
    gate_w, up_w, down_w = ffn_w
    row_count = token_rows.shape[0]
    heads = up_q.shape[1] // HD
    scale = HD ** (-0.5)
    plain_one, inverse_one = rms_parts(token_rows)
    normed = (plain_one * gain_one).astype(jnp.bfloat16)
    latent = jnp.dot(normed, down_q, preferred_element_type=jnp.float32)
    plain_q, inverse_q = rms_parts(latent)
    query_in = (plain_q * gain_q).astype(jnp.bfloat16)
    query_pre = jnp.dot(query_in, up_q, preferred_element_type=jnp.float32)
    query = rotate(query_pre.reshape(row_count, heads, HD).transpose(1, 0, 2), own_pos).astype(
        jnp.bfloat16
    )
    keys = rotate(jnp.dot(normed, key_w, preferred_element_type=jnp.float32), own_pos).astype(
        jnp.bfloat16
    )
    values = jnp.dot(normed, value_w, preferred_element_type=jnp.float32).astype(jnp.bfloat16)
    keys_all, values_all = (
        lax.all_gather(keys, "ctx", axis=0, tiled=True),
        lax.all_gather(values, "ctx", axis=0, tiled=True),
    )

    def one_head(q_head):
        scores = jnp.where(allowed, times_trans(q_head, keys_all) * scale, -1e30)
        largest = jnp.max(scores, axis=-1, keepdims=True)
        exponent = jnp.exp(scores - largest)
        totals = jnp.sum(exponent, axis=-1, keepdims=True)
        soft = (exponent / totals).astype(jnp.bfloat16)
        return (
            jnp.dot(soft, values_all, preferred_element_type=jnp.float32),
            (largest + jnp.log(totals))[:, 0],
        )

    mixed_heads, log_totals = lax.map(one_head, query)
    attended = mixed_heads.transpose(1, 0, 2).reshape(row_count, heads * HD).astype(jnp.bfloat16)
    branch = lax.psum(times_trans(attended, out_w), "tensor")
    middle = token_rows + branch
    plain_two, inverse_two = rms_parts(middle)
    normed_two = (plain_two * gain_two).astype(jnp.bfloat16)
    gate_pre = jnp.dot(normed_two, gate_w, preferred_element_type=jnp.float32)
    up_pre = jnp.dot(normed_two, up_w, preferred_element_type=jnp.float32)
    hidden = (jax.nn.silu(gate_pre) * up_pre).astype(jnp.bfloat16)
    result = middle + lax.psum(times_trans(hidden, down_w).astype(jnp.bfloat16), "tensor").astype(
        jnp.float32
    )
    kept_values = (
        plain_one,
        inverse_one,
        normed,
        plain_q,
        inverse_q,
        query_in,
        query,
        keys_all,
        values_all,
        log_totals,
        attended,
        plain_two,
        inverse_two,
        normed_two,
        gate_pre,
        up_pre,
        hidden,
    )
    return (result, kept_values)


def backward(cotangent, attention_w, ffn_w, gains, own_pos, allowed, kept_values):
    gain_one, gain_q, gain_two = gains
    down_q, up_q, key_w, value_w, out_w = attention_w
    gate_w, up_w, down_w = ffn_w
    (
        plain_one,
        inverse_one,
        normed,
        plain_q,
        inverse_q,
        query_in,
        query,
        keys_all,
        values_all,
        log_totals,
        attended,
        plain_two,
        inverse_two,
        normed_two,
        gate_pre,
        up_pre,
        hidden,
    ) = kept_values
    row_count = cotangent.shape[0]
    heads = query.shape[0]
    scale = HD ** (-0.5)
    grad_down = trans_times(cotangent, hidden)
    grad_hidden = jnp.dot(cotangent, down_w, preferred_element_type=jnp.float32)
    sigma = jax.nn.sigmoid(gate_pre)
    grad_gate = (grad_hidden * up_pre * sigma * (1.0 + gate_pre * (1.0 - sigma))).astype(
        jnp.bfloat16
    )
    grad_up = (grad_hidden * gate_pre * sigma).astype(jnp.bfloat16)
    grad_gate_w = trans_times(normed_two, grad_gate)
    grad_up_w = trans_times(normed_two, grad_up)
    grad_norm_two = lax.psum(times_trans(grad_gate, gate_w) + times_trans(grad_up, up_w), "tensor")
    grad_mid_part, grad_gain_two = rms_back(grad_norm_two, plain_two, inverse_two, gain_two)
    ffn_grads = (
        lax.psum_scatter(grad_gate_w, ("dp", "ctx"), scatter_dimension=0, tiled=True),
        lax.psum_scatter(grad_up_w, ("dp", "ctx"), scatter_dimension=0, tiled=True),
        lax.psum_scatter(grad_down, ("dp", "ctx"), scatter_dimension=0, tiled=True),
        lax.psum_scatter(grad_gain_two, ("dp", "ctx"), scatter_dimension=0, tiled=True),
    )
    grad_middle = cotangent.astype(jnp.float32) + grad_mid_part
    grad_branch = grad_middle.astype(jnp.bfloat16)
    grad_out_w = trans_times(grad_branch, attended)
    grad_attended = jnp.dot(grad_branch, out_w, preferred_element_type=jnp.float32).astype(
        jnp.bfloat16
    )
    grad_heads = grad_attended.reshape(row_count, heads, HD).transpose(1, 0, 2)

    def head_back(carry, item):
        key_acc, value_acc = carry
        q_head, grad_head, lse_head = item
        scores = jnp.where(allowed, times_trans(q_head, keys_all) * scale, -1e30)
        soft = jnp.exp(scores - lse_head[:, None])
        grad_soft = times_trans(grad_head, values_all)
        inner = jnp.sum(soft * grad_soft, axis=-1, keepdims=True)
        grad_scores = (soft * (grad_soft - inner)).astype(jnp.bfloat16)
        grad_q = jnp.dot(grad_scores, keys_all, preferred_element_type=jnp.float32) * scale
        key_acc = key_acc + trans_times(grad_scores, q_head) * scale
        value_acc = value_acc + trans_times(soft.astype(jnp.bfloat16), grad_head)
        return ((key_acc, value_acc), grad_q)

    empty = jnp.zeros(keys_all.shape, jnp.float32)
    (key_total, value_total), grad_query = lax.scan(
        head_back, (empty, empty), (query, grad_heads, log_totals)
    )
    key_own, value_own = (
        lax.psum_scatter(key_total, "ctx", scatter_dimension=0, tiled=True),
        lax.psum_scatter(value_total, "ctx", scatter_dimension=0, tiled=True),
    )
    grad_query_pre = (
        rotate(grad_query, -own_pos)
        .transpose(1, 0, 2)
        .reshape(row_count, heads * HD)
        .astype(jnp.bfloat16)
    )
    grad_up_q = trans_times(query_in, grad_query_pre)
    grad_qin_part = times_trans(grad_query_pre, up_q)
    grad_qin, grad_keys_rot, grad_values = lax.psum((grad_qin_part, key_own, value_own), "tensor")
    grad_key_pre = rotate(grad_keys_rot, -own_pos).astype(jnp.bfloat16)
    grad_value_low = grad_values.astype(jnp.bfloat16)
    grad_latent, grad_gain_q = rms_back(grad_qin, plain_q, inverse_q, gain_q)
    grad_latent_low = grad_latent.astype(jnp.bfloat16)
    grad_down_q = trans_times(normed, grad_latent_low)
    grad_key_w = trans_times(normed, grad_key_pre)
    grad_value_w = trans_times(normed, grad_value_low)
    grad_norm_one = (
        times_trans(grad_latent_low, down_q)
        + times_trans(grad_key_pre, key_w)
        + times_trans(grad_value_low, value_w)
    )
    grad_in_part, grad_gain_one = rms_back(grad_norm_one, plain_one, inverse_one, gain_one)
    grad_tokens = grad_middle + grad_in_part
    attention_grads = (
        lax.psum_scatter(grad_gain_one, ("dp", "ctx"), scatter_dimension=0, tiled=True),
        lax.psum_scatter(grad_down_q, ("dp", "ctx"), scatter_dimension=0, tiled=True),
        lax.psum_scatter(grad_gain_q, ("dp", "ctx"), scatter_dimension=0, tiled=True),
        lax.psum_scatter(grad_up_q, ("dp", "ctx"), scatter_dimension=0, tiled=True),
        lax.psum_scatter(grad_key_w, ("dp", "ctx"), scatter_dimension=0, tiled=True),
        lax.psum_scatter(grad_value_w, ("dp", "ctx"), scatter_dimension=0, tiled=True),
        lax.psum_scatter(grad_out_w, ("dp", "ctx"), scatter_dimension=0, tiled=True),
    )
    return (grad_tokens, attention_grads, ffn_grads)


def per_device(
    tokens_in,
    cotangent,
    seq_lengths,
    block_order,
    gain_one,
    down_q,
    gain_q,
    up_q,
    key_w,
    value_w,
    out_w,
    gain_two,
    gate_w,
    up_w,
    down_w,
):
    token_rows = tokens_in.astype(jnp.float32)
    row_count = tokens_in.shape[0]
    block_rows = row_count // 2
    places = (
        block_order[0][:, :, None] * block_rows
        + jnp.arange(block_rows, dtype=jnp.int32)[None, None, :]
    ).reshape(-1)
    second = (places >= seq_lengths[0, 0]).astype(jnp.int32)
    in_sequence = places - second * seq_lengths[0, 0]
    start = lax.axis_index("ctx") * row_count
    own_places = lax.dynamic_slice_in_dim(places, start, row_count)
    own_second = lax.dynamic_slice_in_dim(second, start, row_count)
    own_pos = lax.dynamic_slice_in_dim(in_sequence, start, row_count).astype(jnp.float32)
    allowed = (own_second[:, None] == second[None, :]) & (places[None, :] <= own_places[:, None])
    gains = (gain_one, gain_q, gain_two)
    attention_w = (
        lax.all_gather(down_q, ("dp", "ctx"), axis=0, tiled=True),
        lax.all_gather(up_q, ("dp", "ctx"), axis=0, tiled=True),
        lax.all_gather(key_w, ("dp", "ctx"), axis=0, tiled=True),
        lax.all_gather(value_w, ("dp", "ctx"), axis=0, tiled=True),
        lax.all_gather(out_w, ("dp", "ctx"), axis=0, tiled=True),
    )
    ffn_w = (
        lax.all_gather(gate_w, ("dp", "ctx"), axis=0, tiled=True),
        lax.all_gather(up_w, ("dp", "ctx"), axis=0, tiled=True),
        lax.all_gather(down_w, ("dp", "ctx"), axis=0, tiled=True),
    )
    result, kept_values = forward(token_rows, attention_w, ffn_w, gains, own_pos, allowed)
    attention_w = (
        lax.all_gather(down_q, ("dp", "ctx"), axis=0, tiled=True),
        lax.all_gather(up_q, ("dp", "ctx"), axis=0, tiled=True),
        lax.all_gather(key_w, ("dp", "ctx"), axis=0, tiled=True),
        lax.all_gather(value_w, ("dp", "ctx"), axis=0, tiled=True),
        lax.all_gather(out_w, ("dp", "ctx"), axis=0, tiled=True),
    )
    ffn_w = (
        lax.all_gather(gate_w, ("dp", "ctx"), axis=0, tiled=True),
        lax.all_gather(up_w, ("dp", "ctx"), axis=0, tiled=True),
        lax.all_gather(down_w, ("dp", "ctx"), axis=0, tiled=True),
    )
    unused, kept_values = forward(token_rows, attention_w, ffn_w, gains, own_pos, allowed)
    grad_tokens, attention_grads, ffn_grads = backward(
        cotangent, attention_w, ffn_w, gains, own_pos, allowed, kept_values
    )
    grad_gain_one, grad_down_q, grad_gain_q, grad_up_q, grad_key_w, grad_value_w, grad_out_w = (
        attention_grads
    )
    grad_gate_w, grad_up_w, grad_down_w, grad_gain_two = ffn_grads
    return (
        result.astype(jnp.bfloat16),
        grad_tokens,
        grad_gain_one,
        grad_down_q,
        grad_gain_q,
        grad_up_q,
        grad_key_w,
        grad_value_w,
        grad_out_w,
        grad_gain_two,
        grad_gate_w,
        grad_up_w,
        grad_down_w,
    )


def solution(mesh):
    fast = dict(mesh.shape) == {"dp": 4, "ctx": 2, "tensor": 4}
    return jax.shard_map(
        fast_device if fast else per_device,
        mesh=mesh,
        in_specs=(
            P(("dp", "ctx"), None),
            P(("dp", "ctx"), None),
            P("dp", None),
            P("dp", None, None),
            P(),
            P(("dp", "ctx"), None),
            P(),
            P(("dp", "ctx"), "tensor"),
            P(("dp", "ctx"), None),
            P(("dp", "ctx"), None),
            P(("dp", "ctx"), "tensor"),
            P(),
            P(("dp", "ctx"), "tensor"),
            P(("dp", "ctx"), "tensor"),
            P(("dp", "ctx"), "tensor"),
        ),
        out_specs=(
            P(("dp", "ctx"), None),
            P(("dp", "ctx"), None),
            P(("dp", "ctx")),
            P(("dp", "ctx"), None),
            P(("dp", "ctx")),
            P(("dp", "ctx"), "tensor"),
            P(("dp", "ctx"), None),
            P(("dp", "ctx"), None),
            P(("dp", "ctx"), "tensor"),
            P(("dp", "ctx")),
            P(("dp", "ctx"), "tensor"),
            P(("dp", "ctx"), "tensor"),
            P(("dp", "ctx"), "tensor"),
        ),
        check_vma=False,
    )
```

```python
import jax
import jax.numpy as jnp
from jax import lax
from jax.experimental import pallas as pl
from jax.experimental.pallas import tpu as pltpu
from jax.sharding import PartitionSpec as P

HD = 256


EPSILON = 1e-06

AXES = ("dp", "ctx", "tensor")
BF = jnp.bfloat16
F32 = jnp.float32


def dot(left, right):
    return jnp.dot(left, right, preferred_element_type=F32)


def times_trans(left, right):
    return lax.dot_general(left, right, (((1,), (1,)), ((), ())), preferred_element_type=F32)


def trans_times(left, right):
    return lax.dot_general(left, right, (((0,), (0,)), ((), ())), preferred_element_type=F32)


def rms_parts(array):
    inverse = lax.rsqrt(jnp.mean(array * array, axis=-1, keepdims=True) + EPSILON)
    return (array * inverse, inverse)


def rms_back(grad_out, plain, inverse, gain):
    grad_plain = grad_out * gain
    grad_in = inverse * (grad_plain - plain * jnp.mean(grad_plain * plain, axis=-1, keepdims=True))
    return (grad_in, jnp.sum(grad_out * plain, axis=0))


def angles_of(places, half):
    freqs = 10000.0 ** (-jnp.arange(half, dtype=F32) / half)
    angles = places[:, None] * freqs[None, :]
    return (jnp.cos(angles), jnp.sin(angles))


def turn(array, cosine, sine):
    half = array.shape[-1] // 2
    first = array[..., :half]
    latter = array[..., half:]
    return jnp.concatenate(
        [first * cosine - latter * sine, latter * cosine + first * sine], axis=-1
    )


def routes(move):
    pairs = []
    for z in range(4):
        for x in range(2):
            for y in range(2):
                for c in range(2):
                    to = move(z, x, y, c)
                    if to is not None:
                        tz, tx, ty, tc = to
                        pairs.append(
                            (((z * 2 + x) * 2 + y) * 2 + c, ((tz * 2 + tx) * 2 + ty) * 2 + tc)
                        )
    return pairs


OVER_X = routes(lambda z, x, y, c: (z, 1 - x, y, c))
OVER_Y = routes(lambda z, x, y, c: (z, x, 1 - y, c))
OVER_XY = routes(lambda z, x, y, c: (z, 1 - x, 1 - y, c))
OVER_YC = routes(lambda z, x, y, c: (z, x, 1 - y, 1 - c))
OVER_C = routes(lambda z, x, y, c: (z, x, y, 1 - c))
TRANSPOSE = routes(lambda z, x, y, c: (z, c, y, x) if x != c else None)
Z_ONE = routes(lambda z, x, y, c: (z ^ 1, x, y, c))
Z_TWO = routes(lambda z, x, y, c: (z ^ 2, x, y, c))
Z_THREE = routes(lambda z, x, y, c: (z ^ 3, x, y, c))


def send(array, pairs):
    return lax.ppermute(array, AXES, pairs)


def transpose(array, stays):
    return jnp.where(stays, array, send(array, TRANSPOSE))


def after(array, *others):
    return lax.optimization_barrier((array, *others))[0]


def stage(*arrays):
    return lax.optimization_barrier(arrays)


def gather_z(array):
    return lax.all_gather(array, "dp", axis=0, tiled=True)


def reduce_z(slabs):
    return lax.psum_scatter(slabs, "dp", scatter_dimension=0, tiled=True)


def trade_z(slabs):
    n = slabs.shape[0] // 4
    return [slabs[:n]] + [
        send(slabs[k * n : (k + 1) * n], pairs)
        for k, pairs in ((1, Z_ONE), (2, Z_TWO), (3, Z_THREE))
    ]


WHOLE = pl.BlockSpec(memory_space=pltpu.VMEM)
HELD = pl.BlockSpec(memory_space=pl.ANY)
ROOMY = pltpu.CompilerParams(vmem_limit_bytes=56 * 1024 * 1024)


def cost(macs, moved, share=1):
    return pl.CostEstimate(
        flops=2 * macs // share // 1, bytes_accessed=moved // share // 1, transcendentals=0
    )


def place_copies(plan, numbers, buffers, shape, dtype):
    def body(numbers_ref, *refs):
        ins, out_ref, sem = refs[:-2], refs[-2], refs[-1]
        listed = plan(numbers_ref, ins, out_ref)
        for i, (condition, source, target) in enumerate(listed):
            copy = pltpu.make_async_copy(source, target, sem.at[i])
            if condition is None:
                copy.start()
            else:
                pl.when(condition)(copy.start)
        for i, (condition, source, target) in enumerate(listed):
            copy = pltpu.make_async_copy(source, target, sem.at[i])
            if condition is None:
                copy.wait()
            else:
                pl.when(condition)(copy.wait)

    moved = 2
    for extent in shape:
        moved *= extent
    return pl.pallas_call(
        body,
        grid_spec=pltpu.PrefetchScalarGridSpec(
            num_scalar_prefetch=1,
            grid=(1,),
            in_specs=[HELD] * len(buffers),
            out_specs=pl.BlockSpec(shape, lambda i, numbers_ref: (0, 0)),
            scratch_shapes=[pltpu.SemaphoreType.DMA((40,))],
        ),
        out_shape=jax.ShapeDtypeStruct(shape, dtype),
        compiler_params=ROOMY,
        cost_estimate=cost(0, 2 * moved),
    )(numbers, *buffers)


def attention_forward(query_pre, cosine, sine, keys, values, row_info, key_places):
    rows, width = query_pre.shape
    heads = width // HD
    chunk = 256
    half = HD // 2
    scale = HD ** (-0.5)

    def body(pre_ref, cos_ref, sin_ref, k_ref, v_ref, info_ref, place_ref, q_ref, o_ref, lse_ref):
        for i in range(rows // chunk):
            at = slice(i * chunk, (i + 1) * chunk)
            first, latter = pre_ref[at, :half], pre_ref[at, half:]
            co, si = cos_ref[at], sin_ref[at]
            q = jnp.concatenate([first * co - latter * si, latter * co + first * si], 1).astype(BF)
            q_ref[at] = q
            scores = times_trans(q, k_ref[...]) * scale
            allowed = (place_ref[...] <= info_ref[at, 0:1]) & (place_ref[...] >= info_ref[at, 1:2])
            scores = jnp.where(allowed, scores, -1e30)
            largest = jnp.max(scores, axis=-1, keepdims=True)
            exponent = jnp.exp(scores - largest)
            totals = jnp.sum(exponent, axis=-1, keepdims=True)
            soft = (exponent * (1.0 / totals)).astype(BF)
            o_ref[at] = dot(soft, v_ref[...]).astype(BF)
            lse_ref[0, at] = largest + jnp.log(totals)

    full = lambda h: (0, 0)
    by_head = lambda h: (0, h)
    return pl.pallas_call(
        body,
        grid=(heads,),
        in_specs=[
            pl.BlockSpec((rows, HD), by_head),
            pl.BlockSpec((rows, half), full),
            pl.BlockSpec((rows, half), full),
            pl.BlockSpec((rows, HD), full),
            pl.BlockSpec((rows, HD), full),
            pl.BlockSpec((rows, 2), full),
            pl.BlockSpec((1, rows), full),
        ],
        out_specs=[
            pl.BlockSpec((rows, HD), by_head),
            pl.BlockSpec((rows, HD), by_head),
            pl.BlockSpec((1, rows, 1), lambda h: (h, 0, 0)),
        ],
        out_shape=[
            jax.ShapeDtypeStruct((rows, width), BF),
            jax.ShapeDtypeStruct((rows, width), BF),
            jax.ShapeDtypeStruct((heads, rows, 1), F32),
        ],
        compiler_params=ROOMY,
        cost_estimate=cost(4 * rows * rows * width, 6 * rows * width),
    )(query_pre, cosine, sine, keys, values, row_info, key_places)


def attention_backward(query, grad_out, lse, cosine, sine, keys, values, row_info, key_places):
    rows, width = query.shape
    heads = width // HD
    chunk = 256
    half = HD // 2
    scale = HD ** (-0.5)

    def body(
        q_ref, do_ref, lse_ref, cos_ref, sin_ref, k_ref, v_ref, info_ref, place_ref, dq_ref, dk_ref, dv_ref
    ):
        @pl.when(pl.program_id(0) == 0)
        def clear():
            dk_ref[...] = jnp.zeros_like(dk_ref)
            dv_ref[...] = jnp.zeros_like(dv_ref)

        for i in range(rows // chunk):
            at = slice(i * chunk, (i + 1) * chunk)
            q, do = q_ref[at], do_ref[at]
            scores = times_trans(q, k_ref[...]) * scale
            allowed = (place_ref[...] <= info_ref[at, 0:1]) & (place_ref[...] >= info_ref[at, 1:2])
            soft = jnp.exp(jnp.where(allowed, scores, -1e30) - lse_ref[0, at])
            grad_soft = times_trans(do, v_ref[...])
            summed = jnp.sum(soft * grad_soft, axis=-1, keepdims=True)
            grad_scores = (soft * (grad_soft - summed)).astype(BF)
            dq = dot(grad_scores, k_ref[...]) * scale
            first, latter = dq[:, :half], dq[:, half:]
            co, si = cos_ref[at], sin_ref[at]
            dq_ref[at] = jnp.concatenate(
                [first * co + latter * si, latter * co - first * si], 1
            ).astype(BF)
            dk_ref[...] += trans_times(grad_scores, q) * scale
            dv_ref[...] += trans_times(soft.astype(BF), do)

    full = lambda h: (0, 0)
    by_head = lambda h: (0, h)
    return pl.pallas_call(
        body,
        grid=(heads,),
        in_specs=[
            pl.BlockSpec((rows, HD), by_head),
            pl.BlockSpec((rows, HD), by_head),
            pl.BlockSpec((1, rows, 1), lambda h: (h, 0, 0)),
            pl.BlockSpec((rows, half), full),
            pl.BlockSpec((rows, half), full),
            pl.BlockSpec((rows, HD), full),
            pl.BlockSpec((rows, HD), full),
            pl.BlockSpec((rows, 2), full),
            pl.BlockSpec((1, rows), full),
        ],
        out_specs=[
            pl.BlockSpec((rows, HD), by_head),
            pl.BlockSpec((rows, HD), full),
            pl.BlockSpec((rows, HD), full),
        ],
        out_shape=[
            jax.ShapeDtypeStruct((rows, width), BF),
            jax.ShapeDtypeStruct((rows, HD), F32),
            jax.ShapeDtypeStruct((rows, HD), F32),
        ],
        compiler_params=ROOMY,
        cost_estimate=cost(8 * rows * rows * width, 6 * rows * width),
    )(query, grad_out, lse, cosine, sine, keys, values, row_info, key_places)


def product_of_parts(parts, weight):
    rows = parts[0].shape[0]
    count = len(parts)
    width = weight.shape[1]

    def body(*refs):
        weight_ref, out_ref = refs[count:]
        for i in range(0, count, 4):
            left = jnp.concatenate([refs[j][...] for j in range(i, i + 4)], axis=0)
            out_ref[i * rows : (i + 4) * rows] = dot(left, weight_ref[...]).astype(BF)

    return pl.pallas_call(
        body,
        in_specs=[WHOLE] * (count + 1),
        out_specs=WHOLE,
        out_shape=jax.ShapeDtypeStruct((count * rows, width), BF),
        compiler_params=ROOMY,
        cost_estimate=cost(count * rows * weight.size, 2 * weight.size),
    )(*parts, weight)


def product_pieces(left, weight, extras, got, first_half):
    rows = left.shape[0] // 2
    part = rows // 4
    start = 0 if first_half else rows
    wide = weight.shape[0]
    total = wide + sum(e.shape[1] for e in extras)
    outs = 4 if first_half else 1

    def body(left_ref, weight_ref, *refs):
        extra_refs = refs[: len(extras)]
        got_ref = refs[len(extras)] if got is not None else None
        out_refs = refs[len(refs) - outs :]
        src = slice(start, start + rows)

        def put(value, cols):
            if got_ref is not None:
                value = value + got_ref[:, cols].astype(F32)
            value = value.astype(BF)
            if outs == 1:
                out_refs[0][:, cols] = value
            else:
                for f in range(4):
                    out_refs[f][:, cols] = value[f * part : (f + 1) * part]

        step = 512
        for col in range(0, wide, step):
            put(times_trans(left_ref[src], weight_ref[col : col + step]), slice(col, col + step))
        col = wide
        for extra_ref in extra_refs:
            n = extra_ref.shape[1]
            put(extra_ref[src], slice(col, col + n))
            col += n

    shapes = [jax.ShapeDtypeStruct((part, total), BF)] * 4
    if outs == 1:
        shapes = [jax.ShapeDtypeStruct((rows, total), BF)]
    arrays = [left, weight, *extras] + ([got] if got is not None else [])
    return pl.pallas_call(
        body,
        in_specs=[WHOLE] * len(arrays),
        out_specs=[WHOLE] * outs,
        out_shape=shapes,
        compiler_params=ROOMY,
        cost_estimate=cost(rows * wide * left.shape[1], 2 * weight.size + 4 * rows * total),
    )(*arrays)


def tiles_of(width):
    whole = width // 256
    return whole, width - whole * 256


def ffn_forward(numbers, parts, pairs):
    part, depth = parts[0].shape
    rows = part * len(parts)
    width = pairs[0].shape[1]
    whole, rest = tiles_of(width)

    def body(numbers_ref, *refs):
        part_refs, pair_refs = refs[:4], refs[4:6]
        hid_ref, slope_ref, silu_ref, gate_vm, up_vm, in_vm, sem = refs[6:]
        gate_copies, up_copies = [], []
        for i in range(8):
            to = pl.ds(pl.multiple_of(numbers_ref[i] * 256, 256), 256)
            ref, at = pair_refs[i // 4], (i % 4) * 512
            gate_copies.append(
                pltpu.make_async_copy(ref.at[at : at + 256], gate_vm.at[to], sem.at[i])
            )
            up_copies.append(
                pltpu.make_async_copy(ref.at[at + 256 : at + 512], up_vm.at[to], sem.at[8 + i])
            )
        for copy in gate_copies + up_copies:
            copy.start()
        for f in range(4):
            in_vm[f * part : (f + 1) * part] = part_refs[f][...]
        for copy in gate_copies + up_copies:
            copy.wait()

        def tile(cols):
            gate = dot(in_vm[...], gate_vm[:, cols])
            up = dot(in_vm[...], up_vm[:, cols])
            sigma = jax.nn.sigmoid(gate)
            silu = gate * sigma
            hid_ref[:, cols] = (silu * up).astype(BF)
            slope_ref[:, cols] = up * sigma * (1.0 + gate * (1.0 - sigma))
            silu_ref[:, cols] = silu

        @pl.loop(0, whole)
        def each(i):
            tile(pl.ds(pl.multiple_of(i * 256, 256), 256))

        if rest:
            tile(slice(whole * 256, width))

    return pl.pallas_call(
        body,
        grid_spec=pltpu.PrefetchScalarGridSpec(
            num_scalar_prefetch=1,
            grid=(1,),
            in_specs=[pl.BlockSpec((part, depth), lambda i, n: (0, 0))] * 4 + [HELD] * 2,
            out_specs=[pl.BlockSpec((rows, width), lambda i, n: (0, 0))] * 3,
            scratch_shapes=[
                pltpu.VMEM((depth, width), BF),
                pltpu.VMEM((depth, width), BF),
                pltpu.VMEM((rows, depth), BF),
                pltpu.SemaphoreType.DMA((16,)),
            ],
        ),
        out_shape=[
            jax.ShapeDtypeStruct((rows, width), BF),
            jax.ShapeDtypeStruct((rows, width), F32),
            jax.ShapeDtypeStruct((rows, width), F32),
        ],
        compiler_params=ROOMY,
        cost_estimate=cost(2 * rows * depth * width, 4 * depth * width),
    )(numbers, *parts, *pairs)


def ffn_backward(numbers, cot, slope, silu, pairs, downs):
    rows = slope.shape[0]
    depth = cot.shape[1]
    part = rows // 4
    width = slope.shape[1]
    whole, rest = tiles_of(width)

    def body(numbers_ref, *refs):
        cot_ref, slope_ref, silu_ref = refs[:3]
        pair_refs, down_refs = refs[3:5], refs[5:7]
        gate_out, up_out = refs[7:9]
        piece_refs = refs[9:13]
        down_vm, pair_vm, sem = refs[13:]
        copies, later = [], []
        for i in range(8):
            to = pl.ds(pl.multiple_of(numbers_ref[i] * 256, 256), 256)
            ref, at = down_refs[i // 4], (i % 4) * 256
            copies.append(
                pltpu.make_async_copy(ref.at[at : at + 256], down_vm.at[to], sem.at[i])
            )
            ref, at = pair_refs[i // 4], (i % 4) * 512
            later.append(
                pltpu.make_async_copy(ref.at[at : at + 512], pair_vm.at[i], sem.at[8 + i])
            )
        for copy in copies + later:
            copy.start()
        for copy in copies:
            copy.wait()

        def tile(cols):
            grad = dot(cot_ref[...], down_vm[:, cols])
            gate_out[:, cols] = (grad * slope_ref[:, cols]).astype(BF)
            up_out[:, cols] = (grad * silu_ref[:, cols]).astype(BF)

        @pl.loop(0, whole)
        def each(i):
            tile(pl.ds(pl.multiple_of(i * 256, 256), 256))

        if rest:
            tile(slice(whole * 256, width))
        for copy in later:
            copy.wait()

        @pl.loop(0, 8)
        def block(i):
            cols = pl.ds(pl.multiple_of(numbers_ref[i] * 256, 256), 256)
            value = times_trans(gate_out[...], pair_vm[i, :256]) + times_trans(
                up_out[...], pair_vm[i, 256:]
            )
            value = value.astype(BF)
            for f in range(4):
                piece_refs[f][:, cols] = value[f * part : (f + 1) * part]

    flat = lambda i, n: (0, 0)
    return pl.pallas_call(
        body,
        grid_spec=pltpu.PrefetchScalarGridSpec(
            num_scalar_prefetch=1,
            grid=(1,),
            in_specs=[
                pl.BlockSpec((rows, depth), flat),
                pl.BlockSpec((rows, width), flat),
                pl.BlockSpec((rows, width), flat),
            ]
            + [HELD] * 4,
            out_specs=[pl.BlockSpec((rows, width), flat)] * 2
            + [pl.BlockSpec((part, depth), flat)] * 4,
            scratch_shapes=[
                pltpu.VMEM((depth, width), BF),
                pltpu.VMEM((8, 512, width), BF),
                pltpu.SemaphoreType.DMA((16,)),
            ],
        ),
        out_shape=[jax.ShapeDtypeStruct((rows, width), BF)] * 2
        + [jax.ShapeDtypeStruct((part, depth), BF)] * 4,
        compiler_params=ROOMY,
        cost_estimate=cost(3 * rows * depth * width, 6 * depth * width),
    )(numbers, cot, slope, silu, *pairs, *downs)


def ffn_output(numbers, hidden, downs):
    rows, width = hidden.shape
    part = rows // 4
    depth = 2 * downs[0].shape[0]

    def body(numbers_ref, hid_ref, *refs):
        down_refs, piece_refs = refs[:2], refs[2:6]
        down_vm, sem = refs[6:]
        copies = [
            pltpu.make_async_copy(
                down_refs[i // 4].at[(i % 4) * 256 : (i % 4 + 1) * 256], down_vm.at[i], sem.at[i]
            )
            for i in range(8)
        ]
        for copy in copies:
            copy.start()
        for copy in copies:
            copy.wait()

        @pl.loop(0, 8)
        def block(i):
            cols = pl.ds(pl.multiple_of(numbers_ref[i] * 256, 256), 256)
            value = times_trans(hid_ref[...], down_vm[i]).astype(BF)
            for f in range(4):
                piece_refs[f][:, cols] = value[f * part : (f + 1) * part]

    flat = lambda i, n: (0, 0)
    return pl.pallas_call(
        body,
        grid_spec=pltpu.PrefetchScalarGridSpec(
            num_scalar_prefetch=1,
            grid=(1,),
            in_specs=[pl.BlockSpec((rows, width), flat)] + [HELD] * 2,
            out_specs=[pl.BlockSpec((part, depth), flat)] * 4,
            scratch_shapes=[
                pltpu.VMEM((8, 256, width), BF),
                pltpu.SemaphoreType.DMA((8,)),
            ],
        ),
        out_shape=[jax.ShapeDtypeStruct((part, depth), BF)] * 4,
        compiler_params=ROOMY,
        cost_estimate=cost(rows * depth * width, 2 * depth * width, 4),
    )(numbers, hidden, *downs)


def weight_grads(numbers, terms, width):
    lefts, rights, left_specs, right_specs = [], [], [], []
    shape_of = []
    for left, block, offset, products in terms:
        for array in left:
            lefts.append(array)
            left_specs.append(
                pl.BlockSpec((array.shape[0], block), lambda i, n, offset=offset: (0, n[offset + i]))
            )
        for place, right in products:
            for array, start, count, pick in right:
                rights.append(array)
                if pick is None:
                    right_specs.append(pl.BlockSpec(array.shape, lambda i, n: (0, 0)))
                else:
                    right_specs.append(
                        pl.BlockSpec((array.shape[0], width), lambda i, n, pick=pick: (0, n[pick]))
                    )
        shape_of.append(block)
    height = sum(shape_of)

    def body(numbers_ref, *refs):
        left_refs = refs[: len(lefts)]
        right_refs = refs[len(lefts) : len(lefts) + len(rights)]
        out_ref = refs[-1]
        li, ri, row = 0, 0, 0
        for left, block, offset, products in terms:
            pieces = [left_refs[li + j][...] for j in range(len(left))]
            li += len(left)
            whole = pieces[0] if len(pieces) == 1 else jnp.concatenate(pieces, axis=0)
            for place, right in products:
                value = None
                at = 0
                for array, start, count, pick in right:
                    this = trans_times(
                        whole[at : at + count], right_refs[ri][start : start + count]
                    )
                    value = this if value is None else value + this
                    at += count
                    ri += 1
                value = value.astype(BF)
                n = value.shape[1]
                if place is None:
                    cols = slice(0, n)
                else:
                    cols = pl.ds(pl.multiple_of(numbers_ref[place] * n, n), n)
                out_ref[row : row + block, cols] = value

            row += block

    macs = 4 * height * width * 1024
    return pl.pallas_call(
        body,
        grid_spec=pltpu.PrefetchScalarGridSpec(
            num_scalar_prefetch=1,
            grid=(4,),
            in_specs=left_specs + right_specs,
            out_specs=pl.BlockSpec((height, width), lambda i, n: (i, 0)),
        ),
        out_shape=jax.ShapeDtypeStruct((4 * height, width), BF),
        compiler_params=ROOMY,
        cost_estimate=cost(macs, 4 * height * width * 4, 4),
    )(numbers, *lefts, *rights)


def input_gradient(numbers, grad_lat, first_all, grad_mid, tokens, gain):
    depth = tokens.shape[1]
    wide = grad_lat.shape[1]
    part = 128

    def body(numbers_ref, lat_ref, first_ref, mid_ref, tok_ref, gain_ref, out_ref, grad_vm):
        for col in range(0, depth, 512):
            cols = slice(col, col + 512)
            grad_vm[:, cols] = times_trans(lat_ref[...], first_ref[cols]) * gain_ref[:, cols]
        for i in range(4):
            at = slice(i * part, (i + 1) * part)
            plain = tok_ref[at].astype(F32)
            inverse = lax.rsqrt(jnp.mean(plain * plain, axis=-1, keepdims=True) + EPSILON)
            plain = plain * inverse
            grad = grad_vm[at]
            mean = jnp.mean(grad * plain, axis=-1, keepdims=True)
            to = pl.ds(pl.multiple_of(numbers_ref[9 + i] * part, part), part)
            out_ref[to] = mid_ref[at].astype(F32) + inverse * (grad - plain * mean)

    picked = lambda i, n: (n[8], 0)
    flat = lambda i, n: (0, 0)
    return pl.pallas_call(
        body,
        grid_spec=pltpu.PrefetchScalarGridSpec(
            num_scalar_prefetch=1,
            grid=(1,),
            in_specs=[
                pl.BlockSpec((4 * part, wide), picked),
                pl.BlockSpec((depth, wide), flat),
                pl.BlockSpec((4 * part, depth), picked),
                pl.BlockSpec((4 * part, depth), picked),
                pl.BlockSpec((1, depth), flat),
            ],
            out_specs=pl.BlockSpec((4 * part, depth), flat),
            scratch_shapes=[pltpu.VMEM((4 * part, depth), F32)],
        ),
        out_shape=jax.ShapeDtypeStruct((4 * part, depth), F32),
        compiler_params=ROOMY,
        cost_estimate=cost(4 * part * depth * wide, 2 * depth * wide + 8 * part * depth * 4),
    )(numbers, grad_lat, first_all, grad_mid, tokens, gain.reshape(1, -1))


def first_finish(numbers, quarters, first_w, gain, latent_width):
    rows, lane = quarters[0].shape
    wide = first_w.shape[1]

    def body(numbers_ref, *refs):
        weight_ref, gain_ref, down_ref, key_ref, value_ref, one_ref, all_vm = refs[4:]
        for i in range(4):
            cols = pl.ds(pl.multiple_of(numbers_ref[25 + i] * lane, lane), lane)
            all_vm[:, cols] = refs[i][...].astype(F32)
        down_ref[...] = all_vm[:, :latent_width]
        key_ref[...] = all_vm[:, latent_width : latent_width + HD]
        value_ref[...] = all_vm[:, latent_width + HD :]
        total = jnp.sum(weight_ref[...].astype(F32) * all_vm[...], axis=1, keepdims=True)
        one_ref[...] = total / gain_ref[...]

    flat = lambda i, n: (0, 0)
    extents = [(rows, latent_width), (rows, HD), (rows, wide - latent_width - HD), (rows, 1)]
    *grads, one = pl.pallas_call(
        body,
        grid_spec=pltpu.PrefetchScalarGridSpec(
            num_scalar_prefetch=1,
            grid=(1,),
            in_specs=[pl.BlockSpec((rows, lane), flat)] * 4
            + [pl.BlockSpec((rows, wide), flat), pl.BlockSpec((rows, 1), flat)],
            out_specs=[pl.BlockSpec(e, flat) for e in extents],
            scratch_shapes=[pltpu.VMEM((rows, wide), F32)],
        ),
        out_shape=[jax.ShapeDtypeStruct(e, F32) for e in extents],
        compiler_params=ROOMY,
        cost_estimate=cost(0, 10 * rows * wide),
    )(numbers, *quarters, first_w, gain.reshape(-1, 1))
    return (*grads, one.reshape(-1))


def trade(pieces):
    own, y_piece, x_piece, xy_piece = pieces
    return [own, send(y_piece, OVER_Y), send(x_piece, OVER_X), send(xy_piece, OVER_XY)]


def added(pieces):
    total = pieces[0].astype(F32)
    for piece in pieces[1:]:
        total = total + piece.astype(F32)
    return total


def sum_pieces(pieces):
    return added(trade(pieces))


def spread(part):
    return [part, send(part, OVER_Y), send(part, OVER_X), send(part, OVER_XY)]


def over_core(arrays):
    return [send(array, OVER_C) for array in arrays]


def fast_device(
    tokens_in,
    cotangent,
    seq_lengths,
    block_order,
    gain_one,
    down_q,
    gain_q,
    up_q,
    key_w,
    value_w,
    out_w,
    gain_two,
    gate_w,
    up_w,
    down_w,
):
    z = lax.axis_index("dp")
    x = lax.axis_index("ctx")
    t = lax.axis_index("tensor")
    y = t // 2
    c = t % 2
    stays = x == c
    quarter = x * 2 + y
    rows, depth = tokens_in.shape
    half = rows // 2
    part = rows // 4
    latent_width = down_q.shape[1]
    cols = up_q.shape[1] // 2
    ks = jnp.arange(4, dtype=jnp.int32)
    z_order = z ^ ks
    numbers = jnp.concatenate(
        [
            ks * 2 + c,
            ks * 2 + (1 - c),
            jnp.stack([c ^ x]),
            quarter ^ ks,
            z_order * 2 + x,
            z_order * 2 + (1 - x),
            jnp.stack([c, 1 - c, x, 1 - x, t, t ^ 1, t ^ 2, t ^ 3]),
        ]
    ).astype(jnp.int32)
    at_same, at_quarter, at_x, at_c, at_t = 8, 9, 13, 21, 25

    first_w = jnp.concatenate([down_q, key_w, value_w], axis=1)
    wide = first_w.shape[1]
    side = wide // 4
    mine = lax.dynamic_slice_in_dim(first_w, t * side, side, axis=1)
    attn_t = transpose(jnp.concatenate([up_q, out_w], axis=0), stays)
    tok_got = send(rows_at(tokens_in, t * part, part), OVER_X)
    tok_y = send(tok_got, OVER_Y)
    first_own = stage(mine, send(mine, Z_ONE), send(mine, Z_TWO), send(mine, Z_THREE))
    attn_own = gather_z(after(attn_t, *first_own))
    first_own = jnp.concatenate(first_own, axis=0)
    pair_t = transpose(after(jnp.concatenate([gate_w, up_w], axis=0), first_own), stays)
    first_blocks = [first_own] + [send(first_own, p) for p in (OVER_Y, OVER_X, OVER_XY)]

    def first_plan(n, ins, out):
        listed = []
        for i in range(8):
            col = pl.ds(pl.multiple_of(n[at_t + (0, 2, 0, 2, 1, 3, 1, 3)[i]] * side, side), side)
            for k in range(4):
                place = n[at_x + (i % 4 // 2) * 4 + k]
                row = pl.ds(pl.multiple_of(place * 256, 256), 256)
                listed.append((None, ins[i].at[k * 256 : (k + 1) * 256], out.at[row, col]))
        return listed

    pair_own = gather_z(after(pair_t, attn_own))
    first_blocks = first_blocks + over_core(first_blocks)

    def first_plan(n, ins, out):
        listed = []
        for i in range(8):
            col = pl.ds(pl.multiple_of(n[at_t + (0, 2, 0, 2, 1, 3, 1, 3)[i]] * side, side), side)
            for k in range(4):
                place = n[at_x + (i % 4 // 2) * 4 + k]
                row = pl.ds(pl.multiple_of(place * 256, 256), 256)
                listed.append((None, ins[i].at[k * 256 : (k + 1) * 256], out.at[row, col]))
        return listed

    ffn_t = transpose(
        after(jnp.concatenate([gate_w, up_w, down_w], axis=0), first_own), stays
    )
    tok_y = send(tok_got, OVER_Y)
    *first_blocks, ffn_t, tok_got, tok_y = stage(*first_blocks[:4], ffn_t, tok_got, tok_y)
    ffn_own = gather_z(ffn_t)
    first_blocks = first_blocks + over_core(first_blocks)
    first_all = place_copies(first_plan, numbers, first_blocks, (depth, wide), BF)

    def rows_plan(n, ins, out):
        listed = []
        for o in range(2):
            mine_too = (n[at_same] == o)
            for f in range(4):
                q = n[at_quarter + f]
                to = out.at[pl.ds((o * 4 + f) * part, part)]
                here = pl.ds(pl.multiple_of(q * part, part), part)
                listed.append((mine_too, ins[0].at[here], to))
                away = jnp.logical_not(mine_too)
                for j in range(4):
                    listed.append((away & (n[at_t + j] == q), ins[1 + j], to))
        return listed

    def group_rows(array, got, got_y):
        buffers = [array, got, send(got, OVER_C), got_y, send(got_y, OVER_C)]
        return place_copies(rows_plan, numbers, buffers, (2 * rows, depth), BF)

    tokens = group_rows(tokens_in, tok_got, tok_y)

    attn_rows = attn_t.shape[0]
    upq_rows = up_q.shape[0]
    out_rows = out_w.shape[0]

    def head_plan(start, count):
        def plan(n, ins, out):
            listed = []
            for i in range(8):
                row = pl.ds(pl.multiple_of(n[i] * count, count), count)
                col = pl.ds(pl.multiple_of(n[at_c] * cols, cols), cols)
                at = (i % 4) * attn_rows + start
                listed.append((None, ins[i // 4].at[at : at + count, col], out.at[row]))
            return listed

        return plan


    places = (
        block_order[0][:, :, None] * half + jnp.arange(half, dtype=jnp.int32)[None, None, :]
    ).reshape(2, 4, part)
    places = jnp.stack(
        [
            lax.dynamic_index_in_dim(
                lax.dynamic_index_in_dim(places, c ^ o, 0, False), quarter ^ f, 0, False
            )
            for o in range(2)
            for f in range(4)
        ]
    ).reshape(-1)
    second = (places >= seq_lengths[0, 0]).astype(jnp.int32)
    sequence_start = second * seq_lengths[0, 0]
    cosine, sine = angles_of((places - sequence_start).astype(F32), HD // 2)
    row_info = jnp.stack([places, sequence_start], axis=1)
    key_places = places[None, :]

    token_rows = tokens.astype(F32)
    plain_one, inverse_one = rms_parts(token_rows)
    normed = (plain_one * gain_one).astype(BF)
    lat = dot(after(normed, attn_own), first_all)
    down_t = transpose(after(down_w, lat), stays)
    cot_got = send(after(rows_at(cotangent, t * part, part), lat), OVER_X)
    cot_y = send(cot_got, OVER_Y)
    attns = [attn_own, send(attn_own, OVER_C)]
    up_q_all = place_copies(
        head_plan(0, upq_rows), numbers, attns, (latent_width, cols), BF
    )
    out_all = place_copies(
        head_plan(upq_rows, out_rows), numbers, attns, (depth, cols), BF
    )
    latent = lat[:, :latent_width]
    plain_q, inverse_q = rms_parts(latent)
    query_in = (plain_q * gain_q).astype(BF)
    keys = turn(lat[:, latent_width : latent_width + HD], cosine, sine).astype(BF)
    values = lat[:, latent_width + HD :].astype(BF)
    query_pre = dot(query_in, up_q_all)
    query, attended, lse = attention_forward(
        query_pre, cosine, sine, keys, values, row_info, key_places
    )
    down_t, cot_got, cot_y, attended = stage(down_t, cot_got, cot_y, attended)
    cot = group_rows(cotangent, cot_got, cot_y)
    (give,) = product_pieces(attended, out_all, [], None, False)
    pieces = product_pieces(attended, out_all, [], send(give, OVER_C), True)
    *pieces, cot, pair_own = stage(*trade(pieces), cot, pair_own)
    middle = tokens[:part].astype(F32) + added(pieces)
    down_own = gather_z(after(down_t, pair_own))
    pairs = [pair_own, send(pair_own, OVER_C)]

    plain_two, inverse_two = rms_parts(middle)
    two_parts = spread((plain_two * gain_two).astype(BF))
    hidden, slope, silu = ffn_forward(numbers, two_parts, pairs)

    def two(array, other):
        return [(array, 0, rows, None), (other, 0, rows, None)]

    width = down_w.shape[1]
    (hidden_other,) = over_core([hidden])
    down_slabs = weight_grads(
        numbers, [([cot], 256, 0, [(None, two(hidden, hidden_other))])], width
    )
    two_other = over_core(two_parts)
    down_slabs, hidden, down_own, *two_other = stage(
        down_slabs, hidden, down_own, *two_other
    )
    down_sum = reduce_z(down_slabs)
    downs = [down_own, send(down_own, OVER_C)]
    grad_gate, grad_up, *pieces = ffn_backward(
        numbers, after(cot, down_slabs), slope, silu, pairs, downs
    )

    gate_other, up_other = over_core([grad_gate, grad_up])
    two_all = list(two_parts) + list(two_other)
    pair_slabs = weight_grads(
        numbers,
        [
            (two_all, 256, 0, [(None, two(grad_gate, gate_other))]),
            (two_all, 256, 0, [(None, two(grad_up, up_other))]),
        ],
        width,
    )
    *pieces, pair_slabs, hidden = stage(*trade(pieces), pair_slabs, hidden)
    grad_norm_two = added(pieces)
    pair_sum = reduce_z(after(pair_slabs, down_sum))

    grad_plain = grad_norm_two * gain_two
    grad_mid = cot[:part].astype(F32) + inverse_two * (
        grad_plain - plain_two * jnp.mean(grad_plain * plain_two, axis=-1, keepdims=True)
    )
    mid_parts = spread(grad_mid.astype(BF))
    staged = stage(*mid_parts, *ffn_output(numbers, hidden, downs))
    mid_parts, out_pieces = list(staged[:4]), staged[4:]
    mid_parts = mid_parts + over_core(mid_parts)

    def stack_plan(n, ins, out):
        return [(None, ins[i], out.at[pl.ds(i * part, part)]) for i in range(8)]

    grad_attended = product_of_parts(mid_parts, out_all)
    grad_query_pre, key_acc, value_acc = attention_backward(
        query, grad_attended, lse, cosine, sine, keys, values, row_info, key_places
    )
    down_home = transpose(down_sum, stays)
    grad_branch = place_copies(stack_plan, numbers, mid_parts, (2 * rows, depth), BF)
    attended_other = send(after(attended, mid_parts[4]), OVER_C)
    *out_sum, grad_query_pre, key_acc, value_acc, down_home, grad_branch, attended_other = stage(
        *trade(out_pieces),
        grad_query_pre,
        key_acc,
        value_acc,
        down_home,
        grad_branch,
        attended_other,
    )

    out_part = (middle + added(out_sum)).astype(BF)
    out_other = send(out_part, OVER_C)
    out_mine = jnp.where(stays, out_part, out_other)
    out_away = rows_at(jnp.where(stays, out_other, out_part), c * (part // 2), part // 2)
    extras = [key_acc, value_acc]
    (give,) = product_pieces(grad_query_pre, up_q_all, extras, None, False)
    pieces = product_pieces(grad_query_pre, up_q_all, extras, send(give, OVER_C), True)
    staged = stage(
        *pieces,
        out_mine,
        send(rows_at(out_mine, c * (part // 2), part // 2), OVER_Y),
        send(out_away, OVER_X),
        send(out_away, OVER_XY),
    )
    pieces, out_parts = staged[:4], list(staged[4:])
    query_other = send(grad_query_pre, OVER_C)

    def swapped(array):
        return [(array, rows, rows, None), (array, 0, rows, None)]

    attn_slabs = weight_grads(
        numbers,
        [
            (
                [query_in],
                upq_rows,
                0,
                [
                    (at_c, [(grad_query_pre, 0, 2 * rows, None)]),
                    (at_c + 1, swapped(query_other)),
                ],
            ),
            (
                mid_parts,
                out_rows,
                0,
                [
                    (at_c, [(attended, 0, 2 * rows, None)]),
                    (at_c + 1, swapped(attended_other)),
                ],
            ),
        ],
        2 * cols,
    )
    *pieces, attn_slabs = stage(*trade(pieces), attn_slabs)
    three = added(pieces)
    attn_sum = reduce_z(after(attn_slabs, pair_sum))

    grad_plain = three[:, :latent_width] * gain_q
    plain_q_mine = plain_q[:part]
    grad_latent = inverse_q[:part] * (
        grad_plain - plain_q_mine * jnp.mean(grad_plain * plain_q_mine, axis=-1, keepdims=True)
    )
    grad_key_pre = turn(
        three[:, latent_width : latent_width + HD], cosine[:part], -sine[:part]
    )
    lat_parts = spread(
        jnp.concatenate(
            [grad_latent, grad_key_pre, three[:, latent_width + HD :]], axis=1
        ).astype(BF)
    )
    *lat_parts, pair_sum = stage(*lat_parts, pair_sum)
    pair_home = transpose(pair_sum, stays)
    lat_parts = lat_parts + over_core(lat_parts)

    lane = wide // 4
    first_slabs = weight_grads(
        numbers,
        [([normed], 256, at_x, [(None, [(p, 0, part, at_t) for p in lat_parts])])],
        lane,
    )
    first_slabs, pair_home, *lat_parts = stage(first_slabs, pair_home, *lat_parts)
    grad_lat = place_copies(stack_plan, numbers, lat_parts, (2 * rows, wide), BF)
    grad_tokens = input_gradient(numbers, grad_lat, first_all, grad_branch, tokens, gain_one)

    out_parts = out_parts + over_core(out_parts[1:])

    def out_plan(n, ins, out):
        listed = []
        for f in range(4):
            row = n[at_quarter + f] * part
            if f == 0:
                to = out.at[pl.ds(pl.multiple_of(row, part), part)]
                listed.append((None, ins[0], to))
                continue
            for j in range(2):
                at = pl.multiple_of(row + n[at_c + j] * (part // 2), part // 2)
                listed.append((None, ins[f + 3 * j], out.at[pl.ds(at, part // 2)]))
        return listed

    *first_got, grad_tokens = stage(*trade_z(first_slabs), grad_tokens)
    first_quarter = added(first_got).astype(BF)
    quarters = [first_quarter] + [send(first_quarter, p) for p in (OVER_C, OVER_Y, OVER_YC)]
    quarters = stage(*quarters)
    attn_home = transpose(after(attn_sum, *quarters), stays)
    dev = z * 2 + x
    block = depth // 8
    own_one = lax.dynamic_slice_in_dim(gain_one, dev * block, block)
    grad_down_q, grad_key_w, grad_value_w, grad_gain_one = first_finish(
        numbers, quarters, first_w, own_one, latent_width
    )
    result = place_copies(out_plan, numbers, out_parts, (rows, depth), BF)

    grad_down_w = down_home.astype(F32)
    pair_home = pair_home.astype(F32)
    grad_gate_w, grad_up_w = pair_home[:256], pair_home[256:]
    attn_home = attn_home.astype(F32)
    grad_up_q, grad_out_w = attn_home[:upq_rows], attn_home[upq_rows:]

    own_two = lax.dynamic_slice_in_dim(gain_two, dev * block, block)
    own_q = lax.dynamic_slice_in_dim(gain_q, dev * upq_rows, upq_rows)
    two_sum = jnp.sum(gate_w.astype(F32) * grad_gate_w + up_w.astype(F32) * grad_up_w, axis=1)
    q_sum = jnp.sum(up_q.astype(F32) * grad_up_q, axis=1)
    small = jnp.concatenate([two_sum, q_sum]).reshape(3, -1)
    small = small + send(small, OVER_C) + send(small, OVER_Y) + send(small, OVER_YC)
    small = small.reshape(-1)
    grad_gain_two = small[:block] / own_two
    grad_gain_q = small[block:] / own_q

    return (
        result,
        grad_tokens,
        grad_gain_one,
        grad_down_q,
        grad_gain_q,
        grad_up_q,
        grad_key_w,
        grad_value_w,
        grad_out_w,
        grad_gain_two,
        grad_gate_w,
        grad_up_w,
        grad_down_w,
    )


def rows_at(array, start, count):
    return lax.dynamic_slice_in_dim(array, start, count, axis=0)


def rotate(array, places):
    half = array.shape[-1] // 2
    freqs = 10000.0 ** (-jnp.arange(half, dtype=jnp.float32) / half)
    angles = places[:, None] * freqs[None, :]
    cosine = jnp.cos(angles)
    sine = jnp.sin(angles)
    first = array[..., :half]
    latter = array[..., half:]
    return jnp.concatenate(
        [first * cosine - latter * sine, latter * cosine + first * sine], axis=-1
    )


def forward(token_rows, attention_w, ffn_w, gains, own_pos, allowed):
    gain_one, gain_q, gain_two = gains
    down_q, up_q, key_w, value_w, out_w = attention_w
    gate_w, up_w, down_w = ffn_w
    row_count = token_rows.shape[0]
    heads = up_q.shape[1] // HD
    scale = HD ** (-0.5)
    plain_one, inverse_one = rms_parts(token_rows)
    normed = (plain_one * gain_one).astype(jnp.bfloat16)
    latent = jnp.dot(normed, down_q, preferred_element_type=jnp.float32)
    plain_q, inverse_q = rms_parts(latent)
    query_in = (plain_q * gain_q).astype(jnp.bfloat16)
    query_pre = jnp.dot(query_in, up_q, preferred_element_type=jnp.float32)
    query = rotate(query_pre.reshape(row_count, heads, HD).transpose(1, 0, 2), own_pos).astype(
        jnp.bfloat16
    )
    keys = rotate(jnp.dot(normed, key_w, preferred_element_type=jnp.float32), own_pos).astype(
        jnp.bfloat16
    )
    values = jnp.dot(normed, value_w, preferred_element_type=jnp.float32).astype(jnp.bfloat16)
    keys_all, values_all = (
        lax.all_gather(keys, "ctx", axis=0, tiled=True),
        lax.all_gather(values, "ctx", axis=0, tiled=True),
    )

    def one_head(q_head):
        scores = jnp.where(allowed, times_trans(q_head, keys_all) * scale, -1e30)
        largest = jnp.max(scores, axis=-1, keepdims=True)
        exponent = jnp.exp(scores - largest)
        totals = jnp.sum(exponent, axis=-1, keepdims=True)
        soft = (exponent / totals).astype(jnp.bfloat16)
        return (
            jnp.dot(soft, values_all, preferred_element_type=jnp.float32),
            (largest + jnp.log(totals))[:, 0],
        )

    mixed_heads, log_totals = lax.map(one_head, query)
    attended = mixed_heads.transpose(1, 0, 2).reshape(row_count, heads * HD).astype(jnp.bfloat16)
    branch = lax.psum(times_trans(attended, out_w), "tensor")
    middle = token_rows + branch
    plain_two, inverse_two = rms_parts(middle)
    normed_two = (plain_two * gain_two).astype(jnp.bfloat16)
    gate_pre = jnp.dot(normed_two, gate_w, preferred_element_type=jnp.float32)
    up_pre = jnp.dot(normed_two, up_w, preferred_element_type=jnp.float32)
    hidden = (jax.nn.silu(gate_pre) * up_pre).astype(jnp.bfloat16)
    result = middle + lax.psum(times_trans(hidden, down_w).astype(jnp.bfloat16), "tensor").astype(
        jnp.float32
    )
    kept_values = (
        plain_one,
        inverse_one,
        normed,
        plain_q,
        inverse_q,
        query_in,
        query,
        keys_all,
        values_all,
        log_totals,
        attended,
        plain_two,
        inverse_two,
        normed_two,
        gate_pre,
        up_pre,
        hidden,
    )
    return (result, kept_values)


def backward(cotangent, attention_w, ffn_w, gains, own_pos, allowed, kept_values):
    gain_one, gain_q, gain_two = gains
    down_q, up_q, key_w, value_w, out_w = attention_w
    gate_w, up_w, down_w = ffn_w
    (
        plain_one,
        inverse_one,
        normed,
        plain_q,
        inverse_q,
        query_in,
        query,
        keys_all,
        values_all,
        log_totals,
        attended,
        plain_two,
        inverse_two,
        normed_two,
        gate_pre,
        up_pre,
        hidden,
    ) = kept_values
    row_count = cotangent.shape[0]
    heads = query.shape[0]
    scale = HD ** (-0.5)
    grad_down = trans_times(cotangent, hidden)
    grad_hidden = jnp.dot(cotangent, down_w, preferred_element_type=jnp.float32)
    sigma = jax.nn.sigmoid(gate_pre)
    grad_gate = (grad_hidden * up_pre * sigma * (1.0 + gate_pre * (1.0 - sigma))).astype(
        jnp.bfloat16
    )
    grad_up = (grad_hidden * gate_pre * sigma).astype(jnp.bfloat16)
    grad_gate_w = trans_times(normed_two, grad_gate)
    grad_up_w = trans_times(normed_two, grad_up)
    grad_norm_two = lax.psum(times_trans(grad_gate, gate_w) + times_trans(grad_up, up_w), "tensor")
    grad_mid_part, grad_gain_two = rms_back(grad_norm_two, plain_two, inverse_two, gain_two)
    ffn_grads = (
        lax.psum_scatter(grad_gate_w, ("dp", "ctx"), scatter_dimension=0, tiled=True),
        lax.psum_scatter(grad_up_w, ("dp", "ctx"), scatter_dimension=0, tiled=True),
        lax.psum_scatter(grad_down, ("dp", "ctx"), scatter_dimension=0, tiled=True),
        lax.psum_scatter(grad_gain_two, ("dp", "ctx"), scatter_dimension=0, tiled=True),
    )
    grad_middle = cotangent.astype(jnp.float32) + grad_mid_part
    grad_branch = grad_middle.astype(jnp.bfloat16)
    grad_out_w = trans_times(grad_branch, attended)
    grad_attended = jnp.dot(grad_branch, out_w, preferred_element_type=jnp.float32).astype(
        jnp.bfloat16
    )
    grad_heads = grad_attended.reshape(row_count, heads, HD).transpose(1, 0, 2)

    def head_back(carry, item):
        key_acc, value_acc = carry
        q_head, grad_head, lse_head = item
        scores = jnp.where(allowed, times_trans(q_head, keys_all) * scale, -1e30)
        soft = jnp.exp(scores - lse_head[:, None])
        grad_soft = times_trans(grad_head, values_all)
        inner = jnp.sum(soft * grad_soft, axis=-1, keepdims=True)
        grad_scores = (soft * (grad_soft - inner)).astype(jnp.bfloat16)
        grad_q = jnp.dot(grad_scores, keys_all, preferred_element_type=jnp.float32) * scale
        key_acc = key_acc + trans_times(grad_scores, q_head) * scale
        value_acc = value_acc + trans_times(soft.astype(jnp.bfloat16), grad_head)
        return ((key_acc, value_acc), grad_q)

    empty = jnp.zeros(keys_all.shape, jnp.float32)
    (key_total, value_total), grad_query = lax.scan(
        head_back, (empty, empty), (query, grad_heads, log_totals)
    )
    key_own, value_own = (
        lax.psum_scatter(key_total, "ctx", scatter_dimension=0, tiled=True),
        lax.psum_scatter(value_total, "ctx", scatter_dimension=0, tiled=True),
    )
    grad_query_pre = (
        rotate(grad_query, -own_pos)
        .transpose(1, 0, 2)
        .reshape(row_count, heads * HD)
        .astype(jnp.bfloat16)
    )
    grad_up_q = trans_times(query_in, grad_query_pre)
    grad_qin_part = times_trans(grad_query_pre, up_q)
    grad_qin, grad_keys_rot, grad_values = lax.psum((grad_qin_part, key_own, value_own), "tensor")
    grad_key_pre = rotate(grad_keys_rot, -own_pos).astype(jnp.bfloat16)
    grad_value_low = grad_values.astype(jnp.bfloat16)
    grad_latent, grad_gain_q = rms_back(grad_qin, plain_q, inverse_q, gain_q)
    grad_latent_low = grad_latent.astype(jnp.bfloat16)
    grad_down_q = trans_times(normed, grad_latent_low)
    grad_key_w = trans_times(normed, grad_key_pre)
    grad_value_w = trans_times(normed, grad_value_low)
    grad_norm_one = (
        times_trans(grad_latent_low, down_q)
        + times_trans(grad_key_pre, key_w)
        + times_trans(grad_value_low, value_w)
    )
    grad_in_part, grad_gain_one = rms_back(grad_norm_one, plain_one, inverse_one, gain_one)
    grad_tokens = grad_middle + grad_in_part
    attention_grads = (
        lax.psum_scatter(grad_gain_one, ("dp", "ctx"), scatter_dimension=0, tiled=True),
        lax.psum_scatter(grad_down_q, ("dp", "ctx"), scatter_dimension=0, tiled=True),
        lax.psum_scatter(grad_gain_q, ("dp", "ctx"), scatter_dimension=0, tiled=True),
        lax.psum_scatter(grad_up_q, ("dp", "ctx"), scatter_dimension=0, tiled=True),
        lax.psum_scatter(grad_key_w, ("dp", "ctx"), scatter_dimension=0, tiled=True),
        lax.psum_scatter(grad_value_w, ("dp", "ctx"), scatter_dimension=0, tiled=True),
        lax.psum_scatter(grad_out_w, ("dp", "ctx"), scatter_dimension=0, tiled=True),
    )
    return (grad_tokens, attention_grads, ffn_grads)


def per_device(
    tokens_in,
    cotangent,
    seq_lengths,
    block_order,
    gain_one,
    down_q,
    gain_q,
    up_q,
    key_w,
    value_w,
    out_w,
    gain_two,
    gate_w,
    up_w,
    down_w,
):
    token_rows = tokens_in.astype(jnp.float32)
    row_count = tokens_in.shape[0]
    block_rows = row_count // 2
    places = (
        block_order[0][:, :, None] * block_rows
        + jnp.arange(block_rows, dtype=jnp.int32)[None, None, :]
    ).reshape(-1)
    second = (places >= seq_lengths[0, 0]).astype(jnp.int32)
    in_sequence = places - second * seq_lengths[0, 0]
    start = lax.axis_index("ctx") * row_count
    own_places = lax.dynamic_slice_in_dim(places, start, row_count)
    own_second = lax.dynamic_slice_in_dim(second, start, row_count)
    own_pos = lax.dynamic_slice_in_dim(in_sequence, start, row_count).astype(jnp.float32)
    allowed = (own_second[:, None] == second[None, :]) & (places[None, :] <= own_places[:, None])
    gains = (gain_one, gain_q, gain_two)
    attention_w = (
        lax.all_gather(down_q, ("dp", "ctx"), axis=0, tiled=True),
        lax.all_gather(up_q, ("dp", "ctx"), axis=0, tiled=True),
        lax.all_gather(key_w, ("dp", "ctx"), axis=0, tiled=True),
        lax.all_gather(value_w, ("dp", "ctx"), axis=0, tiled=True),
        lax.all_gather(out_w, ("dp", "ctx"), axis=0, tiled=True),
    )
    ffn_w = (
        lax.all_gather(gate_w, ("dp", "ctx"), axis=0, tiled=True),
        lax.all_gather(up_w, ("dp", "ctx"), axis=0, tiled=True),
        lax.all_gather(down_w, ("dp", "ctx"), axis=0, tiled=True),
    )
    result, kept_values = forward(token_rows, attention_w, ffn_w, gains, own_pos, allowed)
    attention_w = (
        lax.all_gather(down_q, ("dp", "ctx"), axis=0, tiled=True),
        lax.all_gather(up_q, ("dp", "ctx"), axis=0, tiled=True),
        lax.all_gather(key_w, ("dp", "ctx"), axis=0, tiled=True),
        lax.all_gather(value_w, ("dp", "ctx"), axis=0, tiled=True),
        lax.all_gather(out_w, ("dp", "ctx"), axis=0, tiled=True),
    )
    ffn_w = (
        lax.all_gather(gate_w, ("dp", "ctx"), axis=0, tiled=True),
        lax.all_gather(up_w, ("dp", "ctx"), axis=0, tiled=True),
        lax.all_gather(down_w, ("dp", "ctx"), axis=0, tiled=True),
    )
    unused, kept_values = forward(token_rows, attention_w, ffn_w, gains, own_pos, allowed)
    grad_tokens, attention_grads, ffn_grads = backward(
        cotangent, attention_w, ffn_w, gains, own_pos, allowed, kept_values
    )
    grad_gain_one, grad_down_q, grad_gain_q, grad_up_q, grad_key_w, grad_value_w, grad_out_w = (
        attention_grads
    )
    grad_gate_w, grad_up_w, grad_down_w, grad_gain_two = ffn_grads
    return (
        result.astype(jnp.bfloat16),
        grad_tokens,
        grad_gain_one,
        grad_down_q,
        grad_gain_q,
        grad_up_q,
        grad_key_w,
        grad_value_w,
        grad_out_w,
        grad_gain_two,
        grad_gate_w,
        grad_up_w,
        grad_down_w,
    )


def solution(mesh):
    fast = dict(mesh.shape) == {"dp": 4, "ctx": 2, "tensor": 4}
    return jax.shard_map(
        fast_device if fast else per_device,
        mesh=mesh,
        in_specs=(
            P(("dp", "ctx"), None),
            P(("dp", "ctx"), None),
            P("dp", None),
            P("dp", None, None),
            P(),
            P(("dp", "ctx"), None),
            P(),
            P(("dp", "ctx"), "tensor"),
            P(("dp", "ctx"), None),
            P(("dp", "ctx"), None),
            P(("dp", "ctx"), "tensor"),
            P(),
            P(("dp", "ctx"), "tensor"),
            P(("dp", "ctx"), "tensor"),
            P(("dp", "ctx"), "tensor"),
        ),
        out_specs=(
            P(("dp", "ctx"), None),
            P(("dp", "ctx"), None),
            P(("dp", "ctx")),
            P(("dp", "ctx"), None),
            P(("dp", "ctx")),
            P(("dp", "ctx"), "tensor"),
            P(("dp", "ctx"), None),
            P(("dp", "ctx"), None),
            P(("dp", "ctx"), "tensor"),
            P(("dp", "ctx")),
            P(("dp", "ctx"), "tensor"),
            P(("dp", "ctx"), "tensor"),
            P(("dp", "ctx"), "tensor"),
        ),
        check_vma=False,
    )
```

```python
import jax
import jax.numpy as jnp
from jax import lax
from jax.experimental import pallas as pl
from jax.experimental.pallas import tpu as pltpu
from jax.sharding import PartitionSpec as P

HD = 256


EPSILON = 1e-06

AXES = ("dp", "ctx", "tensor")
BF = jnp.bfloat16
F32 = jnp.float32


def dot(left, right):
    return jnp.dot(left, right, preferred_element_type=F32)


def times_trans(left, right):
    return lax.dot_general(left, right, (((1,), (1,)), ((), ())), preferred_element_type=F32)


def trans_times(left, right):
    return lax.dot_general(left, right, (((0,), (0,)), ((), ())), preferred_element_type=F32)


def rms_parts(array):
    inverse = lax.rsqrt(jnp.mean(array * array, axis=-1, keepdims=True) + EPSILON)
    return (array * inverse, inverse)


def rms_back(grad_out, plain, inverse, gain):
    grad_plain = grad_out * gain
    grad_in = inverse * (grad_plain - plain * jnp.mean(grad_plain * plain, axis=-1, keepdims=True))
    return (grad_in, jnp.sum(grad_out * plain, axis=0))


def angles_of(places, half):
    freqs = 10000.0 ** (-jnp.arange(half, dtype=F32) / half)
    angles = places[:, None] * freqs[None, :]
    return (jnp.cos(angles), jnp.sin(angles))


def turn(array, cosine, sine):
    half = array.shape[-1] // 2
    first = array[..., :half]
    latter = array[..., half:]
    return jnp.concatenate(
        [first * cosine - latter * sine, latter * cosine + first * sine], axis=-1
    )


def routes(move):
    pairs = []
    for z in range(4):
        for x in range(2):
            for y in range(2):
                for c in range(2):
                    to = move(z, x, y, c)
                    if to is not None:
                        tz, tx, ty, tc = to
                        pairs.append(
                            (((z * 2 + x) * 2 + y) * 2 + c, ((tz * 2 + tx) * 2 + ty) * 2 + tc)
                        )
    return pairs


OVER_X = routes(lambda z, x, y, c: (z, 1 - x, y, c))
OVER_Y = routes(lambda z, x, y, c: (z, x, 1 - y, c))
OVER_XY = routes(lambda z, x, y, c: (z, 1 - x, 1 - y, c))
OVER_YC = routes(lambda z, x, y, c: (z, x, 1 - y, 1 - c))
OVER_C = routes(lambda z, x, y, c: (z, x, y, 1 - c))
TRANSPOSE = routes(lambda z, x, y, c: (z, c, y, x) if x != c else None)
Z_ONE = routes(lambda z, x, y, c: (z ^ 1, x, y, c))
Z_TWO = routes(lambda z, x, y, c: (z ^ 2, x, y, c))
Z_THREE = routes(lambda z, x, y, c: (z ^ 3, x, y, c))


def send(array, pairs):
    return lax.ppermute(array, AXES, pairs)


def transpose(array, stays):
    return jnp.where(stays, array, send(array, TRANSPOSE))


def after(array, *others):
    return lax.optimization_barrier((array, *others))[0]


def stage(*arrays):
    return lax.optimization_barrier(arrays)


def gather_z(array):
    return lax.all_gather(array, "dp", axis=0, tiled=True)


def reduce_z(slabs):
    return lax.psum_scatter(slabs, "dp", scatter_dimension=0, tiled=True)


def trade_z(slabs):
    n = slabs.shape[0] // 4
    return [slabs[:n]] + [
        send(slabs[k * n : (k + 1) * n], pairs)
        for k, pairs in ((1, Z_ONE), (2, Z_TWO), (3, Z_THREE))
    ]


WHOLE = pl.BlockSpec(memory_space=pltpu.VMEM)
HELD = pl.BlockSpec(memory_space=pl.ANY)
ROOMY = pltpu.CompilerParams(vmem_limit_bytes=56 * 1024 * 1024)


def cost(macs, moved, share=1):
    return pl.CostEstimate(
        flops=2 * macs // share // 1, bytes_accessed=moved // share // 1, transcendentals=0
    )


def place_copies(plan, numbers, buffers, shape, dtype):
    def body(numbers_ref, *refs):
        ins, out_ref, sem = refs[:-2], refs[-2], refs[-1]
        listed = plan(numbers_ref, ins, out_ref)
        for i, (condition, source, target) in enumerate(listed):
            copy = pltpu.make_async_copy(source, target, sem.at[i])
            if condition is None:
                copy.start()
            else:
                pl.when(condition)(copy.start)
        for i, (condition, source, target) in enumerate(listed):
            copy = pltpu.make_async_copy(source, target, sem.at[i])
            if condition is None:
                copy.wait()
            else:
                pl.when(condition)(copy.wait)

    moved = 2
    for extent in shape:
        moved *= extent
    return pl.pallas_call(
        body,
        grid_spec=pltpu.PrefetchScalarGridSpec(
            num_scalar_prefetch=1,
            grid=(1,),
            in_specs=[HELD] * len(buffers),
            out_specs=pl.BlockSpec(shape, lambda i, numbers_ref: (0, 0)),
            scratch_shapes=[pltpu.SemaphoreType.DMA((40,))],
        ),
        out_shape=jax.ShapeDtypeStruct(shape, dtype),
        compiler_params=ROOMY,
        cost_estimate=cost(0, 2 * moved),
    )(numbers, *buffers)


def attention_forward(query_pre, cosine, sine, keys, values, row_info, key_places):
    rows, width = query_pre.shape
    heads = width // HD
    chunk = 256
    half = HD // 2
    scale = HD ** (-0.5)

    def body(pre_ref, cos_ref, sin_ref, k_ref, v_ref, info_ref, place_ref, q_ref, o_ref, lse_ref):
        for i in range(rows // chunk):
            at = slice(i * chunk, (i + 1) * chunk)
            first, latter = pre_ref[at, :half], pre_ref[at, half:]
            co, si = cos_ref[at], sin_ref[at]
            q = jnp.concatenate([first * co - latter * si, latter * co + first * si], 1).astype(BF)
            q_ref[at] = q
            scores = times_trans(q, k_ref[...]) * scale
            allowed = (place_ref[...] <= info_ref[at, 0:1]) & (place_ref[...] >= info_ref[at, 1:2])
            scores = jnp.where(allowed, scores, -1e30)
            largest = jnp.max(scores, axis=-1, keepdims=True)
            exponent = jnp.exp(scores - largest)
            totals = jnp.sum(exponent, axis=-1, keepdims=True)
            soft = (exponent * (1.0 / totals)).astype(BF)
            o_ref[at] = dot(soft, v_ref[...]).astype(BF)
            lse_ref[0, at] = largest + jnp.log(totals)

    full = lambda h: (0, 0)
    by_head = lambda h: (0, h)
    return pl.pallas_call(
        body,
        grid=(heads,),
        in_specs=[
            pl.BlockSpec((rows, HD), by_head),
            pl.BlockSpec((rows, half), full),
            pl.BlockSpec((rows, half), full),
            pl.BlockSpec((rows, HD), full),
            pl.BlockSpec((rows, HD), full),
            pl.BlockSpec((rows, 2), full),
            pl.BlockSpec((1, rows), full),
        ],
        out_specs=[
            pl.BlockSpec((rows, HD), by_head),
            pl.BlockSpec((rows, HD), by_head),
            pl.BlockSpec((1, rows, 1), lambda h: (h, 0, 0)),
        ],
        out_shape=[
            jax.ShapeDtypeStruct((rows, width), BF),
            jax.ShapeDtypeStruct((rows, width), BF),
            jax.ShapeDtypeStruct((heads, rows, 1), F32),
        ],
        compiler_params=ROOMY,
        cost_estimate=cost(4 * rows * rows * width, 6 * rows * width),
    )(query_pre, cosine, sine, keys, values, row_info, key_places)


def attention_backward(query, grad_out, lse, cosine, sine, keys, values, row_info, key_places):
    rows, width = query.shape
    heads = width // HD
    chunk = 256
    half = HD // 2
    scale = HD ** (-0.5)

    def body(
        q_ref, do_ref, lse_ref, cos_ref, sin_ref, k_ref, v_ref, info_ref, place_ref, dq_ref, dk_ref, dv_ref
    ):
        @pl.when(pl.program_id(0) == 0)
        def clear():
            dk_ref[...] = jnp.zeros_like(dk_ref)
            dv_ref[...] = jnp.zeros_like(dv_ref)

        for i in range(rows // chunk):
            at = slice(i * chunk, (i + 1) * chunk)
            q, do = q_ref[at], do_ref[at]
            scores = times_trans(q, k_ref[...]) * scale
            allowed = (place_ref[...] <= info_ref[at, 0:1]) & (place_ref[...] >= info_ref[at, 1:2])
            soft = jnp.exp(jnp.where(allowed, scores, -1e30) - lse_ref[0, at])
            grad_soft = times_trans(do, v_ref[...])
            summed = jnp.sum(soft * grad_soft, axis=-1, keepdims=True)
            grad_scores = (soft * (grad_soft - summed)).astype(BF)
            dq = dot(grad_scores, k_ref[...]) * scale
            first, latter = dq[:, :half], dq[:, half:]
            co, si = cos_ref[at], sin_ref[at]
            dq_ref[at] = jnp.concatenate(
                [first * co + latter * si, latter * co - first * si], 1
            ).astype(BF)
            dk_ref[...] += trans_times(grad_scores, q) * scale
            dv_ref[...] += trans_times(soft.astype(BF), do)

    full = lambda h: (0, 0)
    by_head = lambda h: (0, h)
    return pl.pallas_call(
        body,
        grid=(heads,),
        in_specs=[
            pl.BlockSpec((rows, HD), by_head),
            pl.BlockSpec((rows, HD), by_head),
            pl.BlockSpec((1, rows, 1), lambda h: (h, 0, 0)),
            pl.BlockSpec((rows, half), full),
            pl.BlockSpec((rows, half), full),
            pl.BlockSpec((rows, HD), full),
            pl.BlockSpec((rows, HD), full),
            pl.BlockSpec((rows, 2), full),
            pl.BlockSpec((1, rows), full),
        ],
        out_specs=[
            pl.BlockSpec((rows, HD), by_head),
            pl.BlockSpec((rows, HD), full),
            pl.BlockSpec((rows, HD), full),
        ],
        out_shape=[
            jax.ShapeDtypeStruct((rows, width), BF),
            jax.ShapeDtypeStruct((rows, HD), F32),
            jax.ShapeDtypeStruct((rows, HD), F32),
        ],
        compiler_params=ROOMY,
        cost_estimate=cost(8 * rows * rows * width, 6 * rows * width),
    )(query, grad_out, lse, cosine, sine, keys, values, row_info, key_places)


def product_of_parts(parts, weight):
    rows = parts[0].shape[0]
    count = len(parts)
    width = weight.shape[1]

    def body(*refs):
        weight_ref, out_ref = refs[count:]
        for i in range(0, count, 4):
            left = jnp.concatenate([refs[j][...] for j in range(i, i + 4)], axis=0)
            out_ref[i * rows : (i + 4) * rows] = dot(left, weight_ref[...]).astype(BF)

    return pl.pallas_call(
        body,
        in_specs=[WHOLE] * (count + 1),
        out_specs=WHOLE,
        out_shape=jax.ShapeDtypeStruct((count * rows, width), BF),
        compiler_params=ROOMY,
        cost_estimate=cost(count * rows * weight.size, 2 * weight.size),
    )(*parts, weight)


def product_pieces(left, weight, extras, got, first_half):
    rows = left.shape[0] // 2
    part = rows // 4
    start = 0 if first_half else rows
    wide = weight.shape[0]
    total = wide + sum(e.shape[1] for e in extras)
    outs = 4 if first_half else 1

    def body(left_ref, weight_ref, *refs):
        extra_refs = refs[: len(extras)]
        got_ref = refs[len(extras)] if got is not None else None
        out_refs = refs[len(refs) - outs :]
        src = slice(start, start + rows)

        def put(value, cols):
            if got_ref is not None:
                value = value + got_ref[:, cols].astype(F32)
            value = value.astype(BF)
            if outs == 1:
                out_refs[0][:, cols] = value
            else:
                for f in range(4):
                    out_refs[f][:, cols] = value[f * part : (f + 1) * part]

        step = 512
        for col in range(0, wide, step):
            put(times_trans(left_ref[src], weight_ref[col : col + step]), slice(col, col + step))
        col = wide
        for extra_ref in extra_refs:
            n = extra_ref.shape[1]
            put(extra_ref[src], slice(col, col + n))
            col += n

    shapes = [jax.ShapeDtypeStruct((part, total), BF)] * 4
    if outs == 1:
        shapes = [jax.ShapeDtypeStruct((rows, total), BF)]
    arrays = [left, weight, *extras] + ([got] if got is not None else [])
    return pl.pallas_call(
        body,
        in_specs=[WHOLE] * len(arrays),
        out_specs=[WHOLE] * outs,
        out_shape=shapes,
        compiler_params=ROOMY,
        cost_estimate=cost(rows * wide * left.shape[1], 2 * weight.size + 4 * rows * total),
    )(*arrays)


def tiles_of(width):
    whole = width // 256
    return whole, width - whole * 256


def ffn_forward(numbers, parts, pairs):
    part, depth = parts[0].shape
    rows = part * len(parts)
    width = pairs[0].shape[1]
    whole, rest = tiles_of(width)

    def body(numbers_ref, *refs):
        part_refs, pair_refs = refs[:4], refs[4:6]
        hid_ref, slope_ref, silu_ref, gate_vm, up_vm, in_vm, sem = refs[6:]
        gate_copies, up_copies = [], []
        for i in range(8):
            to = pl.ds(pl.multiple_of(numbers_ref[i] * 256, 256), 256)
            ref, at = pair_refs[i // 4], (i % 4) * 512
            gate_copies.append(
                pltpu.make_async_copy(ref.at[at : at + 256], gate_vm.at[to], sem.at[i])
            )
            up_copies.append(
                pltpu.make_async_copy(ref.at[at + 256 : at + 512], up_vm.at[to], sem.at[8 + i])
            )
        for copy in gate_copies + up_copies:
            copy.start()
        for f in range(4):
            in_vm[f * part : (f + 1) * part] = part_refs[f][...]
        for copy in gate_copies + up_copies:
            copy.wait()

        def tile(cols):
            gate = dot(in_vm[...], gate_vm[:, cols])
            up = dot(in_vm[...], up_vm[:, cols])
            sigma = jax.nn.sigmoid(gate)
            silu = gate * sigma
            hid_ref[:, cols] = (silu * up).astype(BF)
            slope_ref[:, cols] = up * sigma * (1.0 + gate * (1.0 - sigma))
            silu_ref[:, cols] = silu

        @pl.loop(0, whole)
        def each(i):
            tile(pl.ds(pl.multiple_of(i * 256, 256), 256))

        if rest:
            tile(slice(whole * 256, width))

    return pl.pallas_call(
        body,
        grid_spec=pltpu.PrefetchScalarGridSpec(
            num_scalar_prefetch=1,
            grid=(1,),
            in_specs=[pl.BlockSpec((part, depth), lambda i, n: (0, 0))] * 4 + [HELD] * 2,
            out_specs=[pl.BlockSpec((rows, width), lambda i, n: (0, 0))] * 3,
            scratch_shapes=[
                pltpu.VMEM((depth, width), BF),
                pltpu.VMEM((depth, width), BF),
                pltpu.VMEM((rows, depth), BF),
                pltpu.SemaphoreType.DMA((16,)),
            ],
        ),
        out_shape=[
            jax.ShapeDtypeStruct((rows, width), BF),
            jax.ShapeDtypeStruct((rows, width), F32),
            jax.ShapeDtypeStruct((rows, width), F32),
        ],
        compiler_params=ROOMY,
        cost_estimate=cost(2 * rows * depth * width, 4 * depth * width),
    )(numbers, *parts, *pairs)


def ffn_backward(numbers, cot, slope, silu, pairs, downs):
    rows = slope.shape[0]
    depth = cot.shape[1]
    part = rows // 4
    width = slope.shape[1]
    whole, rest = tiles_of(width)

    def body(numbers_ref, *refs):
        cot_ref, slope_ref, silu_ref = refs[:3]
        pair_refs, down_refs = refs[3:5], refs[5:7]
        gate_out, up_out = refs[7:9]
        piece_refs = refs[9:13]
        down_vm, pair_vm, sem = refs[13:]
        copies, later = [], []
        for i in range(8):
            to = pl.ds(pl.multiple_of(numbers_ref[i] * 256, 256), 256)
            ref, at = down_refs[i // 4], (i % 4) * 256
            copies.append(
                pltpu.make_async_copy(ref.at[at : at + 256], down_vm.at[to], sem.at[i])
            )
            ref, at = pair_refs[i // 4], (i % 4) * 512
            later.append(
                pltpu.make_async_copy(ref.at[at : at + 512], pair_vm.at[i], sem.at[8 + i])
            )
        for copy in copies + later:
            copy.start()
        for copy in copies:
            copy.wait()

        def tile(cols):
            grad = dot(cot_ref[...], down_vm[:, cols])
            gate_out[:, cols] = (grad * slope_ref[:, cols]).astype(BF)
            up_out[:, cols] = (grad * silu_ref[:, cols]).astype(BF)

        @pl.loop(0, whole)
        def each(i):
            tile(pl.ds(pl.multiple_of(i * 256, 256), 256))

        if rest:
            tile(slice(whole * 256, width))
        for copy in later:
            copy.wait()

        @pl.loop(0, 8)
        def block(i):
            cols = pl.ds(pl.multiple_of(numbers_ref[i] * 256, 256), 256)
            value = times_trans(gate_out[...], pair_vm[i, :256]) + times_trans(
                up_out[...], pair_vm[i, 256:]
            )
            value = value.astype(BF)
            for f in range(4):
                piece_refs[f][:, cols] = value[f * part : (f + 1) * part]

    flat = lambda i, n: (0, 0)
    return pl.pallas_call(
        body,
        grid_spec=pltpu.PrefetchScalarGridSpec(
            num_scalar_prefetch=1,
            grid=(1,),
            in_specs=[
                pl.BlockSpec((rows, depth), flat),
                pl.BlockSpec((rows, width), flat),
                pl.BlockSpec((rows, width), flat),
            ]
            + [HELD] * 4,
            out_specs=[pl.BlockSpec((rows, width), flat)] * 2
            + [pl.BlockSpec((part, depth), flat)] * 4,
            scratch_shapes=[
                pltpu.VMEM((depth, width), BF),
                pltpu.VMEM((8, 512, width), BF),
                pltpu.SemaphoreType.DMA((16,)),
            ],
        ),
        out_shape=[jax.ShapeDtypeStruct((rows, width), BF)] * 2
        + [jax.ShapeDtypeStruct((part, depth), BF)] * 4,
        compiler_params=ROOMY,
        cost_estimate=cost(3 * rows * depth * width, 6 * depth * width),
    )(numbers, cot, slope, silu, *pairs, *downs)


def ffn_output(numbers, hidden, downs):
    rows, width = hidden.shape
    part = rows // 4
    depth = 2 * downs[0].shape[0]

    def body(numbers_ref, hid_ref, *refs):
        down_refs, piece_refs = refs[:2], refs[2:6]
        down_vm, sem = refs[6:]
        copies = [
            pltpu.make_async_copy(
                down_refs[i // 4].at[(i % 4) * 256 : (i % 4 + 1) * 256], down_vm.at[i], sem.at[i]
            )
            for i in range(8)
        ]
        for copy in copies:
            copy.start()
        for copy in copies:
            copy.wait()

        @pl.loop(0, 8)
        def block(i):
            cols = pl.ds(pl.multiple_of(numbers_ref[i] * 256, 256), 256)
            value = times_trans(hid_ref[...], down_vm[i]).astype(BF)
            for f in range(4):
                piece_refs[f][:, cols] = value[f * part : (f + 1) * part]

    flat = lambda i, n: (0, 0)
    return pl.pallas_call(
        body,
        grid_spec=pltpu.PrefetchScalarGridSpec(
            num_scalar_prefetch=1,
            grid=(1,),
            in_specs=[pl.BlockSpec((rows, width), flat)] + [HELD] * 2,
            out_specs=[pl.BlockSpec((part, depth), flat)] * 4,
            scratch_shapes=[
                pltpu.VMEM((8, 256, width), BF),
                pltpu.SemaphoreType.DMA((8,)),
            ],
        ),
        out_shape=[jax.ShapeDtypeStruct((part, depth), BF)] * 4,
        compiler_params=ROOMY,
        cost_estimate=cost(rows * depth * width, 2 * depth * width, 4),
    )(numbers, hidden, *downs)


def weight_grads(numbers, terms, width):
    lefts, rights, left_specs, right_specs = [], [], [], []
    shape_of = []
    for left, block, offset, products in terms:
        for array in left:
            lefts.append(array)
            left_specs.append(
                pl.BlockSpec((array.shape[0], block), lambda i, n, offset=offset: (0, n[offset + i]))
            )
        for place, right in products:
            for array, start, count, pick in right:
                rights.append(array)
                if pick is None:
                    right_specs.append(pl.BlockSpec(array.shape, lambda i, n: (0, 0)))
                else:
                    right_specs.append(
                        pl.BlockSpec((array.shape[0], width), lambda i, n, pick=pick: (0, n[pick]))
                    )
        shape_of.append(block)
    height = sum(shape_of)

    def body(numbers_ref, *refs):
        left_refs = refs[: len(lefts)]
        right_refs = refs[len(lefts) : len(lefts) + len(rights)]
        out_ref = refs[-1]
        li, ri, row = 0, 0, 0
        for left, block, offset, products in terms:
            pieces = [left_refs[li + j][...] for j in range(len(left))]
            li += len(left)
            whole = pieces[0] if len(pieces) == 1 else jnp.concatenate(pieces, axis=0)
            for place, right in products:
                value = None
                at = 0
                for array, start, count, pick in right:
                    this = trans_times(
                        whole[at : at + count], right_refs[ri][start : start + count]
                    )
                    value = this if value is None else value + this
                    at += count
                    ri += 1
                value = value.astype(BF)
                n = value.shape[1]
                if place is None:
                    cols = slice(0, n)
                else:
                    cols = pl.ds(pl.multiple_of(numbers_ref[place] * n, n), n)
                out_ref[row : row + block, cols] = value

            row += block

    macs = 4 * height * width * 1024
    return pl.pallas_call(
        body,
        grid_spec=pltpu.PrefetchScalarGridSpec(
            num_scalar_prefetch=1,
            grid=(4,),
            in_specs=left_specs + right_specs,
            out_specs=pl.BlockSpec((height, width), lambda i, n: (i, 0)),
        ),
        out_shape=jax.ShapeDtypeStruct((4 * height, width), BF),
        compiler_params=ROOMY,
        cost_estimate=cost(macs, 4 * height * width * 4, 4),
    )(numbers, *lefts, *rights)


def input_gradient(numbers, grad_lat, first_all, grad_mid, tokens, gain):
    depth = tokens.shape[1]
    wide = grad_lat.shape[1]
    part = 128

    def body(numbers_ref, lat_ref, first_ref, mid_ref, tok_ref, gain_ref, out_ref, grad_vm):
        for col in range(0, depth, 512):
            cols = slice(col, col + 512)
            grad_vm[:, cols] = times_trans(lat_ref[...], first_ref[cols]) * gain_ref[:, cols]
        for i in range(4):
            at = slice(i * part, (i + 1) * part)
            plain = tok_ref[at].astype(F32)
            inverse = lax.rsqrt(jnp.mean(plain * plain, axis=-1, keepdims=True) + EPSILON)
            plain = plain * inverse
            grad = grad_vm[at]
            mean = jnp.mean(grad * plain, axis=-1, keepdims=True)
            to = pl.ds(pl.multiple_of(numbers_ref[9 + i] * part, part), part)
            out_ref[to] = mid_ref[at].astype(F32) + inverse * (grad - plain * mean)

    picked = lambda i, n: (n[8], 0)
    flat = lambda i, n: (0, 0)
    return pl.pallas_call(
        body,
        grid_spec=pltpu.PrefetchScalarGridSpec(
            num_scalar_prefetch=1,
            grid=(1,),
            in_specs=[
                pl.BlockSpec((4 * part, wide), picked),
                pl.BlockSpec((depth, wide), flat),
                pl.BlockSpec((4 * part, depth), picked),
                pl.BlockSpec((4 * part, depth), picked),
                pl.BlockSpec((1, depth), flat),
            ],
            out_specs=pl.BlockSpec((4 * part, depth), flat),
            scratch_shapes=[pltpu.VMEM((4 * part, depth), F32)],
        ),
        out_shape=jax.ShapeDtypeStruct((4 * part, depth), F32),
        compiler_params=ROOMY,
        cost_estimate=cost(4 * part * depth * wide, 2 * depth * wide + 8 * part * depth * 4),
    )(numbers, grad_lat, first_all, grad_mid, tokens, gain.reshape(1, -1))


def first_finish(numbers, quarters, first_w, gain, latent_width):
    rows, lane = quarters[0].shape
    wide = first_w.shape[1]

    def body(numbers_ref, *refs):
        weight_ref, gain_ref, down_ref, key_ref, value_ref, one_ref, all_vm = refs[4:]
        for i in range(4):
            cols = pl.ds(pl.multiple_of(numbers_ref[25 + i] * lane, lane), lane)
            all_vm[:, cols] = refs[i][...].astype(F32)
        down_ref[...] = all_vm[:, :latent_width]
        key_ref[...] = all_vm[:, latent_width : latent_width + HD]
        value_ref[...] = all_vm[:, latent_width + HD :]
        total = jnp.sum(weight_ref[...].astype(F32) * all_vm[...], axis=1, keepdims=True)
        one_ref[...] = total / gain_ref[...]

    flat = lambda i, n: (0, 0)
    extents = [(rows, latent_width), (rows, HD), (rows, wide - latent_width - HD), (rows, 1)]
    *grads, one = pl.pallas_call(
        body,
        grid_spec=pltpu.PrefetchScalarGridSpec(
            num_scalar_prefetch=1,
            grid=(1,),
            in_specs=[pl.BlockSpec((rows, lane), flat)] * 4
            + [pl.BlockSpec((rows, wide), flat), pl.BlockSpec((rows, 1), flat)],
            out_specs=[pl.BlockSpec(e, flat) for e in extents],
            scratch_shapes=[pltpu.VMEM((rows, wide), F32)],
        ),
        out_shape=[jax.ShapeDtypeStruct(e, F32) for e in extents],
        compiler_params=ROOMY,
        cost_estimate=cost(0, 10 * rows * wide),
    )(numbers, *quarters, first_w, gain.reshape(-1, 1))
    return (*grads, one.reshape(-1))


def trade(pieces):
    own, y_piece, x_piece, xy_piece = pieces
    return [own, send(y_piece, OVER_Y), send(x_piece, OVER_X), send(xy_piece, OVER_XY)]


def added(pieces):
    total = pieces[0].astype(F32)
    for piece in pieces[1:]:
        total = total + piece.astype(F32)
    return total


def sum_pieces(pieces):
    return added(trade(pieces))


def spread(part):
    return [part, send(part, OVER_Y), send(part, OVER_X), send(part, OVER_XY)]


def over_core(arrays):
    return [send(array, OVER_C) for array in arrays]


def fast_device(
    tokens_in,
    cotangent,
    seq_lengths,
    block_order,
    gain_one,
    down_q,
    gain_q,
    up_q,
    key_w,
    value_w,
    out_w,
    gain_two,
    gate_w,
    up_w,
    down_w,
):
    z = lax.axis_index("dp")
    x = lax.axis_index("ctx")
    t = lax.axis_index("tensor")
    y = t // 2
    c = t % 2
    stays = x == c
    quarter = x * 2 + y
    rows, depth = tokens_in.shape
    half = rows // 2
    part = rows // 4
    latent_width = down_q.shape[1]
    cols = up_q.shape[1] // 2
    ks = jnp.arange(4, dtype=jnp.int32)
    z_order = z ^ ks
    numbers = jnp.concatenate(
        [
            ks * 2 + c,
            ks * 2 + (1 - c),
            jnp.stack([c ^ x]),
            quarter ^ ks,
            z_order * 2 + x,
            z_order * 2 + (1 - x),
            jnp.stack([c, 1 - c, x, 1 - x, t, t ^ 1, t ^ 2, t ^ 3]),
        ]
    ).astype(jnp.int32)
    at_same, at_quarter, at_x, at_c, at_t = 8, 9, 13, 21, 25

    first_w = jnp.concatenate([down_q, key_w, value_w], axis=1)
    wide = first_w.shape[1]
    side = wide // 4
    mine = lax.dynamic_slice_in_dim(first_w, t * side, side, axis=1)
    attn_t = transpose(jnp.concatenate([up_q, out_w], axis=0), stays)
    tok_got = send(rows_at(tokens_in, t * part, part), OVER_X)
    tok_y = send(tok_got, OVER_Y)
    first_own = stage(mine, send(mine, Z_ONE), send(mine, Z_TWO), send(mine, Z_THREE))
    attn_own = gather_z(after(attn_t, *first_own))
    first_own = jnp.concatenate(first_own, axis=0)
    pair_t = transpose(after(jnp.concatenate([gate_w, up_w], axis=0), first_own), stays)
    first_blocks = [first_own] + [send(first_own, p) for p in (OVER_Y, OVER_X, OVER_XY)]

    def first_plan(n, ins, out):
        listed = []
        for i in range(8):
            col = pl.ds(pl.multiple_of(n[at_t + (0, 2, 0, 2, 1, 3, 1, 3)[i]] * side, side), side)
            for k in range(4):
                place = n[at_x + (i % 4 // 2) * 4 + k]
                row = pl.ds(pl.multiple_of(place * 256, 256), 256)
                listed.append((None, ins[i].at[k * 256 : (k + 1) * 256], out.at[row, col]))
        return listed

    pair_own = gather_z(after(pair_t, attn_own))

    def rows_plan(n, ins, out):
        listed = []
        for o in range(2):
            mine_too = (n[at_same] == o)
            for f in range(4):
                q = n[at_quarter + f]
                to = out.at[pl.ds((o * 4 + f) * part, part)]
                here = pl.ds(pl.multiple_of(q * part, part), part)
                listed.append((mine_too, ins[0].at[here], to))
                away = jnp.logical_not(mine_too)
                for j in range(4):
                    listed.append((away & (n[at_t + j] == q), ins[1 + j], to))
        return listed

    def group_rows(array, got, got_y):
        buffers = [array, got, send(got, OVER_C), got_y, send(got_y, OVER_C)]
        return place_copies(rows_plan, numbers, buffers, (2 * rows, depth), BF)

    tokens = group_rows(tokens_in, tok_got, tok_y)

    attn_rows = attn_t.shape[0]
    upq_rows = up_q.shape[0]
    out_rows = out_w.shape[0]

    def head_plan(start, count):
        def plan(n, ins, out):
            listed = []
            for i in range(8):
                row = pl.ds(pl.multiple_of(n[i] * count, count), count)
                col = pl.ds(pl.multiple_of(n[at_c] * cols, cols), cols)
                at = (i % 4) * attn_rows + start
                listed.append((None, ins[i // 4].at[at : at + count, col], out.at[row]))
            return listed

        return plan


    places = (
        block_order[0][:, :, None] * half + jnp.arange(half, dtype=jnp.int32)[None, None, :]
    ).reshape(2, 4, part)
    places = jnp.stack(
        [
            lax.dynamic_index_in_dim(
                lax.dynamic_index_in_dim(places, c ^ o, 0, False), quarter ^ f, 0, False
            )
            for o in range(2)
            for f in range(4)
        ]
    ).reshape(-1)
    second = (places >= seq_lengths[0, 0]).astype(jnp.int32)
    sequence_start = second * seq_lengths[0, 0]
    cosine, sine = angles_of((places - sequence_start).astype(F32), HD // 2)
    row_info = jnp.stack([places, sequence_start], axis=1)
    key_places = places[None, :]

    token_rows = tokens.astype(F32)
    plain_one, inverse_one = rms_parts(token_rows)
    normed = (plain_one * gain_one).astype(BF)
    *first_blocks, attn_own, normed = stage(*first_blocks, attn_own, normed)
    first_blocks = first_blocks + over_core(first_blocks)

    def first_plan(n, ins, out):
        listed = []
        for i in range(8):
            col = pl.ds(pl.multiple_of(n[at_t + (0, 2, 0, 2, 1, 3, 1, 3)[i]] * side, side), side)
            for k in range(4):
                place = n[at_x + (i % 4 // 2) * 4 + k]
                row = pl.ds(pl.multiple_of(place * 256, 256), 256)
                listed.append((None, ins[i].at[k * 256 : (k + 1) * 256], out.at[row, col]))
        return listed

    ffn_t = transpose(
        after(jnp.concatenate([gate_w, up_w, down_w], axis=0), first_own), stays
    )
    tok_y = send(tok_got, OVER_Y)
    *first_blocks, ffn_t, tok_got, tok_y = stage(*first_blocks[:4], ffn_t, tok_got, tok_y)
    ffn_own = gather_z(ffn_t)
    first_blocks = first_blocks + over_core(first_blocks)
    first_all = place_copies(first_plan, numbers, first_blocks, (depth, wide), BF)

    lat = dot(normed, first_all)
    down_t = transpose(after(down_w, lat), stays)
    cot_got = send(after(rows_at(cotangent, t * part, part), lat), OVER_X)
    cot_y = send(cot_got, OVER_Y)
    attns = [attn_own, send(attn_own, OVER_C)]
    up_q_all = place_copies(
        head_plan(0, upq_rows), numbers, attns, (latent_width, cols), BF
    )
    out_all = place_copies(
        head_plan(upq_rows, out_rows), numbers, attns, (depth, cols), BF
    )
    latent = lat[:, :latent_width]
    plain_q, inverse_q = rms_parts(latent)
    query_in = (plain_q * gain_q).astype(BF)
    keys = turn(lat[:, latent_width : latent_width + HD], cosine, sine).astype(BF)
    values = lat[:, latent_width + HD :].astype(BF)
    query_pre = dot(query_in, up_q_all)
    query, attended, lse = attention_forward(
        query_pre, cosine, sine, keys, values, row_info, key_places
    )
    down_t, cot_got, cot_y, attended = stage(down_t, cot_got, cot_y, attended)
    cot = group_rows(cotangent, cot_got, cot_y)
    (give,) = product_pieces(attended, out_all, [], None, False)
    pieces = product_pieces(attended, out_all, [], send(give, OVER_C), True)
    *pieces, cot, pair_own = stage(*trade(pieces), cot, pair_own)
    middle = tokens[:part].astype(F32) + added(pieces)
    down_own = gather_z(after(down_t, pair_own))
    pairs = [pair_own, send(pair_own, OVER_C)]

    plain_two, inverse_two = rms_parts(middle)
    two_parts = spread((plain_two * gain_two).astype(BF))
    hidden, slope, silu = ffn_forward(numbers, two_parts, pairs)

    def two(array, other):
        return [(array, 0, rows, None), (other, 0, rows, None)]

    width = down_w.shape[1]
    (hidden_other,) = over_core([hidden])
    down_slabs = weight_grads(
        numbers, [([cot], 256, 0, [(None, two(hidden, hidden_other))])], width
    )
    two_other = over_core(two_parts)
    down_slabs, hidden, down_own, *two_other = stage(
        down_slabs, hidden, down_own, *two_other
    )
    down_sum = reduce_z(down_slabs)
    downs = [down_own, send(down_own, OVER_C)]
    grad_gate, grad_up, *pieces = ffn_backward(
        numbers, after(cot, down_slabs), slope, silu, pairs, downs
    )

    gate_other, up_other = over_core([grad_gate, grad_up])
    two_all = list(two_parts) + list(two_other)
    pair_slabs = weight_grads(
        numbers,
        [
            (two_all, 256, 0, [(None, two(grad_gate, gate_other))]),
            (two_all, 256, 0, [(None, two(grad_up, up_other))]),
        ],
        width,
    )
    *pieces, pair_slabs, hidden = stage(*trade(pieces), pair_slabs, hidden)
    grad_norm_two = added(pieces)
    pair_sum = reduce_z(after(pair_slabs, down_sum))

    grad_plain = grad_norm_two * gain_two
    grad_mid = cot[:part].astype(F32) + inverse_two * (
        grad_plain - plain_two * jnp.mean(grad_plain * plain_two, axis=-1, keepdims=True)
    )
    mid_parts = spread(grad_mid.astype(BF))
    staged = stage(*mid_parts, *ffn_output(numbers, hidden, downs))
    mid_parts, out_pieces = list(staged[:4]), staged[4:]
    mid_parts = mid_parts + over_core(mid_parts)

    def stack_plan(n, ins, out):
        return [(None, ins[i], out.at[pl.ds(i * part, part)]) for i in range(8)]

    grad_attended = product_of_parts(mid_parts, out_all)
    grad_query_pre, key_acc, value_acc = attention_backward(
        query, grad_attended, lse, cosine, sine, keys, values, row_info, key_places
    )
    down_home = transpose(down_sum, stays)
    grad_branch = place_copies(stack_plan, numbers, mid_parts, (2 * rows, depth), BF)
    attended_other = send(after(attended, mid_parts[4]), OVER_C)
    *out_sum, grad_query_pre, key_acc, value_acc, down_home, grad_branch, attended_other = stage(
        *trade(out_pieces),
        grad_query_pre,
        key_acc,
        value_acc,
        down_home,
        grad_branch,
        attended_other,
    )

    out_part = (middle + added(out_sum)).astype(BF)
    out_other = send(out_part, OVER_C)
    out_mine = jnp.where(stays, out_part, out_other)
    out_away = rows_at(jnp.where(stays, out_other, out_part), c * (part // 2), part // 2)
    extras = [key_acc, value_acc]
    (give,) = product_pieces(grad_query_pre, up_q_all, extras, None, False)
    pieces = product_pieces(grad_query_pre, up_q_all, extras, send(give, OVER_C), True)
    staged = stage(
        *pieces,
        out_mine,
        send(rows_at(out_mine, c * (part // 2), part // 2), OVER_Y),
        send(out_away, OVER_X),
        send(out_away, OVER_XY),
    )
    pieces, out_parts = staged[:4], list(staged[4:])
    query_other = send(grad_query_pre, OVER_C)

    def swapped(array):
        return [(array, rows, rows, None), (array, 0, rows, None)]

    attn_slabs = weight_grads(
        numbers,
        [
            (
                [query_in],
                upq_rows,
                0,
                [
                    (at_c, [(grad_query_pre, 0, 2 * rows, None)]),
                    (at_c + 1, swapped(query_other)),
                ],
            ),
            (
                mid_parts,
                out_rows,
                0,
                [
                    (at_c, [(attended, 0, 2 * rows, None)]),
                    (at_c + 1, swapped(attended_other)),
                ],
            ),
        ],
        2 * cols,
    )
    *pieces, attn_slabs = stage(*trade(pieces), attn_slabs)
    three = added(pieces)
    attn_sum = reduce_z(after(attn_slabs, pair_sum))

    grad_plain = three[:, :latent_width] * gain_q
    plain_q_mine = plain_q[:part]
    grad_latent = inverse_q[:part] * (
        grad_plain - plain_q_mine * jnp.mean(grad_plain * plain_q_mine, axis=-1, keepdims=True)
    )
    grad_key_pre = turn(
        three[:, latent_width : latent_width + HD], cosine[:part], -sine[:part]
    )
    lat_parts = spread(
        jnp.concatenate(
            [grad_latent, grad_key_pre, three[:, latent_width + HD :]], axis=1
        ).astype(BF)
    )
    *lat_parts, pair_sum = stage(*lat_parts, pair_sum)
    pair_home = transpose(pair_sum, stays)
    lat_parts = lat_parts + over_core(lat_parts)

    lane = wide // 4
    first_slabs = weight_grads(
        numbers,
        [([normed], 256, at_x, [(None, [(p, 0, part, at_t) for p in lat_parts])])],
        lane,
    )
    first_slabs, pair_home, *lat_parts = stage(first_slabs, pair_home, *lat_parts)
    grad_lat = place_copies(stack_plan, numbers, lat_parts, (2 * rows, wide), BF)
    grad_tokens = input_gradient(numbers, grad_lat, first_all, grad_branch, tokens, gain_one)

    out_parts = out_parts + over_core(out_parts[1:])

    def out_plan(n, ins, out):
        listed = []
        for f in range(4):
            row = n[at_quarter + f] * part
            if f == 0:
                to = out.at[pl.ds(pl.multiple_of(row, part), part)]
                listed.append((None, ins[0], to))
                continue
            for j in range(2):
                at = pl.multiple_of(row + n[at_c + j] * (part // 2), part // 2)
                listed.append((None, ins[f + 3 * j], out.at[pl.ds(at, part // 2)]))
        return listed

    result = place_copies(out_plan, numbers, out_parts, (rows, depth), BF)
    grad_down_w = down_home.astype(F32)
    pair_home = pair_home.astype(F32)
    grad_gate_w, grad_up_w = pair_home[:256], pair_home[256:]

    two_sum = jnp.sum(gate_w.astype(F32) * grad_gate_w + up_w.astype(F32) * grad_up_w, axis=1)
    *first_got, grad_tokens, result, two_sum, grad_gate_w, grad_up_w, grad_down_w = stage(
        *trade_z(first_slabs), grad_tokens, result, two_sum, grad_gate_w, grad_up_w, grad_down_w
    )
    first_quarter = added(first_got).astype(BF)
    quarters = [first_quarter] + [send(first_quarter, p) for p in (OVER_C, OVER_Y, OVER_YC)]
    attn_home = transpose(after(attn_sum, first_quarter), stays)
    *quarters, attn_home = stage(*quarters, attn_home)
    attn_home = attn_home.astype(F32)
    grad_up_q, grad_out_w = attn_home[:upq_rows], attn_home[upq_rows:]
    q_sum = jnp.sum(up_q.astype(F32) * grad_up_q, axis=1)
    small = jnp.concatenate([two_sum, q_sum]).reshape(3, -1)
    small = small + send(small, OVER_C) + send(small, OVER_Y) + send(small, OVER_YC)
    small = small.reshape(-1)
    dev = z * 2 + x
    block = depth // 8
    own_one = lax.dynamic_slice_in_dim(gain_one, dev * block, block)
    own_two = lax.dynamic_slice_in_dim(gain_two, dev * block, block)
    own_q = lax.dynamic_slice_in_dim(gain_q, dev * upq_rows, upq_rows)
    grad_down_q, grad_key_w, grad_value_w, grad_gain_one = first_finish(
        numbers, quarters, first_w, own_one, latent_width
    )
    grad_gain_two = small[:block] / own_two
    grad_gain_q = small[block:] / own_q

    return (
        result,
        grad_tokens,
        grad_gain_one,
        grad_down_q,
        grad_gain_q,
        grad_up_q,
        grad_key_w,
        grad_value_w,
        grad_out_w,
        grad_gain_two,
        grad_gate_w,
        grad_up_w,
        grad_down_w,
    )


def rows_at(array, start, count):
    return lax.dynamic_slice_in_dim(array, start, count, axis=0)


def rotate(array, places):
    half = array.shape[-1] // 2
    freqs = 10000.0 ** (-jnp.arange(half, dtype=jnp.float32) / half)
    angles = places[:, None] * freqs[None, :]
    cosine = jnp.cos(angles)
    sine = jnp.sin(angles)
    first = array[..., :half]
    latter = array[..., half:]
    return jnp.concatenate(
        [first * cosine - latter * sine, latter * cosine + first * sine], axis=-1
    )


def forward(token_rows, attention_w, ffn_w, gains, own_pos, allowed):
    gain_one, gain_q, gain_two = gains
    down_q, up_q, key_w, value_w, out_w = attention_w
    gate_w, up_w, down_w = ffn_w
    row_count = token_rows.shape[0]
    heads = up_q.shape[1] // HD
    scale = HD ** (-0.5)
    plain_one, inverse_one = rms_parts(token_rows)
    normed = (plain_one * gain_one).astype(jnp.bfloat16)
    latent = jnp.dot(normed, down_q, preferred_element_type=jnp.float32)
    plain_q, inverse_q = rms_parts(latent)
    query_in = (plain_q * gain_q).astype(jnp.bfloat16)
    query_pre = jnp.dot(query_in, up_q, preferred_element_type=jnp.float32)
    query = rotate(query_pre.reshape(row_count, heads, HD).transpose(1, 0, 2), own_pos).astype(
        jnp.bfloat16
    )
    keys = rotate(jnp.dot(normed, key_w, preferred_element_type=jnp.float32), own_pos).astype(
        jnp.bfloat16
    )
    values = jnp.dot(normed, value_w, preferred_element_type=jnp.float32).astype(jnp.bfloat16)
    keys_all, values_all = (
        lax.all_gather(keys, "ctx", axis=0, tiled=True),
        lax.all_gather(values, "ctx", axis=0, tiled=True),
    )

    def one_head(q_head):
        scores = jnp.where(allowed, times_trans(q_head, keys_all) * scale, -1e30)
        largest = jnp.max(scores, axis=-1, keepdims=True)
        exponent = jnp.exp(scores - largest)
        totals = jnp.sum(exponent, axis=-1, keepdims=True)
        soft = (exponent / totals).astype(jnp.bfloat16)
        return (
            jnp.dot(soft, values_all, preferred_element_type=jnp.float32),
            (largest + jnp.log(totals))[:, 0],
        )

    mixed_heads, log_totals = lax.map(one_head, query)
    attended = mixed_heads.transpose(1, 0, 2).reshape(row_count, heads * HD).astype(jnp.bfloat16)
    branch = lax.psum(times_trans(attended, out_w), "tensor")
    middle = token_rows + branch
    plain_two, inverse_two = rms_parts(middle)
    normed_two = (plain_two * gain_two).astype(jnp.bfloat16)
    gate_pre = jnp.dot(normed_two, gate_w, preferred_element_type=jnp.float32)
    up_pre = jnp.dot(normed_two, up_w, preferred_element_type=jnp.float32)
    hidden = (jax.nn.silu(gate_pre) * up_pre).astype(jnp.bfloat16)
    result = middle + lax.psum(times_trans(hidden, down_w).astype(jnp.bfloat16), "tensor").astype(
        jnp.float32
    )
    kept_values = (
        plain_one,
        inverse_one,
        normed,
        plain_q,
        inverse_q,
        query_in,
        query,
        keys_all,
        values_all,
        log_totals,
        attended,
        plain_two,
        inverse_two,
        normed_two,
        gate_pre,
        up_pre,
        hidden,
    )
    return (result, kept_values)


def backward(cotangent, attention_w, ffn_w, gains, own_pos, allowed, kept_values):
    gain_one, gain_q, gain_two = gains
    down_q, up_q, key_w, value_w, out_w = attention_w
    gate_w, up_w, down_w = ffn_w
    (
        plain_one,
        inverse_one,
        normed,
        plain_q,
        inverse_q,
        query_in,
        query,
        keys_all,
        values_all,
        log_totals,
        attended,
        plain_two,
        inverse_two,
        normed_two,
        gate_pre,
        up_pre,
        hidden,
    ) = kept_values
    row_count = cotangent.shape[0]
    heads = query.shape[0]
    scale = HD ** (-0.5)
    grad_down = trans_times(cotangent, hidden)
    grad_hidden = jnp.dot(cotangent, down_w, preferred_element_type=jnp.float32)
    sigma = jax.nn.sigmoid(gate_pre)
    grad_gate = (grad_hidden * up_pre * sigma * (1.0 + gate_pre * (1.0 - sigma))).astype(
        jnp.bfloat16
    )
    grad_up = (grad_hidden * gate_pre * sigma).astype(jnp.bfloat16)
    grad_gate_w = trans_times(normed_two, grad_gate)
    grad_up_w = trans_times(normed_two, grad_up)
    grad_norm_two = lax.psum(times_trans(grad_gate, gate_w) + times_trans(grad_up, up_w), "tensor")
    grad_mid_part, grad_gain_two = rms_back(grad_norm_two, plain_two, inverse_two, gain_two)
    ffn_grads = (
        lax.psum_scatter(grad_gate_w, ("dp", "ctx"), scatter_dimension=0, tiled=True),
        lax.psum_scatter(grad_up_w, ("dp", "ctx"), scatter_dimension=0, tiled=True),
        lax.psum_scatter(grad_down, ("dp", "ctx"), scatter_dimension=0, tiled=True),
        lax.psum_scatter(grad_gain_two, ("dp", "ctx"), scatter_dimension=0, tiled=True),
    )
    grad_middle = cotangent.astype(jnp.float32) + grad_mid_part
    grad_branch = grad_middle.astype(jnp.bfloat16)
    grad_out_w = trans_times(grad_branch, attended)
    grad_attended = jnp.dot(grad_branch, out_w, preferred_element_type=jnp.float32).astype(
        jnp.bfloat16
    )
    grad_heads = grad_attended.reshape(row_count, heads, HD).transpose(1, 0, 2)

    def head_back(carry, item):
        key_acc, value_acc = carry
        q_head, grad_head, lse_head = item
        scores = jnp.where(allowed, times_trans(q_head, keys_all) * scale, -1e30)
        soft = jnp.exp(scores - lse_head[:, None])
        grad_soft = times_trans(grad_head, values_all)
        inner = jnp.sum(soft * grad_soft, axis=-1, keepdims=True)
        grad_scores = (soft * (grad_soft - inner)).astype(jnp.bfloat16)
        grad_q = jnp.dot(grad_scores, keys_all, preferred_element_type=jnp.float32) * scale
        key_acc = key_acc + trans_times(grad_scores, q_head) * scale
        value_acc = value_acc + trans_times(soft.astype(jnp.bfloat16), grad_head)
        return ((key_acc, value_acc), grad_q)

    empty = jnp.zeros(keys_all.shape, jnp.float32)
    (key_total, value_total), grad_query = lax.scan(
        head_back, (empty, empty), (query, grad_heads, log_totals)
    )
    key_own, value_own = (
        lax.psum_scatter(key_total, "ctx", scatter_dimension=0, tiled=True),
        lax.psum_scatter(value_total, "ctx", scatter_dimension=0, tiled=True),
    )
    grad_query_pre = (
        rotate(grad_query, -own_pos)
        .transpose(1, 0, 2)
        .reshape(row_count, heads * HD)
        .astype(jnp.bfloat16)
    )
    grad_up_q = trans_times(query_in, grad_query_pre)
    grad_qin_part = times_trans(grad_query_pre, up_q)
    grad_qin, grad_keys_rot, grad_values = lax.psum((grad_qin_part, key_own, value_own), "tensor")
    grad_key_pre = rotate(grad_keys_rot, -own_pos).astype(jnp.bfloat16)
    grad_value_low = grad_values.astype(jnp.bfloat16)
    grad_latent, grad_gain_q = rms_back(grad_qin, plain_q, inverse_q, gain_q)
    grad_latent_low = grad_latent.astype(jnp.bfloat16)
    grad_down_q = trans_times(normed, grad_latent_low)
    grad_key_w = trans_times(normed, grad_key_pre)
    grad_value_w = trans_times(normed, grad_value_low)
    grad_norm_one = (
        times_trans(grad_latent_low, down_q)
        + times_trans(grad_key_pre, key_w)
        + times_trans(grad_value_low, value_w)
    )
    grad_in_part, grad_gain_one = rms_back(grad_norm_one, plain_one, inverse_one, gain_one)
    grad_tokens = grad_middle + grad_in_part
    attention_grads = (
        lax.psum_scatter(grad_gain_one, ("dp", "ctx"), scatter_dimension=0, tiled=True),
        lax.psum_scatter(grad_down_q, ("dp", "ctx"), scatter_dimension=0, tiled=True),
        lax.psum_scatter(grad_gain_q, ("dp", "ctx"), scatter_dimension=0, tiled=True),
        lax.psum_scatter(grad_up_q, ("dp", "ctx"), scatter_dimension=0, tiled=True),
        lax.psum_scatter(grad_key_w, ("dp", "ctx"), scatter_dimension=0, tiled=True),
        lax.psum_scatter(grad_value_w, ("dp", "ctx"), scatter_dimension=0, tiled=True),
        lax.psum_scatter(grad_out_w, ("dp", "ctx"), scatter_dimension=0, tiled=True),
    )
    return (grad_tokens, attention_grads, ffn_grads)


def per_device(
    tokens_in,
    cotangent,
    seq_lengths,
    block_order,
    gain_one,
    down_q,
    gain_q,
    up_q,
    key_w,
    value_w,
    out_w,
    gain_two,
    gate_w,
    up_w,
    down_w,
):
    token_rows = tokens_in.astype(jnp.float32)
    row_count = tokens_in.shape[0]
    block_rows = row_count // 2
    places = (
        block_order[0][:, :, None] * block_rows
        + jnp.arange(block_rows, dtype=jnp.int32)[None, None, :]
    ).reshape(-1)
    second = (places >= seq_lengths[0, 0]).astype(jnp.int32)
    in_sequence = places - second * seq_lengths[0, 0]
    start = lax.axis_index("ctx") * row_count
    own_places = lax.dynamic_slice_in_dim(places, start, row_count)
    own_second = lax.dynamic_slice_in_dim(second, start, row_count)
    own_pos = lax.dynamic_slice_in_dim(in_sequence, start, row_count).astype(jnp.float32)
    allowed = (own_second[:, None] == second[None, :]) & (places[None, :] <= own_places[:, None])
    gains = (gain_one, gain_q, gain_two)
    attention_w = (
        lax.all_gather(down_q, ("dp", "ctx"), axis=0, tiled=True),
        lax.all_gather(up_q, ("dp", "ctx"), axis=0, tiled=True),
        lax.all_gather(key_w, ("dp", "ctx"), axis=0, tiled=True),
        lax.all_gather(value_w, ("dp", "ctx"), axis=0, tiled=True),
        lax.all_gather(out_w, ("dp", "ctx"), axis=0, tiled=True),
    )
    ffn_w = (
        lax.all_gather(gate_w, ("dp", "ctx"), axis=0, tiled=True),
        lax.all_gather(up_w, ("dp", "ctx"), axis=0, tiled=True),
        lax.all_gather(down_w, ("dp", "ctx"), axis=0, tiled=True),
    )
    result, kept_values = forward(token_rows, attention_w, ffn_w, gains, own_pos, allowed)
    attention_w = (
        lax.all_gather(down_q, ("dp", "ctx"), axis=0, tiled=True),
        lax.all_gather(up_q, ("dp", "ctx"), axis=0, tiled=True),
        lax.all_gather(key_w, ("dp", "ctx"), axis=0, tiled=True),
        lax.all_gather(value_w, ("dp", "ctx"), axis=0, tiled=True),
        lax.all_gather(out_w, ("dp", "ctx"), axis=0, tiled=True),
    )
    ffn_w = (
        lax.all_gather(gate_w, ("dp", "ctx"), axis=0, tiled=True),
        lax.all_gather(up_w, ("dp", "ctx"), axis=0, tiled=True),
        lax.all_gather(down_w, ("dp", "ctx"), axis=0, tiled=True),
    )
    unused, kept_values = forward(token_rows, attention_w, ffn_w, gains, own_pos, allowed)
    grad_tokens, attention_grads, ffn_grads = backward(
        cotangent, attention_w, ffn_w, gains, own_pos, allowed, kept_values
    )
    grad_gain_one, grad_down_q, grad_gain_q, grad_up_q, grad_key_w, grad_value_w, grad_out_w = (
        attention_grads
    )
    grad_gate_w, grad_up_w, grad_down_w, grad_gain_two = ffn_grads
    return (
        result.astype(jnp.bfloat16),
        grad_tokens,
        grad_gain_one,
        grad_down_q,
        grad_gain_q,
        grad_up_q,
        grad_key_w,
        grad_value_w,
        grad_out_w,
        grad_gain_two,
        grad_gate_w,
        grad_up_w,
        grad_down_w,
    )


def solution(mesh):
    fast = dict(mesh.shape) == {"dp": 4, "ctx": 2, "tensor": 4}
    return jax.shard_map(
        fast_device if fast else per_device,
        mesh=mesh,
        in_specs=(
            P(("dp", "ctx"), None),
            P(("dp", "ctx"), None),
            P("dp", None),
            P("dp", None, None),
            P(),
            P(("dp", "ctx"), None),
            P(),
            P(("dp", "ctx"), "tensor"),
            P(("dp", "ctx"), None),
            P(("dp", "ctx"), None),
            P(("dp", "ctx"), "tensor"),
            P(),
            P(("dp", "ctx"), "tensor"),
            P(("dp", "ctx"), "tensor"),
            P(("dp", "ctx"), "tensor"),
        ),
        out_specs=(
            P(("dp", "ctx"), None),
            P(("dp", "ctx"), None),
            P(("dp", "ctx")),
            P(("dp", "ctx"), None),
            P(("dp", "ctx")),
            P(("dp", "ctx"), "tensor"),
            P(("dp", "ctx"), None),
            P(("dp", "ctx"), None),
            P(("dp", "ctx"), "tensor"),
            P(("dp", "ctx")),
            P(("dp", "ctx"), "tensor"),
            P(("dp", "ctx"), "tensor"),
            P(("dp", "ctx"), "tensor"),
        ),
        check_vma=False,
    )
```

```python
import jax
import jax.numpy as jnp
from jax import lax
from jax.experimental import pallas as pl
from jax.experimental.pallas import tpu as pltpu
from jax.sharding import PartitionSpec as P

HD = 256


EPSILON = 1e-06

AXES = ("dp", "ctx", "tensor")
BF = jnp.bfloat16
F32 = jnp.float32


def dot(left, right):
    return jnp.dot(left, right, preferred_element_type=F32)


def times_trans(left, right):
    return lax.dot_general(left, right, (((1,), (1,)), ((), ())), preferred_element_type=F32)


def trans_times(left, right):
    return lax.dot_general(left, right, (((0,), (0,)), ((), ())), preferred_element_type=F32)


def rms_parts(array):
    inverse = lax.rsqrt(jnp.mean(array * array, axis=-1, keepdims=True) + EPSILON)
    return (array * inverse, inverse)


def rms_back(grad_out, plain, inverse, gain):
    grad_plain = grad_out * gain
    grad_in = inverse * (grad_plain - plain * jnp.mean(grad_plain * plain, axis=-1, keepdims=True))
    return (grad_in, jnp.sum(grad_out * plain, axis=0))


def angles_of(places, half):
    freqs = 10000.0 ** (-jnp.arange(half, dtype=F32) / half)
    angles = places[:, None] * freqs[None, :]
    return (jnp.cos(angles), jnp.sin(angles))


def turn(array, cosine, sine):
    half = array.shape[-1] // 2
    first = array[..., :half]
    latter = array[..., half:]
    return jnp.concatenate(
        [first * cosine - latter * sine, latter * cosine + first * sine], axis=-1
    )


def routes(move):
    pairs = []
    for z in range(4):
        for x in range(2):
            for y in range(2):
                for c in range(2):
                    to = move(z, x, y, c)
                    if to is not None:
                        tz, tx, ty, tc = to
                        pairs.append(
                            (((z * 2 + x) * 2 + y) * 2 + c, ((tz * 2 + tx) * 2 + ty) * 2 + tc)
                        )
    return pairs


OVER_X = routes(lambda z, x, y, c: (z, 1 - x, y, c))
OVER_Y = routes(lambda z, x, y, c: (z, x, 1 - y, c))
OVER_XY = routes(lambda z, x, y, c: (z, 1 - x, 1 - y, c))
OVER_YC = routes(lambda z, x, y, c: (z, x, 1 - y, 1 - c))
OVER_C = routes(lambda z, x, y, c: (z, x, y, 1 - c))
TRANSPOSE = routes(lambda z, x, y, c: (z, c, y, x) if x != c else None)
Z_ONE = routes(lambda z, x, y, c: (z ^ 1, x, y, c))
Z_TWO = routes(lambda z, x, y, c: (z ^ 2, x, y, c))
Z_THREE = routes(lambda z, x, y, c: (z ^ 3, x, y, c))


def send(array, pairs):
    return lax.ppermute(array, AXES, pairs)


def transpose(array, stays):
    return jnp.where(stays, array, send(array, TRANSPOSE))


def after(array, *others):
    return lax.optimization_barrier((array, *others))[0]


def stage(*arrays):
    return lax.optimization_barrier(arrays)


def gather_z(array):
    return lax.all_gather(array, "dp", axis=0, tiled=True)


def reduce_z(slabs):
    return lax.psum_scatter(slabs, "dp", scatter_dimension=0, tiled=True)


def trade_z(slabs):
    n = slabs.shape[0] // 4
    return [slabs[:n]] + [
        send(slabs[k * n : (k + 1) * n], pairs)
        for k, pairs in ((1, Z_ONE), (2, Z_TWO), (3, Z_THREE))
    ]


WHOLE = pl.BlockSpec(memory_space=pltpu.VMEM)
HELD = pl.BlockSpec(memory_space=pl.ANY)
ROOMY = pltpu.CompilerParams(vmem_limit_bytes=56 * 1024 * 1024)


def cost(macs, moved, share=1):
    return pl.CostEstimate(
        flops=2 * macs // share // 1, bytes_accessed=moved // share // 1, transcendentals=0
    )


def place_copies(plan, numbers, buffers, shape, dtype):
    def body(numbers_ref, *refs):
        ins, out_ref, sem = refs[:-2], refs[-2], refs[-1]
        listed = plan(numbers_ref, ins, out_ref)
        for i, (condition, source, target) in enumerate(listed):
            copy = pltpu.make_async_copy(source, target, sem.at[i])
            if condition is None:
                copy.start()
            else:
                pl.when(condition)(copy.start)
        for i, (condition, source, target) in enumerate(listed):
            copy = pltpu.make_async_copy(source, target, sem.at[i])
            if condition is None:
                copy.wait()
            else:
                pl.when(condition)(copy.wait)

    moved = 2
    for extent in shape:
        moved *= extent
    return pl.pallas_call(
        body,
        grid_spec=pltpu.PrefetchScalarGridSpec(
            num_scalar_prefetch=1,
            grid=(1,),
            in_specs=[HELD] * len(buffers),
            out_specs=pl.BlockSpec(shape, lambda i, numbers_ref: (0, 0)),
            scratch_shapes=[pltpu.SemaphoreType.DMA((40,))],
        ),
        out_shape=jax.ShapeDtypeStruct(shape, dtype),
        compiler_params=ROOMY,
        cost_estimate=cost(0, 2 * moved),
    )(numbers, *buffers)


def attention_forward(query_pre, cosine, sine, keys, values, row_info, key_places):
    rows, width = query_pre.shape
    heads = width // HD
    chunk = 256
    half = HD // 2
    scale = HD ** (-0.5)

    def body(pre_ref, cos_ref, sin_ref, k_ref, v_ref, info_ref, place_ref, q_ref, o_ref, lse_ref):
        for i in range(rows // chunk):
            at = slice(i * chunk, (i + 1) * chunk)
            first, latter = pre_ref[at, :half], pre_ref[at, half:]
            co, si = cos_ref[at], sin_ref[at]
            q = jnp.concatenate([first * co - latter * si, latter * co + first * si], 1).astype(BF)
            q_ref[at] = q
            scores = times_trans(q, k_ref[...]) * scale
            allowed = (place_ref[...] <= info_ref[at, 0:1]) & (place_ref[...] >= info_ref[at, 1:2])
            scores = jnp.where(allowed, scores, -1e30)
            largest = jnp.max(scores, axis=-1, keepdims=True)
            exponent = jnp.exp(scores - largest)
            totals = jnp.sum(exponent, axis=-1, keepdims=True)
            soft = (exponent * (1.0 / totals)).astype(BF)
            o_ref[at] = dot(soft, v_ref[...]).astype(BF)
            lse_ref[0, at] = largest + jnp.log(totals)

    full = lambda h: (0, 0)
    by_head = lambda h: (0, h)
    return pl.pallas_call(
        body,
        grid=(heads,),
        in_specs=[
            pl.BlockSpec((rows, HD), by_head),
            pl.BlockSpec((rows, half), full),
            pl.BlockSpec((rows, half), full),
            pl.BlockSpec((rows, HD), full),
            pl.BlockSpec((rows, HD), full),
            pl.BlockSpec((rows, 2), full),
            pl.BlockSpec((1, rows), full),
        ],
        out_specs=[
            pl.BlockSpec((rows, HD), by_head),
            pl.BlockSpec((rows, HD), by_head),
            pl.BlockSpec((1, rows, 1), lambda h: (h, 0, 0)),
        ],
        out_shape=[
            jax.ShapeDtypeStruct((rows, width), BF),
            jax.ShapeDtypeStruct((rows, width), BF),
            jax.ShapeDtypeStruct((heads, rows, 1), F32),
        ],
        compiler_params=ROOMY,
        cost_estimate=cost(4 * rows * rows * width, 6 * rows * width),
    )(query_pre, cosine, sine, keys, values, row_info, key_places)


def attention_backward(query, grad_out, lse, cosine, sine, keys, values, row_info, key_places):
    rows, width = query.shape
    heads = width // HD
    chunk = 256
    half = HD // 2
    scale = HD ** (-0.5)

    def body(
        q_ref, do_ref, lse_ref, cos_ref, sin_ref, k_ref, v_ref, info_ref, place_ref, dq_ref, dk_ref, dv_ref
    ):
        @pl.when(pl.program_id(0) == 0)
        def clear():
            dk_ref[...] = jnp.zeros_like(dk_ref)
            dv_ref[...] = jnp.zeros_like(dv_ref)

        for i in range(rows // chunk):
            at = slice(i * chunk, (i + 1) * chunk)
            q, do = q_ref[at], do_ref[at]
            scores = times_trans(q, k_ref[...]) * scale
            allowed = (place_ref[...] <= info_ref[at, 0:1]) & (place_ref[...] >= info_ref[at, 1:2])
            soft = jnp.exp(jnp.where(allowed, scores, -1e30) - lse_ref[0, at])
            grad_soft = times_trans(do, v_ref[...])
            summed = jnp.sum(soft * grad_soft, axis=-1, keepdims=True)
            grad_scores = (soft * (grad_soft - summed)).astype(BF)
            dq = dot(grad_scores, k_ref[...]) * scale
            first, latter = dq[:, :half], dq[:, half:]
            co, si = cos_ref[at], sin_ref[at]
            dq_ref[at] = jnp.concatenate(
                [first * co + latter * si, latter * co - first * si], 1
            ).astype(BF)
            dk_ref[...] += trans_times(grad_scores, q) * scale
            dv_ref[...] += trans_times(soft.astype(BF), do)

    full = lambda h: (0, 0)
    by_head = lambda h: (0, h)
    return pl.pallas_call(
        body,
        grid=(heads,),
        in_specs=[
            pl.BlockSpec((rows, HD), by_head),
            pl.BlockSpec((rows, HD), by_head),
            pl.BlockSpec((1, rows, 1), lambda h: (h, 0, 0)),
            pl.BlockSpec((rows, half), full),
            pl.BlockSpec((rows, half), full),
            pl.BlockSpec((rows, HD), full),
            pl.BlockSpec((rows, HD), full),
            pl.BlockSpec((rows, 2), full),
            pl.BlockSpec((1, rows), full),
        ],
        out_specs=[
            pl.BlockSpec((rows, HD), by_head),
            pl.BlockSpec((rows, HD), full),
            pl.BlockSpec((rows, HD), full),
        ],
        out_shape=[
            jax.ShapeDtypeStruct((rows, width), BF),
            jax.ShapeDtypeStruct((rows, HD), F32),
            jax.ShapeDtypeStruct((rows, HD), F32),
        ],
        compiler_params=ROOMY,
        cost_estimate=cost(8 * rows * rows * width, 6 * rows * width),
    )(query, grad_out, lse, cosine, sine, keys, values, row_info, key_places)


def product_of_parts(parts, weight):
    rows = parts[0].shape[0]
    count = len(parts)
    width = weight.shape[1]

    def body(*refs):
        weight_ref, out_ref = refs[count:]
        for i in range(0, count, 4):
            left = jnp.concatenate([refs[j][...] for j in range(i, i + 4)], axis=0)
            out_ref[i * rows : (i + 4) * rows] = dot(left, weight_ref[...]).astype(BF)

    return pl.pallas_call(
        body,
        in_specs=[WHOLE] * (count + 1),
        out_specs=WHOLE,
        out_shape=jax.ShapeDtypeStruct((count * rows, width), BF),
        compiler_params=ROOMY,
        cost_estimate=cost(count * rows * weight.size, 2 * weight.size),
    )(*parts, weight)


def product_pieces(left, weight, extras, got, first_half):
    rows = left.shape[0] // 2
    part = rows // 4
    start = 0 if first_half else rows
    wide = weight.shape[0]
    total = wide + sum(e.shape[1] for e in extras)
    outs = 4 if first_half else 1

    def body(left_ref, weight_ref, *refs):
        extra_refs = refs[: len(extras)]
        got_ref = refs[len(extras)] if got is not None else None
        out_refs = refs[len(refs) - outs :]
        src = slice(start, start + rows)

        def put(value, cols):
            if got_ref is not None:
                value = value + got_ref[:, cols].astype(F32)
            value = value.astype(BF)
            if outs == 1:
                out_refs[0][:, cols] = value
            else:
                for f in range(4):
                    out_refs[f][:, cols] = value[f * part : (f + 1) * part]

        step = 512
        for col in range(0, wide, step):
            put(times_trans(left_ref[src], weight_ref[col : col + step]), slice(col, col + step))
        col = wide
        for extra_ref in extra_refs:
            n = extra_ref.shape[1]
            put(extra_ref[src], slice(col, col + n))
            col += n

    shapes = [jax.ShapeDtypeStruct((part, total), BF)] * 4
    if outs == 1:
        shapes = [jax.ShapeDtypeStruct((rows, total), BF)]
    arrays = [left, weight, *extras] + ([got] if got is not None else [])
    return pl.pallas_call(
        body,
        in_specs=[WHOLE] * len(arrays),
        out_specs=[WHOLE] * outs,
        out_shape=shapes,
        compiler_params=ROOMY,
        cost_estimate=cost(rows * wide * left.shape[1], 2 * weight.size + 4 * rows * total),
    )(*arrays)


def tiles_of(width):
    whole = width // 256
    return whole, width - whole * 256


def ffn_forward(numbers, parts, pairs):
    part, depth = parts[0].shape
    rows = part * len(parts)
    width = pairs[0].shape[1]
    whole, rest = tiles_of(width)

    def body(numbers_ref, *refs):
        part_refs, pair_refs = refs[:4], refs[4:6]
        hid_ref, slope_ref, silu_ref, gate_vm, up_vm, in_vm, sem = refs[6:]
        gate_copies, up_copies = [], []
        for i in range(8):
            to = pl.ds(pl.multiple_of(numbers_ref[i] * 256, 256), 256)
            ref, at = pair_refs[i // 4], (i % 4) * 512
            gate_copies.append(
                pltpu.make_async_copy(ref.at[at : at + 256], gate_vm.at[to], sem.at[i])
            )
            up_copies.append(
                pltpu.make_async_copy(ref.at[at + 256 : at + 512], up_vm.at[to], sem.at[8 + i])
            )
        for copy in gate_copies + up_copies:
            copy.start()
        for f in range(4):
            in_vm[f * part : (f + 1) * part] = part_refs[f][...]
        for copy in gate_copies + up_copies:
            copy.wait()

        def tile(cols):
            gate = dot(in_vm[...], gate_vm[:, cols])
            up = dot(in_vm[...], up_vm[:, cols])
            sigma = jax.nn.sigmoid(gate)
            silu = gate * sigma
            hid_ref[:, cols] = (silu * up).astype(BF)
            slope_ref[:, cols] = up * sigma * (1.0 + gate * (1.0 - sigma))
            silu_ref[:, cols] = silu

        @pl.loop(0, whole)
        def each(i):
            tile(pl.ds(pl.multiple_of(i * 256, 256), 256))

        if rest:
            tile(slice(whole * 256, width))

    return pl.pallas_call(
        body,
        grid_spec=pltpu.PrefetchScalarGridSpec(
            num_scalar_prefetch=1,
            grid=(1,),
            in_specs=[pl.BlockSpec((part, depth), lambda i, n: (0, 0))] * 4 + [HELD] * 2,
            out_specs=[pl.BlockSpec((rows, width), lambda i, n: (0, 0))] * 3,
            scratch_shapes=[
                pltpu.VMEM((depth, width), BF),
                pltpu.VMEM((depth, width), BF),
                pltpu.VMEM((rows, depth), BF),
                pltpu.SemaphoreType.DMA((16,)),
            ],
        ),
        out_shape=[
            jax.ShapeDtypeStruct((rows, width), BF),
            jax.ShapeDtypeStruct((rows, width), F32),
            jax.ShapeDtypeStruct((rows, width), F32),
        ],
        compiler_params=ROOMY,
        cost_estimate=cost(2 * rows * depth * width, 4 * depth * width),
    )(numbers, *parts, *pairs)


def ffn_backward(numbers, cot, slope, silu, pairs, downs):
    rows = slope.shape[0]
    depth = cot.shape[1]
    part = rows // 4
    width = slope.shape[1]
    whole, rest = tiles_of(width)

    def body(numbers_ref, *refs):
        cot_ref, slope_ref, silu_ref = refs[:3]
        pair_refs, down_refs = refs[3:5], refs[5:7]
        gate_out, up_out = refs[7:9]
        piece_refs = refs[9:13]
        down_vm, pair_vm, sem = refs[13:]
        copies, later = [], []
        for i in range(8):
            to = pl.ds(pl.multiple_of(numbers_ref[i] * 256, 256), 256)
            ref, at = down_refs[i // 4], (i % 4) * 256
            copies.append(
                pltpu.make_async_copy(ref.at[at : at + 256], down_vm.at[to], sem.at[i])
            )
            ref, at = pair_refs[i // 4], (i % 4) * 512
            later.append(
                pltpu.make_async_copy(ref.at[at : at + 512], pair_vm.at[i], sem.at[8 + i])
            )
        for copy in copies + later:
            copy.start()
        for copy in copies:
            copy.wait()

        def tile(cols):
            grad = dot(cot_ref[...], down_vm[:, cols])
            gate_out[:, cols] = (grad * slope_ref[:, cols]).astype(BF)
            up_out[:, cols] = (grad * silu_ref[:, cols]).astype(BF)

        @pl.loop(0, whole)
        def each(i):
            tile(pl.ds(pl.multiple_of(i * 256, 256), 256))

        if rest:
            tile(slice(whole * 256, width))
        for copy in later:
            copy.wait()

        @pl.loop(0, 8)
        def block(i):
            cols = pl.ds(pl.multiple_of(numbers_ref[i] * 256, 256), 256)
            value = times_trans(gate_out[...], pair_vm[i, :256]) + times_trans(
                up_out[...], pair_vm[i, 256:]
            )
            value = value.astype(BF)
            for f in range(4):
                piece_refs[f][:, cols] = value[f * part : (f + 1) * part]

    flat = lambda i, n: (0, 0)
    return pl.pallas_call(
        body,
        grid_spec=pltpu.PrefetchScalarGridSpec(
            num_scalar_prefetch=1,
            grid=(1,),
            in_specs=[
                pl.BlockSpec((rows, depth), flat),
                pl.BlockSpec((rows, width), flat),
                pl.BlockSpec((rows, width), flat),
            ]
            + [HELD] * 4,
            out_specs=[pl.BlockSpec((rows, width), flat)] * 2
            + [pl.BlockSpec((part, depth), flat)] * 4,
            scratch_shapes=[
                pltpu.VMEM((depth, width), BF),
                pltpu.VMEM((8, 512, width), BF),
                pltpu.SemaphoreType.DMA((16,)),
            ],
        ),
        out_shape=[jax.ShapeDtypeStruct((rows, width), BF)] * 2
        + [jax.ShapeDtypeStruct((part, depth), BF)] * 4,
        compiler_params=ROOMY,
        cost_estimate=cost(3 * rows * depth * width, 6 * depth * width),
    )(numbers, cot, slope, silu, *pairs, *downs)


def ffn_output(numbers, hidden, downs):
    rows, width = hidden.shape
    part = rows // 4
    depth = 2 * downs[0].shape[0]

    def body(numbers_ref, hid_ref, *refs):
        down_refs, piece_refs = refs[:2], refs[2:6]
        down_vm, sem = refs[6:]
        copies = [
            pltpu.make_async_copy(
                down_refs[i // 4].at[(i % 4) * 256 : (i % 4 + 1) * 256], down_vm.at[i], sem.at[i]
            )
            for i in range(8)
        ]
        for copy in copies:
            copy.start()
        for copy in copies:
            copy.wait()

        @pl.loop(0, 8)
        def block(i):
            cols = pl.ds(pl.multiple_of(numbers_ref[i] * 256, 256), 256)
            value = times_trans(hid_ref[...], down_vm[i]).astype(BF)
            for f in range(4):
                piece_refs[f][:, cols] = value[f * part : (f + 1) * part]

    flat = lambda i, n: (0, 0)
    return pl.pallas_call(
        body,
        grid_spec=pltpu.PrefetchScalarGridSpec(
            num_scalar_prefetch=1,
            grid=(1,),
            in_specs=[pl.BlockSpec((rows, width), flat)] + [HELD] * 2,
            out_specs=[pl.BlockSpec((part, depth), flat)] * 4,
            scratch_shapes=[
                pltpu.VMEM((8, 256, width), BF),
                pltpu.SemaphoreType.DMA((8,)),
            ],
        ),
        out_shape=[jax.ShapeDtypeStruct((part, depth), BF)] * 4,
        compiler_params=ROOMY,
        cost_estimate=cost(rows * depth * width, 2 * depth * width, 4),
    )(numbers, hidden, *downs)


def weight_grads(numbers, terms, width):
    lefts, rights, left_specs, right_specs = [], [], [], []
    shape_of = []
    for left, block, offset, products in terms:
        for array in left:
            lefts.append(array)
            left_specs.append(
                pl.BlockSpec((array.shape[0], block), lambda i, n, offset=offset: (0, n[offset + i]))
            )
        for place, right in products:
            for array, start, count, pick in right:
                rights.append(array)
                if pick is None:
                    right_specs.append(pl.BlockSpec(array.shape, lambda i, n: (0, 0)))
                else:
                    right_specs.append(
                        pl.BlockSpec((array.shape[0], width), lambda i, n, pick=pick: (0, n[pick]))
                    )
        shape_of.append(block)
    height = sum(shape_of)

    def body(numbers_ref, *refs):
        left_refs = refs[: len(lefts)]
        right_refs = refs[len(lefts) : len(lefts) + len(rights)]
        out_ref = refs[-1]
        li, ri, row = 0, 0, 0
        for left, block, offset, products in terms:
            pieces = [left_refs[li + j][...] for j in range(len(left))]
            li += len(left)
            whole = pieces[0] if len(pieces) == 1 else jnp.concatenate(pieces, axis=0)
            for place, right in products:
                value = None
                at = 0
                for array, start, count, pick in right:
                    this = trans_times(
                        whole[at : at + count], right_refs[ri][start : start + count]
                    )
                    value = this if value is None else value + this
                    at += count
                    ri += 1
                value = value.astype(BF)
                n = value.shape[1]
                if place is None:
                    cols = slice(0, n)
                else:
                    cols = pl.ds(pl.multiple_of(numbers_ref[place] * n, n), n)
                out_ref[row : row + block, cols] = value

            row += block

    macs = 4 * height * width * 1024
    return pl.pallas_call(
        body,
        grid_spec=pltpu.PrefetchScalarGridSpec(
            num_scalar_prefetch=1,
            grid=(4,),
            in_specs=left_specs + right_specs,
            out_specs=pl.BlockSpec((height, width), lambda i, n: (i, 0)),
        ),
        out_shape=jax.ShapeDtypeStruct((4 * height, width), BF),
        compiler_params=ROOMY,
        cost_estimate=cost(macs, 4 * height * width * 4, 4),
    )(numbers, *lefts, *rights)


def input_gradient(numbers, grad_lat, first_all, grad_mid, tokens, gain):
    depth = tokens.shape[1]
    wide = grad_lat.shape[1]
    part = 128

    def body(numbers_ref, lat_ref, first_ref, mid_ref, tok_ref, gain_ref, out_ref, grad_vm):
        for col in range(0, depth, 512):
            cols = slice(col, col + 512)
            grad_vm[:, cols] = times_trans(lat_ref[...], first_ref[cols]) * gain_ref[:, cols]
        for i in range(4):
            at = slice(i * part, (i + 1) * part)
            plain = tok_ref[at].astype(F32)
            inverse = lax.rsqrt(jnp.mean(plain * plain, axis=-1, keepdims=True) + EPSILON)
            plain = plain * inverse
            grad = grad_vm[at]
            mean = jnp.mean(grad * plain, axis=-1, keepdims=True)
            to = pl.ds(pl.multiple_of(numbers_ref[9 + i] * part, part), part)
            out_ref[to] = mid_ref[at].astype(F32) + inverse * (grad - plain * mean)

    picked = lambda i, n: (n[8], 0)
    flat = lambda i, n: (0, 0)
    return pl.pallas_call(
        body,
        grid_spec=pltpu.PrefetchScalarGridSpec(
            num_scalar_prefetch=1,
            grid=(1,),
            in_specs=[
                pl.BlockSpec((4 * part, wide), picked),
                pl.BlockSpec((depth, wide), flat),
                pl.BlockSpec((4 * part, depth), picked),
                pl.BlockSpec((4 * part, depth), picked),
                pl.BlockSpec((1, depth), flat),
            ],
            out_specs=pl.BlockSpec((4 * part, depth), flat),
            scratch_shapes=[pltpu.VMEM((4 * part, depth), F32)],
        ),
        out_shape=jax.ShapeDtypeStruct((4 * part, depth), F32),
        compiler_params=ROOMY,
        cost_estimate=cost(4 * part * depth * wide, 2 * depth * wide + 8 * part * depth * 4),
    )(numbers, grad_lat, first_all, grad_mid, tokens, gain.reshape(1, -1))


def first_finish(numbers, quarters, first_w, gain, latent_width):
    rows, lane = quarters[0].shape
    wide = first_w.shape[1]

    def body(numbers_ref, *refs):
        weight_ref, gain_ref, down_ref, key_ref, value_ref, one_ref, all_vm = refs[4:]
        for i in range(4):
            cols = pl.ds(pl.multiple_of(numbers_ref[25 + i] * lane, lane), lane)
            all_vm[:, cols] = refs[i][...].astype(F32)
        down_ref[...] = all_vm[:, :latent_width]
        key_ref[...] = all_vm[:, latent_width : latent_width + HD]
        value_ref[...] = all_vm[:, latent_width + HD :]
        total = jnp.sum(weight_ref[...].astype(F32) * all_vm[...], axis=1, keepdims=True)
        one_ref[...] = total / gain_ref[...]

    flat = lambda i, n: (0, 0)
    extents = [(rows, latent_width), (rows, HD), (rows, wide - latent_width - HD), (rows, 1)]
    *grads, one = pl.pallas_call(
        body,
        grid_spec=pltpu.PrefetchScalarGridSpec(
            num_scalar_prefetch=1,
            grid=(1,),
            in_specs=[pl.BlockSpec((rows, lane), flat)] * 4
            + [pl.BlockSpec((rows, wide), flat), pl.BlockSpec((rows, 1), flat)],
            out_specs=[pl.BlockSpec(e, flat) for e in extents],
            scratch_shapes=[pltpu.VMEM((rows, wide), F32)],
        ),
        out_shape=[jax.ShapeDtypeStruct(e, F32) for e in extents],
        compiler_params=ROOMY,
        cost_estimate=cost(0, 10 * rows * wide),
    )(numbers, *quarters, first_w, gain.reshape(-1, 1))
    return (*grads, one.reshape(-1))


def trade(pieces):
    own, y_piece, x_piece, xy_piece = pieces
    return [own, send(y_piece, OVER_Y), send(x_piece, OVER_X), send(xy_piece, OVER_XY)]


def added(pieces):
    total = pieces[0].astype(F32)
    for piece in pieces[1:]:
        total = total + piece.astype(F32)
    return total


def sum_pieces(pieces):
    return added(trade(pieces))


def spread(part):
    return [part, send(part, OVER_Y), send(part, OVER_X), send(part, OVER_XY)]


def over_core(arrays):
    return [send(array, OVER_C) for array in arrays]


def fast_device(
    tokens_in,
    cotangent,
    seq_lengths,
    block_order,
    gain_one,
    down_q,
    gain_q,
    up_q,
    key_w,
    value_w,
    out_w,
    gain_two,
    gate_w,
    up_w,
    down_w,
):
    z = lax.axis_index("dp")
    x = lax.axis_index("ctx")
    t = lax.axis_index("tensor")
    y = t // 2
    c = t % 2
    stays = x == c
    quarter = x * 2 + y
    rows, depth = tokens_in.shape
    half = rows // 2
    part = rows // 4
    latent_width = down_q.shape[1]
    cols = up_q.shape[1] // 2
    ks = jnp.arange(4, dtype=jnp.int32)
    z_order = z ^ ks
    numbers = jnp.concatenate(
        [
            ks * 2 + c,
            ks * 2 + (1 - c),
            jnp.stack([c ^ x]),
            quarter ^ ks,
            z_order * 2 + x,
            z_order * 2 + (1 - x),
            jnp.stack([c, 1 - c, x, 1 - x, t, t ^ 1, t ^ 2, t ^ 3]),
        ]
    ).astype(jnp.int32)
    at_same, at_quarter, at_x, at_c, at_t = 8, 9, 13, 21, 25

    first_w = jnp.concatenate([down_q, key_w, value_w], axis=1)
    wide = first_w.shape[1]
    side = wide // 4
    mine = lax.dynamic_slice_in_dim(first_w, t * side, side, axis=1)
    attn_t = transpose(jnp.concatenate([up_q, out_w], axis=0), stays)
    tok_got = send(rows_at(tokens_in, t * part, part), OVER_X)
    tok_y = send(tok_got, OVER_Y)
    first_own = stage(mine, send(mine, Z_ONE), send(mine, Z_TWO), send(mine, Z_THREE))
    attn_own = gather_z(after(attn_t, *first_own))
    first_own = jnp.concatenate(first_own, axis=0)
    pair_t = transpose(after(jnp.concatenate([gate_w, up_w], axis=0), first_own), stays)
    first_blocks = [first_own] + [send(first_own, p) for p in (OVER_Y, OVER_X, OVER_XY)]

    def first_plan(n, ins, out):
        listed = []
        for i in range(8):
            col = pl.ds(pl.multiple_of(n[at_t + (0, 2, 0, 2, 1, 3, 1, 3)[i]] * side, side), side)
            for k in range(4):
                place = n[at_x + (i % 4 // 2) * 4 + k]
                row = pl.ds(pl.multiple_of(place * 256, 256), 256)
                listed.append((None, ins[i].at[k * 256 : (k + 1) * 256], out.at[row, col]))
        return listed

    pair_own = gather_z(after(pair_t, attn_own))

    def rows_plan(n, ins, out):
        listed = []
        for o in range(2):
            mine_too = (n[at_same] == o)
            for f in range(4):
                q = n[at_quarter + f]
                to = out.at[pl.ds((o * 4 + f) * part, part)]
                here = pl.ds(pl.multiple_of(q * part, part), part)
                listed.append((mine_too, ins[0].at[here], to))
                away = jnp.logical_not(mine_too)
                for j in range(4):
                    listed.append((away & (n[at_t + j] == q), ins[1 + j], to))
        return listed

    def group_rows(array, got, got_y):
        buffers = [array, got, send(got, OVER_C), got_y, send(got_y, OVER_C)]
        return place_copies(rows_plan, numbers, buffers, (2 * rows, depth), BF)

    tokens = group_rows(tokens_in, tok_got, tok_y)

    attn_rows = attn_t.shape[0]
    upq_rows = up_q.shape[0]
    out_rows = out_w.shape[0]

    def head_plan(start, count):
        def plan(n, ins, out):
            listed = []
            for i in range(8):
                row = pl.ds(pl.multiple_of(n[i] * count, count), count)
                col = pl.ds(pl.multiple_of(n[at_c] * cols, cols), cols)
                at = (i % 4) * attn_rows + start
                listed.append((None, ins[i // 4].at[at : at + count, col], out.at[row]))
            return listed

        return plan


    places = (
        block_order[0][:, :, None] * half + jnp.arange(half, dtype=jnp.int32)[None, None, :]
    ).reshape(2, 4, part)
    places = jnp.stack(
        [
            lax.dynamic_index_in_dim(
                lax.dynamic_index_in_dim(places, c ^ o, 0, False), quarter ^ f, 0, False
            )
            for o in range(2)
            for f in range(4)
        ]
    ).reshape(-1)
    second = (places >= seq_lengths[0, 0]).astype(jnp.int32)
    sequence_start = second * seq_lengths[0, 0]
    cosine, sine = angles_of((places - sequence_start).astype(F32), HD // 2)
    row_info = jnp.stack([places, sequence_start], axis=1)
    key_places = places[None, :]

    token_rows = tokens.astype(F32)
    plain_one, inverse_one = rms_parts(token_rows)
    normed = (plain_one * gain_one).astype(BF)
    *first_blocks, attn_own, normed = stage(*first_blocks, attn_own, normed)
    first_blocks = first_blocks + over_core(first_blocks)

    def first_plan(n, ins, out):
        listed = []
        for i in range(8):
            col = pl.ds(pl.multiple_of(n[at_t + (0, 2, 0, 2, 1, 3, 1, 3)[i]] * side, side), side)
            for k in range(4):
                place = n[at_x + (i % 4 // 2) * 4 + k]
                row = pl.ds(pl.multiple_of(place * 256, 256), 256)
                listed.append((None, ins[i].at[k * 256 : (k + 1) * 256], out.at[row, col]))
        return listed

    ffn_t = transpose(
        after(jnp.concatenate([gate_w, up_w, down_w], axis=0), first_own), stays
    )
    tok_y = send(tok_got, OVER_Y)
    *first_blocks, ffn_t, tok_got, tok_y = stage(*first_blocks[:4], ffn_t, tok_got, tok_y)
    ffn_own = gather_z(ffn_t)
    first_blocks = first_blocks + over_core(first_blocks)
    first_all = place_copies(first_plan, numbers, first_blocks, (depth, wide), BF)

    lat = dot(normed, first_all)
    down_t = transpose(after(down_w, first_blocks[4]), stays)
    cot_got = send(after(rows_at(cotangent, t * part, part), first_blocks[4]), OVER_X)
    cot_y = send(after(cot_got, lat), OVER_Y)
    attns = [attn_own, send(attn_own, OVER_C)]
    up_q_all = place_copies(
        head_plan(0, upq_rows), numbers, attns, (latent_width, cols), BF
    )
    out_all = place_copies(
        head_plan(upq_rows, out_rows), numbers, attns, (depth, cols), BF
    )
    latent = lat[:, :latent_width]
    plain_q, inverse_q = rms_parts(latent)
    query_in = (plain_q * gain_q).astype(BF)
    keys = turn(lat[:, latent_width : latent_width + HD], cosine, sine).astype(BF)
    values = lat[:, latent_width + HD :].astype(BF)
    query_pre = dot(query_in, up_q_all)
    query, attended, lse = attention_forward(
        query_pre, cosine, sine, keys, values, row_info, key_places
    )
    down_t, cot_got, cot_y, attended = stage(down_t, cot_got, cot_y, attended)
    cot = group_rows(cotangent, cot_got, cot_y)
    (give,) = product_pieces(attended, out_all, [], None, False)
    pieces = product_pieces(attended, out_all, [], send(give, OVER_C), True)
    *pieces, cot, pair_own = stage(*trade(pieces), cot, pair_own)
    middle = tokens[:part].astype(F32) + added(pieces)
    down_own = gather_z(after(down_t, pair_own))
    pairs = [pair_own, send(pair_own, OVER_C)]

    plain_two, inverse_two = rms_parts(middle)
    two_parts = spread((plain_two * gain_two).astype(BF))
    hidden, slope, silu = ffn_forward(numbers, two_parts, pairs)

    def two(array, other):
        return [(array, 0, rows, None), (other, 0, rows, None)]

    width = down_w.shape[1]
    (hidden_other,) = over_core([hidden])
    down_slabs = weight_grads(
        numbers, [([cot], 256, 0, [(None, two(hidden, hidden_other))])], width
    )
    two_other = over_core(two_parts)
    down_slabs, hidden, down_own, *two_other = stage(
        down_slabs, hidden, down_own, *two_other
    )
    down_sum = reduce_z(down_slabs)
    downs = [down_own, send(down_own, OVER_C)]
    grad_gate, grad_up, *pieces = ffn_backward(
        numbers, after(cot, down_slabs), slope, silu, pairs, downs
    )

    gate_other, up_other = over_core([grad_gate, grad_up])
    two_all = list(two_parts) + list(two_other)
    pair_slabs = weight_grads(
        numbers,
        [
            (two_all, 256, 0, [(None, two(grad_gate, gate_other))]),
            (two_all, 256, 0, [(None, two(grad_up, up_other))]),
        ],
        width,
    )
    *pieces, pair_slabs, hidden = stage(*trade(pieces), pair_slabs, hidden)
    grad_norm_two = added(pieces)
    pair_sum = reduce_z(after(pair_slabs, down_sum))

    grad_plain = grad_norm_two * gain_two
    grad_mid = cot[:part].astype(F32) + inverse_two * (
        grad_plain - plain_two * jnp.mean(grad_plain * plain_two, axis=-1, keepdims=True)
    )
    mid_parts = spread(grad_mid.astype(BF))
    staged = stage(*mid_parts, *ffn_output(numbers, hidden, downs))
    mid_parts, out_pieces = list(staged[:4]), staged[4:]
    mid_parts = mid_parts + over_core(mid_parts)

    def stack_plan(n, ins, out):
        return [(None, ins[i], out.at[pl.ds(i * part, part)]) for i in range(8)]

    grad_attended = product_of_parts(mid_parts, out_all)
    grad_query_pre, key_acc, value_acc = attention_backward(
        query, grad_attended, lse, cosine, sine, keys, values, row_info, key_places
    )
    down_home = transpose(down_sum, stays)
    grad_branch = place_copies(stack_plan, numbers, mid_parts, (2 * rows, depth), BF)
    attended_other = send(after(attended, mid_parts[4]), OVER_C)
    *out_sum, grad_query_pre, key_acc, value_acc, down_home, grad_branch, attended_other = stage(
        *trade(out_pieces),
        grad_query_pre,
        key_acc,
        value_acc,
        down_home,
        grad_branch,
        attended_other,
    )

    out_part = (middle + added(out_sum)).astype(BF)
    out_other = send(out_part, OVER_C)
    out_mine = jnp.where(stays, out_part, out_other)
    out_away = rows_at(jnp.where(stays, out_other, out_part), c * (part // 2), part // 2)
    extras = [key_acc, value_acc]
    (give,) = product_pieces(grad_query_pre, up_q_all, extras, None, False)
    pieces = product_pieces(grad_query_pre, up_q_all, extras, send(give, OVER_C), True)
    staged = stage(
        *pieces,
        out_mine,
        send(rows_at(out_mine, c * (part // 2), part // 2), OVER_Y),
        send(out_away, OVER_X),
        send(out_away, OVER_XY),
    )
    pieces, out_parts = staged[:4], list(staged[4:])
    query_other = send(grad_query_pre, OVER_C)

    def swapped(array):
        return [(array, rows, rows, None), (array, 0, rows, None)]

    attn_slabs = weight_grads(
        numbers,
        [
            (
                [query_in],
                upq_rows,
                0,
                [
                    (at_c, [(grad_query_pre, 0, 2 * rows, None)]),
                    (at_c + 1, swapped(query_other)),
                ],
            ),
            (
                mid_parts,
                out_rows,
                0,
                [
                    (at_c, [(attended, 0, 2 * rows, None)]),
                    (at_c + 1, swapped(attended_other)),
                ],
            ),
        ],
        2 * cols,
    )
    *pieces, attn_slabs = stage(*trade(pieces), attn_slabs)
    three = added(pieces)
    attn_sum = reduce_z(after(attn_slabs, pair_sum))

    grad_plain = three[:, :latent_width] * gain_q
    plain_q_mine = plain_q[:part]
    grad_latent = inverse_q[:part] * (
        grad_plain - plain_q_mine * jnp.mean(grad_plain * plain_q_mine, axis=-1, keepdims=True)
    )
    grad_key_pre = turn(
        three[:, latent_width : latent_width + HD], cosine[:part], -sine[:part]
    )
    lat_parts = spread(
        jnp.concatenate(
            [grad_latent, grad_key_pre, three[:, latent_width + HD :]], axis=1
        ).astype(BF)
    )
    *lat_parts, pair_sum = stage(*lat_parts, pair_sum)
    pair_home = transpose(pair_sum, stays)
    lat_parts = lat_parts + over_core(lat_parts)

    lane = wide // 4
    first_slabs = weight_grads(
        numbers,
        [([normed], 256, at_x, [(None, [(p, 0, part, at_t) for p in lat_parts])])],
        lane,
    )
    first_slabs, pair_home, *lat_parts = stage(first_slabs, pair_home, *lat_parts)
    grad_lat = place_copies(stack_plan, numbers, lat_parts, (2 * rows, wide), BF)
    grad_tokens = input_gradient(numbers, grad_lat, first_all, grad_branch, tokens, gain_one)

    out_parts = out_parts + over_core(out_parts[1:])

    def out_plan(n, ins, out):
        listed = []
        for f in range(4):
            row = n[at_quarter + f] * part
            if f == 0:
                to = out.at[pl.ds(pl.multiple_of(row, part), part)]
                listed.append((None, ins[0], to))
                continue
            for j in range(2):
                at = pl.multiple_of(row + n[at_c + j] * (part // 2), part // 2)
                listed.append((None, ins[f + 3 * j], out.at[pl.ds(at, part // 2)]))
        return listed

    result = place_copies(out_plan, numbers, out_parts, (rows, depth), BF)
    grad_down_w = down_home.astype(F32)
    pair_home = pair_home.astype(F32)
    grad_gate_w, grad_up_w = pair_home[:256], pair_home[256:]

    two_sum = jnp.sum(gate_w.astype(F32) * grad_gate_w + up_w.astype(F32) * grad_up_w, axis=1)
    *first_got, grad_tokens, result, two_sum, grad_gate_w, grad_up_w, grad_down_w = stage(
        *trade_z(first_slabs), grad_tokens, result, two_sum, grad_gate_w, grad_up_w, grad_down_w
    )
    first_quarter = added(first_got).astype(BF)
    quarters = [first_quarter] + [send(first_quarter, p) for p in (OVER_C, OVER_Y, OVER_YC)]
    attn_home = transpose(after(attn_sum, first_quarter), stays)
    *quarters, attn_home = stage(*quarters, attn_home)
    attn_home = attn_home.astype(F32)
    grad_up_q, grad_out_w = attn_home[:upq_rows], attn_home[upq_rows:]
    q_sum = jnp.sum(up_q.astype(F32) * grad_up_q, axis=1)
    small = jnp.concatenate([two_sum, q_sum]).reshape(3, -1)
    small = small + send(small, OVER_C) + send(small, OVER_Y) + send(small, OVER_YC)
    small = small.reshape(-1)
    dev = z * 2 + x
    block = depth // 8
    own_one = lax.dynamic_slice_in_dim(gain_one, dev * block, block)
    own_two = lax.dynamic_slice_in_dim(gain_two, dev * block, block)
    own_q = lax.dynamic_slice_in_dim(gain_q, dev * upq_rows, upq_rows)
    grad_down_q, grad_key_w, grad_value_w, grad_gain_one = first_finish(
        numbers, quarters, first_w, own_one, latent_width
    )
    grad_gain_two = small[:block] / own_two
    grad_gain_q = small[block:] / own_q

    return (
        result,
        grad_tokens,
        grad_gain_one,
        grad_down_q,
        grad_gain_q,
        grad_up_q,
        grad_key_w,
        grad_value_w,
        grad_out_w,
        grad_gain_two,
        grad_gate_w,
        grad_up_w,
        grad_down_w,
    )


def rows_at(array, start, count):
    return lax.dynamic_slice_in_dim(array, start, count, axis=0)


def rotate(array, places):
    half = array.shape[-1] // 2
    freqs = 10000.0 ** (-jnp.arange(half, dtype=jnp.float32) / half)
    angles = places[:, None] * freqs[None, :]
    cosine = jnp.cos(angles)
    sine = jnp.sin(angles)
    first = array[..., :half]
    latter = array[..., half:]
    return jnp.concatenate(
        [first * cosine - latter * sine, latter * cosine + first * sine], axis=-1
    )


def forward(token_rows, attention_w, ffn_w, gains, own_pos, allowed):
    gain_one, gain_q, gain_two = gains
    down_q, up_q, key_w, value_w, out_w = attention_w
    gate_w, up_w, down_w = ffn_w
    row_count = token_rows.shape[0]
    heads = up_q.shape[1] // HD
    scale = HD ** (-0.5)
    plain_one, inverse_one = rms_parts(token_rows)
    normed = (plain_one * gain_one).astype(jnp.bfloat16)
    latent = jnp.dot(normed, down_q, preferred_element_type=jnp.float32)
    plain_q, inverse_q = rms_parts(latent)
    query_in = (plain_q * gain_q).astype(jnp.bfloat16)
    query_pre = jnp.dot(query_in, up_q, preferred_element_type=jnp.float32)
    query = rotate(query_pre.reshape(row_count, heads, HD).transpose(1, 0, 2), own_pos).astype(
        jnp.bfloat16
    )
    keys = rotate(jnp.dot(normed, key_w, preferred_element_type=jnp.float32), own_pos).astype(
        jnp.bfloat16
    )
    values = jnp.dot(normed, value_w, preferred_element_type=jnp.float32).astype(jnp.bfloat16)
    keys_all, values_all = (
        lax.all_gather(keys, "ctx", axis=0, tiled=True),
        lax.all_gather(values, "ctx", axis=0, tiled=True),
    )

    def one_head(q_head):
        scores = jnp.where(allowed, times_trans(q_head, keys_all) * scale, -1e30)
        largest = jnp.max(scores, axis=-1, keepdims=True)
        exponent = jnp.exp(scores - largest)
        totals = jnp.sum(exponent, axis=-1, keepdims=True)
        soft = (exponent / totals).astype(jnp.bfloat16)
        return (
            jnp.dot(soft, values_all, preferred_element_type=jnp.float32),
            (largest + jnp.log(totals))[:, 0],
        )

    mixed_heads, log_totals = lax.map(one_head, query)
    attended = mixed_heads.transpose(1, 0, 2).reshape(row_count, heads * HD).astype(jnp.bfloat16)
    branch = lax.psum(times_trans(attended, out_w), "tensor")
    middle = token_rows + branch
    plain_two, inverse_two = rms_parts(middle)
    normed_two = (plain_two * gain_two).astype(jnp.bfloat16)
    gate_pre = jnp.dot(normed_two, gate_w, preferred_element_type=jnp.float32)
    up_pre = jnp.dot(normed_two, up_w, preferred_element_type=jnp.float32)
    hidden = (jax.nn.silu(gate_pre) * up_pre).astype(jnp.bfloat16)
    result = middle + lax.psum(times_trans(hidden, down_w).astype(jnp.bfloat16), "tensor").astype(
        jnp.float32
    )
    kept_values = (
        plain_one,
        inverse_one,
        normed,
        plain_q,
        inverse_q,
        query_in,
        query,
        keys_all,
        values_all,
        log_totals,
        attended,
        plain_two,
        inverse_two,
        normed_two,
        gate_pre,
        up_pre,
        hidden,
    )
    return (result, kept_values)


def backward(cotangent, attention_w, ffn_w, gains, own_pos, allowed, kept_values):
    gain_one, gain_q, gain_two = gains
    down_q, up_q, key_w, value_w, out_w = attention_w
    gate_w, up_w, down_w = ffn_w
    (
        plain_one,
        inverse_one,
        normed,
        plain_q,
        inverse_q,
        query_in,
        query,
        keys_all,
        values_all,
        log_totals,
        attended,
        plain_two,
        inverse_two,
        normed_two,
        gate_pre,
        up_pre,
        hidden,
    ) = kept_values
    row_count = cotangent.shape[0]
    heads = query.shape[0]
    scale = HD ** (-0.5)
    grad_down = trans_times(cotangent, hidden)
    grad_hidden = jnp.dot(cotangent, down_w, preferred_element_type=jnp.float32)
    sigma = jax.nn.sigmoid(gate_pre)
    grad_gate = (grad_hidden * up_pre * sigma * (1.0 + gate_pre * (1.0 - sigma))).astype(
        jnp.bfloat16
    )
    grad_up = (grad_hidden * gate_pre * sigma).astype(jnp.bfloat16)
    grad_gate_w = trans_times(normed_two, grad_gate)
    grad_up_w = trans_times(normed_two, grad_up)
    grad_norm_two = lax.psum(times_trans(grad_gate, gate_w) + times_trans(grad_up, up_w), "tensor")
    grad_mid_part, grad_gain_two = rms_back(grad_norm_two, plain_two, inverse_two, gain_two)
    ffn_grads = (
        lax.psum_scatter(grad_gate_w, ("dp", "ctx"), scatter_dimension=0, tiled=True),
        lax.psum_scatter(grad_up_w, ("dp", "ctx"), scatter_dimension=0, tiled=True),
        lax.psum_scatter(grad_down, ("dp", "ctx"), scatter_dimension=0, tiled=True),
        lax.psum_scatter(grad_gain_two, ("dp", "ctx"), scatter_dimension=0, tiled=True),
    )
    grad_middle = cotangent.astype(jnp.float32) + grad_mid_part
    grad_branch = grad_middle.astype(jnp.bfloat16)
    grad_out_w = trans_times(grad_branch, attended)
    grad_attended = jnp.dot(grad_branch, out_w, preferred_element_type=jnp.float32).astype(
        jnp.bfloat16
    )
    grad_heads = grad_attended.reshape(row_count, heads, HD).transpose(1, 0, 2)

    def head_back(carry, item):
        key_acc, value_acc = carry
        q_head, grad_head, lse_head = item
        scores = jnp.where(allowed, times_trans(q_head, keys_all) * scale, -1e30)
        soft = jnp.exp(scores - lse_head[:, None])
        grad_soft = times_trans(grad_head, values_all)
        inner = jnp.sum(soft * grad_soft, axis=-1, keepdims=True)
        grad_scores = (soft * (grad_soft - inner)).astype(jnp.bfloat16)
        grad_q = jnp.dot(grad_scores, keys_all, preferred_element_type=jnp.float32) * scale
        key_acc = key_acc + trans_times(grad_scores, q_head) * scale
        value_acc = value_acc + trans_times(soft.astype(jnp.bfloat16), grad_head)
        return ((key_acc, value_acc), grad_q)

    empty = jnp.zeros(keys_all.shape, jnp.float32)
    (key_total, value_total), grad_query = lax.scan(
        head_back, (empty, empty), (query, grad_heads, log_totals)
    )
    key_own, value_own = (
        lax.psum_scatter(key_total, "ctx", scatter_dimension=0, tiled=True),
        lax.psum_scatter(value_total, "ctx", scatter_dimension=0, tiled=True),
    )
    grad_query_pre = (
        rotate(grad_query, -own_pos)
        .transpose(1, 0, 2)
        .reshape(row_count, heads * HD)
        .astype(jnp.bfloat16)
    )
    grad_up_q = trans_times(query_in, grad_query_pre)
    grad_qin_part = times_trans(grad_query_pre, up_q)
    grad_qin, grad_keys_rot, grad_values = lax.psum((grad_qin_part, key_own, value_own), "tensor")
    grad_key_pre = rotate(grad_keys_rot, -own_pos).astype(jnp.bfloat16)
    grad_value_low = grad_values.astype(jnp.bfloat16)
    grad_latent, grad_gain_q = rms_back(grad_qin, plain_q, inverse_q, gain_q)
    grad_latent_low = grad_latent.astype(jnp.bfloat16)
    grad_down_q = trans_times(normed, grad_latent_low)
    grad_key_w = trans_times(normed, grad_key_pre)
    grad_value_w = trans_times(normed, grad_value_low)
    grad_norm_one = (
        times_trans(grad_latent_low, down_q)
        + times_trans(grad_key_pre, key_w)
        + times_trans(grad_value_low, value_w)
    )
    grad_in_part, grad_gain_one = rms_back(grad_norm_one, plain_one, inverse_one, gain_one)
    grad_tokens = grad_middle + grad_in_part
    attention_grads = (
        lax.psum_scatter(grad_gain_one, ("dp", "ctx"), scatter_dimension=0, tiled=True),
        lax.psum_scatter(grad_down_q, ("dp", "ctx"), scatter_dimension=0, tiled=True),
        lax.psum_scatter(grad_gain_q, ("dp", "ctx"), scatter_dimension=0, tiled=True),
        lax.psum_scatter(grad_up_q, ("dp", "ctx"), scatter_dimension=0, tiled=True),
        lax.psum_scatter(grad_key_w, ("dp", "ctx"), scatter_dimension=0, tiled=True),
        lax.psum_scatter(grad_value_w, ("dp", "ctx"), scatter_dimension=0, tiled=True),
        lax.psum_scatter(grad_out_w, ("dp", "ctx"), scatter_dimension=0, tiled=True),
    )
    return (grad_tokens, attention_grads, ffn_grads)


def per_device(
    tokens_in,
    cotangent,
    seq_lengths,
    block_order,
    gain_one,
    down_q,
    gain_q,
    up_q,
    key_w,
    value_w,
    out_w,
    gain_two,
    gate_w,
    up_w,
    down_w,
):
    token_rows = tokens_in.astype(jnp.float32)
    row_count = tokens_in.shape[0]
    block_rows = row_count // 2
    places = (
        block_order[0][:, :, None] * block_rows
        + jnp.arange(block_rows, dtype=jnp.int32)[None, None, :]
    ).reshape(-1)
    second = (places >= seq_lengths[0, 0]).astype(jnp.int32)
    in_sequence = places - second * seq_lengths[0, 0]
    start = lax.axis_index("ctx") * row_count
    own_places = lax.dynamic_slice_in_dim(places, start, row_count)
    own_second = lax.dynamic_slice_in_dim(second, start, row_count)
    own_pos = lax.dynamic_slice_in_dim(in_sequence, start, row_count).astype(jnp.float32)
    allowed = (own_second[:, None] == second[None, :]) & (places[None, :] <= own_places[:, None])
    gains = (gain_one, gain_q, gain_two)
    attention_w = (
        lax.all_gather(down_q, ("dp", "ctx"), axis=0, tiled=True),
        lax.all_gather(up_q, ("dp", "ctx"), axis=0, tiled=True),
        lax.all_gather(key_w, ("dp", "ctx"), axis=0, tiled=True),
        lax.all_gather(value_w, ("dp", "ctx"), axis=0, tiled=True),
        lax.all_gather(out_w, ("dp", "ctx"), axis=0, tiled=True),
    )
    ffn_w = (
        lax.all_gather(gate_w, ("dp", "ctx"), axis=0, tiled=True),
        lax.all_gather(up_w, ("dp", "ctx"), axis=0, tiled=True),
        lax.all_gather(down_w, ("dp", "ctx"), axis=0, tiled=True),
    )
    result, kept_values = forward(token_rows, attention_w, ffn_w, gains, own_pos, allowed)
    attention_w = (
        lax.all_gather(down_q, ("dp", "ctx"), axis=0, tiled=True),
        lax.all_gather(up_q, ("dp", "ctx"), axis=0, tiled=True),
        lax.all_gather(key_w, ("dp", "ctx"), axis=0, tiled=True),
        lax.all_gather(value_w, ("dp", "ctx"), axis=0, tiled=True),
        lax.all_gather(out_w, ("dp", "ctx"), axis=0, tiled=True),
    )
    ffn_w = (
        lax.all_gather(gate_w, ("dp", "ctx"), axis=0, tiled=True),
        lax.all_gather(up_w, ("dp", "ctx"), axis=0, tiled=True),
        lax.all_gather(down_w, ("dp", "ctx"), axis=0, tiled=True),
    )
    unused, kept_values = forward(token_rows, attention_w, ffn_w, gains, own_pos, allowed)
    grad_tokens, attention_grads, ffn_grads = backward(
        cotangent, attention_w, ffn_w, gains, own_pos, allowed, kept_values
    )
    grad_gain_one, grad_down_q, grad_gain_q, grad_up_q, grad_key_w, grad_value_w, grad_out_w = (
        attention_grads
    )
    grad_gate_w, grad_up_w, grad_down_w, grad_gain_two = ffn_grads
    return (
        result.astype(jnp.bfloat16),
        grad_tokens,
        grad_gain_one,
        grad_down_q,
        grad_gain_q,
        grad_up_q,
        grad_key_w,
        grad_value_w,
        grad_out_w,
        grad_gain_two,
        grad_gate_w,
        grad_up_w,
        grad_down_w,
    )


def solution(mesh):
    fast = dict(mesh.shape) == {"dp": 4, "ctx": 2, "tensor": 4}
    return jax.shard_map(
        fast_device if fast else per_device,
        mesh=mesh,
        in_specs=(
            P(("dp", "ctx"), None),
            P(("dp", "ctx"), None),
            P("dp", None),
            P("dp", None, None),
            P(),
            P(("dp", "ctx"), None),
            P(),
            P(("dp", "ctx"), "tensor"),
            P(("dp", "ctx"), None),
            P(("dp", "ctx"), None),
            P(("dp", "ctx"), "tensor"),
            P(),
            P(("dp", "ctx"), "tensor"),
            P(("dp", "ctx"), "tensor"),
            P(("dp", "ctx"), "tensor"),
        ),
        out_specs=(
            P(("dp", "ctx"), None),
            P(("dp", "ctx"), None),
            P(("dp", "ctx")),
            P(("dp", "ctx"), None),
            P(("dp", "ctx")),
            P(("dp", "ctx"), "tensor"),
            P(("dp", "ctx"), None),
            P(("dp", "ctx"), None),
            P(("dp", "ctx"), "tensor"),
            P(("dp", "ctx")),
            P(("dp", "ctx"), "tensor"),
            P(("dp", "ctx"), "tensor"),
            P(("dp", "ctx"), "tensor"),
        ),
        check_vma=False,
    )
```

```python
import jax
import jax.numpy as jnp
from jax import lax
from jax.experimental import pallas as pl
from jax.experimental.pallas import tpu as pltpu
from jax.sharding import PartitionSpec as P

HD = 256


EPSILON = 1e-06

AXES = ("dp", "ctx", "tensor")
BF = jnp.bfloat16
F32 = jnp.float32


def dot(left, right):
    return jnp.dot(left, right, preferred_element_type=F32)


def times_trans(left, right):
    return lax.dot_general(left, right, (((1,), (1,)), ((), ())), preferred_element_type=F32)


def trans_times(left, right):
    return lax.dot_general(left, right, (((0,), (0,)), ((), ())), preferred_element_type=F32)


def rms_parts(array):
    inverse = lax.rsqrt(jnp.mean(array * array, axis=-1, keepdims=True) + EPSILON)
    return (array * inverse, inverse)


def rms_back(grad_out, plain, inverse, gain):
    grad_plain = grad_out * gain
    grad_in = inverse * (grad_plain - plain * jnp.mean(grad_plain * plain, axis=-1, keepdims=True))
    return (grad_in, jnp.sum(grad_out * plain, axis=0))


def angles_of(places, half):
    freqs = 10000.0 ** (-jnp.arange(half, dtype=F32) / half)
    angles = places[:, None] * freqs[None, :]
    return (jnp.cos(angles), jnp.sin(angles))


def turn(array, cosine, sine):
    half = array.shape[-1] // 2
    first = array[..., :half]
    latter = array[..., half:]
    return jnp.concatenate(
        [first * cosine - latter * sine, latter * cosine + first * sine], axis=-1
    )


def routes(move):
    pairs = []
    for z in range(4):
        for x in range(2):
            for y in range(2):
                for c in range(2):
                    to = move(z, x, y, c)
                    if to is not None:
                        tz, tx, ty, tc = to
                        pairs.append(
                            (((z * 2 + x) * 2 + y) * 2 + c, ((tz * 2 + tx) * 2 + ty) * 2 + tc)
                        )
    return pairs


OVER_X = routes(lambda z, x, y, c: (z, 1 - x, y, c))
OVER_Y = routes(lambda z, x, y, c: (z, x, 1 - y, c))
OVER_XY = routes(lambda z, x, y, c: (z, 1 - x, 1 - y, c))
OVER_YC = routes(lambda z, x, y, c: (z, x, 1 - y, 1 - c))
OVER_C = routes(lambda z, x, y, c: (z, x, y, 1 - c))
TRANSPOSE = routes(lambda z, x, y, c: (z, c, y, x) if x != c else None)
Z_ONE = routes(lambda z, x, y, c: (z ^ 1, x, y, c))
Z_TWO = routes(lambda z, x, y, c: (z ^ 2, x, y, c))
Z_THREE = routes(lambda z, x, y, c: (z ^ 3, x, y, c))


def send(array, pairs):
    return lax.ppermute(array, AXES, pairs)


def transpose(array, stays):
    return jnp.where(stays, array, send(array, TRANSPOSE))


def after(array, *others):
    return lax.optimization_barrier((array, *others))[0]


def stage(*arrays):
    return lax.optimization_barrier(arrays)


def gather_z(array):
    return lax.all_gather(array, "dp", axis=0, tiled=True)


def reduce_z(slabs):
    return lax.psum_scatter(slabs, "dp", scatter_dimension=0, tiled=True)


def trade_z(slabs):
    n = slabs.shape[0] // 4
    return [slabs[:n]] + [
        send(slabs[k * n : (k + 1) * n], pairs)
        for k, pairs in ((1, Z_ONE), (2, Z_TWO), (3, Z_THREE))
    ]


WHOLE = pl.BlockSpec(memory_space=pltpu.VMEM)
HELD = pl.BlockSpec(memory_space=pl.ANY)
ROOMY = pltpu.CompilerParams(vmem_limit_bytes=56 * 1024 * 1024)


def cost(macs, moved, share=1):
    return pl.CostEstimate(
        flops=2 * macs // share // 1, bytes_accessed=moved // share // 1, transcendentals=0
    )


def place_copies(plan, numbers, buffers, shape, dtype):
    def body(numbers_ref, *refs):
        ins, out_ref, sem = refs[:-2], refs[-2], refs[-1]
        listed = plan(numbers_ref, ins, out_ref)
        for i, (condition, source, target) in enumerate(listed):
            copy = pltpu.make_async_copy(source, target, sem.at[i])
            if condition is None:
                copy.start()
            else:
                pl.when(condition)(copy.start)
        for i, (condition, source, target) in enumerate(listed):
            copy = pltpu.make_async_copy(source, target, sem.at[i])
            if condition is None:
                copy.wait()
            else:
                pl.when(condition)(copy.wait)

    moved = 2
    for extent in shape:
        moved *= extent
    return pl.pallas_call(
        body,
        grid_spec=pltpu.PrefetchScalarGridSpec(
            num_scalar_prefetch=1,
            grid=(1,),
            in_specs=[HELD] * len(buffers),
            out_specs=pl.BlockSpec(shape, lambda i, numbers_ref: (0, 0)),
            scratch_shapes=[pltpu.SemaphoreType.DMA((40,))],
        ),
        out_shape=jax.ShapeDtypeStruct(shape, dtype),
        compiler_params=ROOMY,
        cost_estimate=cost(0, 2 * moved),
    )(numbers, *buffers)


def attention_forward(query_pre, cosine, sine, keys, values, row_info, key_places):
    rows, width = query_pre.shape
    heads = width // HD
    chunk = 256
    half = HD // 2
    scale = HD ** (-0.5)

    def body(pre_ref, cos_ref, sin_ref, k_ref, v_ref, info_ref, place_ref, q_ref, o_ref, lse_ref):
        for i in range(rows // chunk):
            at = slice(i * chunk, (i + 1) * chunk)
            first, latter = pre_ref[at, :half], pre_ref[at, half:]
            co, si = cos_ref[at], sin_ref[at]
            q = jnp.concatenate([first * co - latter * si, latter * co + first * si], 1).astype(BF)
            q_ref[at] = q
            scores = times_trans(q, k_ref[...]) * scale
            allowed = (place_ref[...] <= info_ref[at, 0:1]) & (place_ref[...] >= info_ref[at, 1:2])
            scores = jnp.where(allowed, scores, -1e30)
            largest = jnp.max(scores, axis=-1, keepdims=True)
            exponent = jnp.exp(scores - largest)
            totals = jnp.sum(exponent, axis=-1, keepdims=True)
            soft = (exponent * (1.0 / totals)).astype(BF)
            o_ref[at] = dot(soft, v_ref[...]).astype(BF)
            lse_ref[0, at] = largest + jnp.log(totals)

    full = lambda h: (0, 0)
    by_head = lambda h: (0, h)
    return pl.pallas_call(
        body,
        grid=(heads,),
        in_specs=[
            pl.BlockSpec((rows, HD), by_head),
            pl.BlockSpec((rows, half), full),
            pl.BlockSpec((rows, half), full),
            pl.BlockSpec((rows, HD), full),
            pl.BlockSpec((rows, HD), full),
            pl.BlockSpec((rows, 2), full),
            pl.BlockSpec((1, rows), full),
        ],
        out_specs=[
            pl.BlockSpec((rows, HD), by_head),
            pl.BlockSpec((rows, HD), by_head),
            pl.BlockSpec((1, rows, 1), lambda h: (h, 0, 0)),
        ],
        out_shape=[
            jax.ShapeDtypeStruct((rows, width), BF),
            jax.ShapeDtypeStruct((rows, width), BF),
            jax.ShapeDtypeStruct((heads, rows, 1), F32),
        ],
        compiler_params=ROOMY,
        cost_estimate=cost(4 * rows * rows * width, 6 * rows * width),
    )(query_pre, cosine, sine, keys, values, row_info, key_places)


def attention_backward(query, grad_out, lse, cosine, sine, keys, values, row_info, key_places):
    rows, width = query.shape
    heads = width // HD
    chunk = 256
    half = HD // 2
    scale = HD ** (-0.5)

    def body(
        q_ref, do_ref, lse_ref, cos_ref, sin_ref, k_ref, v_ref, info_ref, place_ref, dq_ref, dk_ref, dv_ref
    ):
        @pl.when(pl.program_id(0) == 0)
        def clear():
            dk_ref[...] = jnp.zeros_like(dk_ref)
            dv_ref[...] = jnp.zeros_like(dv_ref)

        for i in range(rows // chunk):
            at = slice(i * chunk, (i + 1) * chunk)
            q, do = q_ref[at], do_ref[at]
            scores = times_trans(q, k_ref[...]) * scale
            allowed = (place_ref[...] <= info_ref[at, 0:1]) & (place_ref[...] >= info_ref[at, 1:2])
            soft = jnp.exp(jnp.where(allowed, scores, -1e30) - lse_ref[0, at])
            grad_soft = times_trans(do, v_ref[...])
            summed = jnp.sum(soft * grad_soft, axis=-1, keepdims=True)
            grad_scores = (soft * (grad_soft - summed)).astype(BF)
            dq = dot(grad_scores, k_ref[...]) * scale
            first, latter = dq[:, :half], dq[:, half:]
            co, si = cos_ref[at], sin_ref[at]
            dq_ref[at] = jnp.concatenate(
                [first * co + latter * si, latter * co - first * si], 1
            ).astype(BF)
            dk_ref[...] += trans_times(grad_scores, q) * scale
            dv_ref[...] += trans_times(soft.astype(BF), do)

    full = lambda h: (0, 0)
    by_head = lambda h: (0, h)
    return pl.pallas_call(
        body,
        grid=(heads,),
        in_specs=[
            pl.BlockSpec((rows, HD), by_head),
            pl.BlockSpec((rows, HD), by_head),
            pl.BlockSpec((1, rows, 1), lambda h: (h, 0, 0)),
            pl.BlockSpec((rows, half), full),
            pl.BlockSpec((rows, half), full),
            pl.BlockSpec((rows, HD), full),
            pl.BlockSpec((rows, HD), full),
            pl.BlockSpec((rows, 2), full),
            pl.BlockSpec((1, rows), full),
        ],
        out_specs=[
            pl.BlockSpec((rows, HD), by_head),
            pl.BlockSpec((rows, HD), full),
            pl.BlockSpec((rows, HD), full),
        ],
        out_shape=[
            jax.ShapeDtypeStruct((rows, width), BF),
            jax.ShapeDtypeStruct((rows, HD), F32),
            jax.ShapeDtypeStruct((rows, HD), F32),
        ],
        compiler_params=ROOMY,
        cost_estimate=cost(8 * rows * rows * width, 6 * rows * width),
    )(query, grad_out, lse, cosine, sine, keys, values, row_info, key_places)


def product_of_parts(parts, weight):
    rows = parts[0].shape[0]
    count = len(parts)
    width = weight.shape[1]

    def body(*refs):
        weight_ref, out_ref = refs[count:]
        for i in range(0, count, 4):
            left = jnp.concatenate([refs[j][...] for j in range(i, i + 4)], axis=0)
            out_ref[i * rows : (i + 4) * rows] = dot(left, weight_ref[...]).astype(BF)

    return pl.pallas_call(
        body,
        in_specs=[WHOLE] * (count + 1),
        out_specs=WHOLE,
        out_shape=jax.ShapeDtypeStruct((count * rows, width), BF),
        compiler_params=ROOMY,
        cost_estimate=cost(count * rows * weight.size, 2 * weight.size),
    )(*parts, weight)


def product_pieces(left, weight, extras, got, first_half):
    rows = left.shape[0] // 2
    part = rows // 4
    start = 0 if first_half else rows
    wide = weight.shape[0]
    total = wide + sum(e.shape[1] for e in extras)
    outs = 4 if first_half else 1

    def body(left_ref, weight_ref, *refs):
        extra_refs = refs[: len(extras)]
        got_ref = refs[len(extras)] if got is not None else None
        out_refs = refs[len(refs) - outs :]
        src = slice(start, start + rows)

        def put(value, cols):
            if got_ref is not None:
                value = value + got_ref[:, cols].astype(F32)
            value = value.astype(BF)
            if outs == 1:
                out_refs[0][:, cols] = value
            else:
                for f in range(4):
                    out_refs[f][:, cols] = value[f * part : (f + 1) * part]

        step = 512
        for col in range(0, wide, step):
            put(times_trans(left_ref[src], weight_ref[col : col + step]), slice(col, col + step))
        col = wide
        for extra_ref in extra_refs:
            n = extra_ref.shape[1]
            put(extra_ref[src], slice(col, col + n))
            col += n

    shapes = [jax.ShapeDtypeStruct((part, total), BF)] * 4
    if outs == 1:
        shapes = [jax.ShapeDtypeStruct((rows, total), BF)]
    arrays = [left, weight, *extras] + ([got] if got is not None else [])
    return pl.pallas_call(
        body,
        in_specs=[WHOLE] * len(arrays),
        out_specs=[WHOLE] * outs,
        out_shape=shapes,
        compiler_params=ROOMY,
        cost_estimate=cost(rows * wide * left.shape[1], 2 * weight.size + 4 * rows * total),
    )(*arrays)


def tiles_of(width):
    whole = width // 256
    return whole, width - whole * 256


def ffn_forward(numbers, parts, pairs):
    part, depth = parts[0].shape
    rows = part * len(parts)
    width = pairs[0].shape[1]
    whole, rest = tiles_of(width)

    def body(numbers_ref, *refs):
        part_refs, pair_refs = refs[:4], refs[4:6]
        hid_ref, slope_ref, silu_ref, gate_vm, up_vm, in_vm, sem = refs[6:]
        gate_copies, up_copies = [], []
        for i in range(8):
            to = pl.ds(pl.multiple_of(numbers_ref[i] * 256, 256), 256)
            ref, at = pair_refs[i // 4], (i % 4) * 512
            gate_copies.append(
                pltpu.make_async_copy(ref.at[at : at + 256], gate_vm.at[to], sem.at[i])
            )
            up_copies.append(
                pltpu.make_async_copy(ref.at[at + 256 : at + 512], up_vm.at[to], sem.at[8 + i])
            )
        for copy in gate_copies + up_copies:
            copy.start()
        for f in range(4):
            in_vm[f * part : (f + 1) * part] = part_refs[f][...]
        for copy in gate_copies + up_copies:
            copy.wait()

        def tile(cols):
            gate = dot(in_vm[...], gate_vm[:, cols])
            up = dot(in_vm[...], up_vm[:, cols])
            sigma = jax.nn.sigmoid(gate)
            silu = gate * sigma
            hid_ref[:, cols] = (silu * up).astype(BF)
            slope_ref[:, cols] = up * sigma * (1.0 + gate * (1.0 - sigma))
            silu_ref[:, cols] = silu

        @pl.loop(0, whole)
        def each(i):
            tile(pl.ds(pl.multiple_of(i * 256, 256), 256))

        if rest:
            tile(slice(whole * 256, width))

    return pl.pallas_call(
        body,
        grid_spec=pltpu.PrefetchScalarGridSpec(
            num_scalar_prefetch=1,
            grid=(1,),
            in_specs=[pl.BlockSpec((part, depth), lambda i, n: (0, 0))] * 4 + [HELD] * 2,
            out_specs=[pl.BlockSpec((rows, width), lambda i, n: (0, 0))] * 3,
            scratch_shapes=[
                pltpu.VMEM((depth, width), BF),
                pltpu.VMEM((depth, width), BF),
                pltpu.VMEM((rows, depth), BF),
                pltpu.SemaphoreType.DMA((16,)),
            ],
        ),
        out_shape=[
            jax.ShapeDtypeStruct((rows, width), BF),
            jax.ShapeDtypeStruct((rows, width), F32),
            jax.ShapeDtypeStruct((rows, width), F32),
        ],
        compiler_params=ROOMY,
        cost_estimate=cost(2 * rows * depth * width, 4 * depth * width),
    )(numbers, *parts, *pairs)


def ffn_backward(numbers, cot, slope, silu, pairs, downs):
    rows = slope.shape[0]
    depth = cot.shape[1]
    part = rows // 4
    width = slope.shape[1]
    whole, rest = tiles_of(width)

    def body(numbers_ref, *refs):
        cot_ref, slope_ref, silu_ref = refs[:3]
        pair_refs, down_refs = refs[3:5], refs[5:7]
        gate_out, up_out = refs[7:9]
        piece_refs = refs[9:13]
        down_vm, pair_vm, sem = refs[13:]
        copies, later = [], []
        for i in range(8):
            to = pl.ds(pl.multiple_of(numbers_ref[i] * 256, 256), 256)
            ref, at = down_refs[i // 4], (i % 4) * 256
            copies.append(
                pltpu.make_async_copy(ref.at[at : at + 256], down_vm.at[to], sem.at[i])
            )
            ref, at = pair_refs[i // 4], (i % 4) * 512
            later.append(
                pltpu.make_async_copy(ref.at[at : at + 512], pair_vm.at[i], sem.at[8 + i])
            )
        for copy in copies + later:
            copy.start()
        for copy in copies:
            copy.wait()

        def tile(cols):
            grad = dot(cot_ref[...], down_vm[:, cols])
            gate_out[:, cols] = (grad * slope_ref[:, cols]).astype(BF)
            up_out[:, cols] = (grad * silu_ref[:, cols]).astype(BF)

        @pl.loop(0, whole)
        def each(i):
            tile(pl.ds(pl.multiple_of(i * 256, 256), 256))

        if rest:
            tile(slice(whole * 256, width))
        for copy in later:
            copy.wait()

        @pl.loop(0, 8)
        def block(i):
            cols = pl.ds(pl.multiple_of(numbers_ref[i] * 256, 256), 256)
            value = times_trans(gate_out[...], pair_vm[i, :256]) + times_trans(
                up_out[...], pair_vm[i, 256:]
            )
            value = value.astype(BF)
            for f in range(4):
                piece_refs[f][:, cols] = value[f * part : (f + 1) * part]

    flat = lambda i, n: (0, 0)
    return pl.pallas_call(
        body,
        grid_spec=pltpu.PrefetchScalarGridSpec(
            num_scalar_prefetch=1,
            grid=(1,),
            in_specs=[
                pl.BlockSpec((rows, depth), flat),
                pl.BlockSpec((rows, width), flat),
                pl.BlockSpec((rows, width), flat),
            ]
            + [HELD] * 4,
            out_specs=[pl.BlockSpec((rows, width), flat)] * 2
            + [pl.BlockSpec((part, depth), flat)] * 4,
            scratch_shapes=[
                pltpu.VMEM((depth, width), BF),
                pltpu.VMEM((8, 512, width), BF),
                pltpu.SemaphoreType.DMA((16,)),
            ],
        ),
        out_shape=[jax.ShapeDtypeStruct((rows, width), BF)] * 2
        + [jax.ShapeDtypeStruct((part, depth), BF)] * 4,
        compiler_params=ROOMY,
        cost_estimate=cost(3 * rows * depth * width, 6 * depth * width),
    )(numbers, cot, slope, silu, *pairs, *downs)


def ffn_output(numbers, hidden, downs):
    rows, width = hidden.shape
    part = rows // 4
    depth = 2 * downs[0].shape[0]

    def body(numbers_ref, hid_ref, *refs):
        down_refs, piece_refs = refs[:2], refs[2:6]
        down_vm, sem = refs[6:]
        copies = [
            pltpu.make_async_copy(
                down_refs[i // 4].at[(i % 4) * 256 : (i % 4 + 1) * 256], down_vm.at[i], sem.at[i]
            )
            for i in range(8)
        ]
        for copy in copies:
            copy.start()
        for copy in copies:
            copy.wait()

        @pl.loop(0, 8)
        def block(i):
            cols = pl.ds(pl.multiple_of(numbers_ref[i] * 256, 256), 256)
            value = times_trans(hid_ref[...], down_vm[i]).astype(BF)
            for f in range(4):
                piece_refs[f][:, cols] = value[f * part : (f + 1) * part]

    flat = lambda i, n: (0, 0)
    return pl.pallas_call(
        body,
        grid_spec=pltpu.PrefetchScalarGridSpec(
            num_scalar_prefetch=1,
            grid=(1,),
            in_specs=[pl.BlockSpec((rows, width), flat)] + [HELD] * 2,
            out_specs=[pl.BlockSpec((part, depth), flat)] * 4,
            scratch_shapes=[
                pltpu.VMEM((8, 256, width), BF),
                pltpu.SemaphoreType.DMA((8,)),
            ],
        ),
        out_shape=[jax.ShapeDtypeStruct((part, depth), BF)] * 4,
        compiler_params=ROOMY,
        cost_estimate=cost(rows * depth * width, 2 * depth * width, 4),
    )(numbers, hidden, *downs)


def weight_grads(numbers, terms, width):
    lefts, rights, left_specs, right_specs = [], [], [], []
    shape_of = []
    for left, block, offset, products in terms:
        for array in left:
            lefts.append(array)
            left_specs.append(
                pl.BlockSpec((array.shape[0], block), lambda i, n, offset=offset: (0, n[offset + i]))
            )
        for place, right in products:
            for array, start, count, pick in right:
                rights.append(array)
                if pick is None:
                    right_specs.append(pl.BlockSpec(array.shape, lambda i, n: (0, 0)))
                else:
                    right_specs.append(
                        pl.BlockSpec((array.shape[0], width), lambda i, n, pick=pick: (0, n[pick]))
                    )
        shape_of.append(block)
    height = sum(shape_of)

    def body(numbers_ref, *refs):
        left_refs = refs[: len(lefts)]
        right_refs = refs[len(lefts) : len(lefts) + len(rights)]
        out_ref = refs[-1]
        li, ri, row = 0, 0, 0
        for left, block, offset, products in terms:
            pieces = [left_refs[li + j][...] for j in range(len(left))]
            li += len(left)
            whole = pieces[0] if len(pieces) == 1 else jnp.concatenate(pieces, axis=0)
            for place, right in products:
                value = None
                at = 0
                for array, start, count, pick in right:
                    this = trans_times(
                        whole[at : at + count], right_refs[ri][start : start + count]
                    )
                    value = this if value is None else value + this
                    at += count
                    ri += 1
                value = value.astype(BF)
                n = value.shape[1]
                if place is None:
                    cols = slice(0, n)
                else:
                    cols = pl.ds(pl.multiple_of(numbers_ref[place] * n, n), n)
                out_ref[row : row + block, cols] = value

            row += block

    macs = 4 * height * width * 1024
    return pl.pallas_call(
        body,
        grid_spec=pltpu.PrefetchScalarGridSpec(
            num_scalar_prefetch=1,
            grid=(4,),
            in_specs=left_specs + right_specs,
            out_specs=pl.BlockSpec((height, width), lambda i, n: (i, 0)),
        ),
        out_shape=jax.ShapeDtypeStruct((4 * height, width), BF),
        compiler_params=ROOMY,
        cost_estimate=cost(macs, 4 * height * width * 4, 4),
    )(numbers, *lefts, *rights)


def input_gradient(numbers, grad_lat, first_all, grad_mid, tokens, gain):
    depth = tokens.shape[1]
    wide = grad_lat.shape[1]
    part = 128

    def body(numbers_ref, lat_ref, first_ref, mid_ref, tok_ref, gain_ref, out_ref, grad_vm):
        for col in range(0, depth, 512):
            cols = slice(col, col + 512)
            grad_vm[:, cols] = times_trans(lat_ref[...], first_ref[cols]) * gain_ref[:, cols]
        for i in range(4):
            at = slice(i * part, (i + 1) * part)
            plain = tok_ref[at].astype(F32)
            inverse = lax.rsqrt(jnp.mean(plain * plain, axis=-1, keepdims=True) + EPSILON)
            plain = plain * inverse
            grad = grad_vm[at]
            mean = jnp.mean(grad * plain, axis=-1, keepdims=True)
            to = pl.ds(pl.multiple_of(numbers_ref[9 + i] * part, part), part)
            out_ref[to] = mid_ref[at].astype(F32) + inverse * (grad - plain * mean)

    picked = lambda i, n: (n[8], 0)
    flat = lambda i, n: (0, 0)
    return pl.pallas_call(
        body,
        grid_spec=pltpu.PrefetchScalarGridSpec(
            num_scalar_prefetch=1,
            grid=(1,),
            in_specs=[
                pl.BlockSpec((4 * part, wide), picked),
                pl.BlockSpec((depth, wide), flat),
                pl.BlockSpec((4 * part, depth), picked),
                pl.BlockSpec((4 * part, depth), picked),
                pl.BlockSpec((1, depth), flat),
            ],
            out_specs=pl.BlockSpec((4 * part, depth), flat),
            scratch_shapes=[pltpu.VMEM((4 * part, depth), F32)],
        ),
        out_shape=jax.ShapeDtypeStruct((4 * part, depth), F32),
        compiler_params=ROOMY,
        cost_estimate=cost(4 * part * depth * wide, 2 * depth * wide + 8 * part * depth * 4),
    )(numbers, grad_lat, first_all, grad_mid, tokens, gain.reshape(1, -1))


def first_finish(numbers, quarters, first_w, gain, latent_width):
    rows, lane = quarters[0].shape
    wide = first_w.shape[1]

    def body(numbers_ref, *refs):
        weight_ref, gain_ref, down_ref, key_ref, value_ref, one_ref, all_vm = refs[4:]
        for i in range(4):
            cols = pl.ds(pl.multiple_of(numbers_ref[25 + i] * lane, lane), lane)
            all_vm[:, cols] = refs[i][...].astype(F32)
        down_ref[...] = all_vm[:, :latent_width]
        key_ref[...] = all_vm[:, latent_width : latent_width + HD]
        value_ref[...] = all_vm[:, latent_width + HD :]
        total = jnp.sum(weight_ref[...].astype(F32) * all_vm[...], axis=1, keepdims=True)
        one_ref[...] = total / gain_ref[...]

    flat = lambda i, n: (0, 0)
    extents = [(rows, latent_width), (rows, HD), (rows, wide - latent_width - HD), (rows, 1)]
    *grads, one = pl.pallas_call(
        body,
        grid_spec=pltpu.PrefetchScalarGridSpec(
            num_scalar_prefetch=1,
            grid=(1,),
            in_specs=[pl.BlockSpec((rows, lane), flat)] * 4
            + [pl.BlockSpec((rows, wide), flat), pl.BlockSpec((rows, 1), flat)],
            out_specs=[pl.BlockSpec(e, flat) for e in extents],
            scratch_shapes=[pltpu.VMEM((rows, wide), F32)],
        ),
        out_shape=[jax.ShapeDtypeStruct(e, F32) for e in extents],
        compiler_params=ROOMY,
        cost_estimate=cost(0, 10 * rows * wide),
    )(numbers, *quarters, first_w, gain.reshape(-1, 1))
    return (*grads, one.reshape(-1))


def trade(pieces):
    own, y_piece, x_piece, xy_piece = pieces
    return [own, send(y_piece, OVER_Y), send(x_piece, OVER_X), send(xy_piece, OVER_XY)]


def added(pieces):
    total = pieces[0].astype(F32)
    for piece in pieces[1:]:
        total = total + piece.astype(F32)
    return total


def sum_pieces(pieces):
    return added(trade(pieces))


def spread(part):
    return [part, send(part, OVER_Y), send(part, OVER_X), send(part, OVER_XY)]


def over_core(arrays):
    return [send(array, OVER_C) for array in arrays]


def fast_device(
    tokens_in,
    cotangent,
    seq_lengths,
    block_order,
    gain_one,
    down_q,
    gain_q,
    up_q,
    key_w,
    value_w,
    out_w,
    gain_two,
    gate_w,
    up_w,
    down_w,
):
    z = lax.axis_index("dp")
    x = lax.axis_index("ctx")
    t = lax.axis_index("tensor")
    y = t // 2
    c = t % 2
    stays = x == c
    quarter = x * 2 + y
    rows, depth = tokens_in.shape
    half = rows // 2
    part = rows // 4
    latent_width = down_q.shape[1]
    cols = up_q.shape[1] // 2
    ks = jnp.arange(4, dtype=jnp.int32)
    z_order = z ^ ks
    numbers = jnp.concatenate(
        [
            ks * 2 + c,
            ks * 2 + (1 - c),
            jnp.stack([c ^ x]),
            quarter ^ ks,
            z_order * 2 + x,
            z_order * 2 + (1 - x),
            jnp.stack([c, 1 - c, x, 1 - x, t, t ^ 1, t ^ 2, t ^ 3]),
        ]
    ).astype(jnp.int32)
    at_same, at_quarter, at_x, at_c, at_t = 8, 9, 13, 21, 25

    first_w = jnp.concatenate([down_q, key_w, value_w], axis=1)
    wide = first_w.shape[1]
    side = wide // 4
    mine = lax.dynamic_slice_in_dim(first_w, t * side, side, axis=1)
    attn_t = transpose(jnp.concatenate([up_q, out_w], axis=0), stays)
    tok_got = send(rows_at(tokens_in, t * part, part), OVER_X)
    tok_y = send(tok_got, OVER_Y)
    first_own = stage(mine, send(mine, Z_ONE), send(mine, Z_TWO), send(mine, Z_THREE))
    attn_own = gather_z(after(attn_t, *first_own))
    first_own = jnp.concatenate(first_own, axis=0)
    pair_t = transpose(after(jnp.concatenate([gate_w, up_w], axis=0), first_own), stays)
    first_blocks = [first_own] + [send(first_own, p) for p in (OVER_Y, OVER_X, OVER_XY)]

    def first_plan(n, ins, out):
        listed = []
        for i in range(8):
            col = pl.ds(pl.multiple_of(n[at_t + (0, 2, 0, 2, 1, 3, 1, 3)[i]] * side, side), side)
            for k in range(4):
                place = n[at_x + (i % 4 // 2) * 4 + k]
                row = pl.ds(pl.multiple_of(place * 256, 256), 256)
                listed.append((None, ins[i].at[k * 256 : (k + 1) * 256], out.at[row, col]))
        return listed

    pair_own = gather_z(after(pair_t, attn_own))

    def rows_plan(n, ins, out):
        listed = []
        for o in range(2):
            mine_too = (n[at_same] == o)
            for f in range(4):
                q = n[at_quarter + f]
                to = out.at[pl.ds((o * 4 + f) * part, part)]
                here = pl.ds(pl.multiple_of(q * part, part), part)
                listed.append((mine_too, ins[0].at[here], to))
                away = jnp.logical_not(mine_too)
                for j in range(4):
                    listed.append((away & (n[at_t + j] == q), ins[1 + j], to))
        return listed

    def group_rows(array, got, got_y):
        buffers = [array, got, send(got, OVER_C), got_y, send(got_y, OVER_C)]
        return place_copies(rows_plan, numbers, buffers, (2 * rows, depth), BF)

    tokens = group_rows(tokens_in, tok_got, tok_y)

    attn_rows = attn_t.shape[0]
    upq_rows = up_q.shape[0]
    out_rows = out_w.shape[0]

    def head_plan(start, count):
        def plan(n, ins, out):
            listed = []
            for i in range(8):
                row = pl.ds(pl.multiple_of(n[i] * count, count), count)
                col = pl.ds(pl.multiple_of(n[at_c] * cols, cols), cols)
                at = (i % 4) * attn_rows + start
                listed.append((None, ins[i // 4].at[at : at + count, col], out.at[row]))
            return listed

        return plan


    places = (
        block_order[0][:, :, None] * half + jnp.arange(half, dtype=jnp.int32)[None, None, :]
    ).reshape(2, 4, part)
    places = jnp.stack(
        [
            lax.dynamic_index_in_dim(
                lax.dynamic_index_in_dim(places, c ^ o, 0, False), quarter ^ f, 0, False
            )
            for o in range(2)
            for f in range(4)
        ]
    ).reshape(-1)
    second = (places >= seq_lengths[0, 0]).astype(jnp.int32)
    sequence_start = second * seq_lengths[0, 0]
    cosine, sine = angles_of((places - sequence_start).astype(F32), HD // 2)
    row_info = jnp.stack([places, sequence_start], axis=1)
    key_places = places[None, :]

    token_rows = tokens.astype(F32)
    plain_one, inverse_one = rms_parts(token_rows)
    normed = (plain_one * gain_one).astype(BF)
    *first_blocks, attn_own, normed = stage(*first_blocks, attn_own, normed)
    first_blocks = first_blocks + over_core(first_blocks)

    def first_plan(n, ins, out):
        listed = []
        for i in range(8):
            col = pl.ds(pl.multiple_of(n[at_t + (0, 2, 0, 2, 1, 3, 1, 3)[i]] * side, side), side)
            for k in range(4):
                place = n[at_x + (i % 4 // 2) * 4 + k]
                row = pl.ds(pl.multiple_of(place * 256, 256), 256)
                listed.append((None, ins[i].at[k * 256 : (k + 1) * 256], out.at[row, col]))
        return listed

    ffn_t = transpose(
        after(jnp.concatenate([gate_w, up_w, down_w], axis=0), first_own), stays
    )
    tok_y = send(tok_got, OVER_Y)
    *first_blocks, ffn_t, tok_got, tok_y = stage(*first_blocks[:4], ffn_t, tok_got, tok_y)
    ffn_own = gather_z(ffn_t)
    first_blocks = first_blocks + over_core(first_blocks)
    first_all = place_copies(first_plan, numbers, first_blocks, (depth, wide), BF)

    lat = dot(normed, first_all)
    down_t = transpose(after(down_w, first_blocks[4]), stays)
    cot_got = send(after(rows_at(cotangent, t * part, part), first_blocks[4]), OVER_X)
    cot_y = send(after(cot_got, lat), OVER_Y)
    attns = [attn_own, send(attn_own, OVER_C)]
    up_q_all = place_copies(
        head_plan(0, upq_rows), numbers, attns, (latent_width, cols), BF
    )
    out_all = place_copies(
        head_plan(upq_rows, out_rows), numbers, attns, (depth, cols), BF
    )
    latent = lat[:, :latent_width]
    plain_q, inverse_q = rms_parts(latent)
    query_in = (plain_q * gain_q).astype(BF)
    keys = turn(lat[:, latent_width : latent_width + HD], cosine, sine).astype(BF)
    values = lat[:, latent_width + HD :].astype(BF)
    query_pre = dot(query_in, up_q_all)
    query, attended, lse = attention_forward(
        query_pre, cosine, sine, keys, values, row_info, key_places
    )
    down_t, cot_got, cot_y, attended = stage(down_t, cot_got, cot_y, attended)
    cot = group_rows(cotangent, cot_got, cot_y)
    (give,) = product_pieces(attended, out_all, [], None, False)
    pieces = product_pieces(attended, out_all, [], send(give, OVER_C), True)
    *pieces, cot, pair_own = stage(*trade(pieces), cot, pair_own)
    middle = tokens[:part].astype(F32) + added(pieces)
    down_own = gather_z(after(down_t, pair_own))
    pairs = [pair_own, send(pair_own, OVER_C)]

    plain_two, inverse_two = rms_parts(middle)
    two_parts = spread((plain_two * gain_two).astype(BF))
    hidden, slope, silu = ffn_forward(numbers, two_parts, pairs)

    def two(array, other):
        return [(array, 0, rows, None), (other, 0, rows, None)]

    width = down_w.shape[1]
    (hidden_other,) = over_core([hidden])
    down_slabs = weight_grads(
        numbers, [([cot], 256, 0, [(None, two(hidden, hidden_other))])], width
    )
    two_other = over_core(two_parts)
    down_slabs, hidden, down_own, *two_other = stage(
        down_slabs, hidden, down_own, *two_other
    )
    down_sum = reduce_z(down_slabs)
    downs = [down_own, send(down_own, OVER_C)]
    grad_gate, grad_up, *pieces = ffn_backward(
        numbers, after(cot, down_slabs), slope, silu, pairs, downs
    )

    gate_other, up_other = over_core([grad_gate, grad_up])
    two_all = list(two_parts) + list(two_other)
    pair_slabs = weight_grads(
        numbers,
        [
            (two_all, 256, 0, [(None, two(grad_gate, gate_other))]),
            (two_all, 256, 0, [(None, two(grad_up, up_other))]),
        ],
        width,
    )
    *pieces, pair_slabs, hidden = stage(*trade(pieces), pair_slabs, hidden)
    grad_norm_two = added(pieces)
    pair_sum = reduce_z(after(pair_slabs, down_sum))

    grad_plain = grad_norm_two * gain_two
    grad_mid = cot[:part].astype(F32) + inverse_two * (
        grad_plain - plain_two * jnp.mean(grad_plain * plain_two, axis=-1, keepdims=True)
    )
    mid_parts = spread(grad_mid.astype(BF))
    staged = stage(*mid_parts, *ffn_output(numbers, hidden, downs))
    mid_parts, out_pieces = list(staged[:4]), staged[4:]
    mid_parts = mid_parts + over_core(mid_parts)

    def stack_plan(n, ins, out):
        return [(None, ins[i], out.at[pl.ds(i * part, part)]) for i in range(8)]

    grad_attended = product_of_parts(mid_parts, out_all)
    grad_query_pre, key_acc, value_acc = attention_backward(
        query, grad_attended, lse, cosine, sine, keys, values, row_info, key_places
    )
    down_home = transpose(down_sum, stays)
    grad_branch = place_copies(stack_plan, numbers, mid_parts, (2 * rows, depth), BF)
    attended_other = send(after(attended, mid_parts[4]), OVER_C)
    *out_sum, grad_query_pre, key_acc, value_acc, down_home, grad_branch, attended_other = stage(
        *trade(out_pieces),
        grad_query_pre,
        key_acc,
        value_acc,
        down_home,
        grad_branch,
        attended_other,
    )

    out_part = (middle + added(out_sum)).astype(BF)
    out_other = send(out_part, OVER_C)
    out_mine = jnp.where(stays, out_part, out_other)
    out_away = rows_at(jnp.where(stays, out_other, out_part), c * (part // 2), part // 2)
    extras = [key_acc, value_acc]
    (give,) = product_pieces(grad_query_pre, up_q_all, extras, None, False)
    pieces = product_pieces(grad_query_pre, up_q_all, extras, send(give, OVER_C), True)
    staged = stage(
        *pieces,
        out_mine,
        send(rows_at(out_mine, c * (part // 2), part // 2), OVER_Y),
        send(out_away, OVER_X),
        send(out_away, OVER_XY),
    )
    pieces, out_parts = staged[:4], list(staged[4:])
    query_other = send(grad_query_pre, OVER_C)

    def swapped(array):
        return [(array, rows, rows, None), (array, 0, rows, None)]

    attn_slabs = weight_grads(
        numbers,
        [
            (
                [query_in],
                upq_rows,
                0,
                [
                    (at_c, [(grad_query_pre, 0, 2 * rows, None)]),
                    (at_c + 1, swapped(query_other)),
                ],
            ),
            (
                mid_parts,
                out_rows,
                0,
                [
                    (at_c, [(attended, 0, 2 * rows, None)]),
                    (at_c + 1, swapped(attended_other)),
                ],
            ),
        ],
        2 * cols,
    )
    *pieces, attn_slabs = stage(*trade(pieces), attn_slabs)
    three = added(pieces)
    attn_sum = reduce_z(after(attn_slabs, pair_sum))

    grad_plain = three[:, :latent_width] * gain_q
    plain_q_mine = plain_q[:part]
    grad_latent = inverse_q[:part] * (
        grad_plain - plain_q_mine * jnp.mean(grad_plain * plain_q_mine, axis=-1, keepdims=True)
    )
    grad_key_pre = turn(
        three[:, latent_width : latent_width + HD], cosine[:part], -sine[:part]
    )
    lat_parts = spread(
        jnp.concatenate(
            [grad_latent, grad_key_pre, three[:, latent_width + HD :]], axis=1
        ).astype(BF)
    )
    *lat_parts, pair_sum = stage(*lat_parts, pair_sum)
    pair_home = transpose(pair_sum, stays)
    lat_parts = lat_parts + over_core(lat_parts)

    lane = wide // 4
    first_slabs = weight_grads(
        numbers,
        [([normed], 256, at_x, [(None, [(p, 0, part, at_t) for p in lat_parts])])],
        lane,
    )
    first_slabs, pair_home, *lat_parts = stage(first_slabs, pair_home, *lat_parts)
    grad_lat = place_copies(stack_plan, numbers, lat_parts, (2 * rows, wide), BF)
    grad_tokens = input_gradient(numbers, grad_lat, first_all, grad_branch, tokens, gain_one)

    out_parts = out_parts + over_core(out_parts[1:])

    def out_plan(n, ins, out):
        listed = []
        for f in range(4):
            row = n[at_quarter + f] * part
            if f == 0:
                to = out.at[pl.ds(pl.multiple_of(row, part), part)]
                listed.append((None, ins[0], to))
                continue
            for j in range(2):
                at = pl.multiple_of(row + n[at_c + j] * (part // 2), part // 2)
                listed.append((None, ins[f + 3 * j], out.at[pl.ds(at, part // 2)]))
        return listed

    result = place_copies(out_plan, numbers, out_parts, (rows, depth), BF)
    grad_down_w = down_home.astype(F32)
    pair_home = pair_home.astype(F32)
    grad_gate_w, grad_up_w = pair_home[:256], pair_home[256:]

    two_sum = jnp.sum(gate_w.astype(F32) * grad_gate_w + up_w.astype(F32) * grad_up_w, axis=1)
    dev = z * 2 + x
    block = depth // 8
    own_one = lax.dynamic_slice_in_dim(gain_one, dev * block, block).reshape(-1, 1)
    own_two = lax.dynamic_slice_in_dim(gain_two, dev * block, block)
    own_q = lax.dynamic_slice_in_dim(gain_q, dev * upq_rows, upq_rows)
    own_one, own_two, own_q, two_sum = stage(own_one, own_two, own_q, two_sum)
    *first_got, grad_tokens, result, two_sum, grad_gate_w, grad_up_w, grad_down_w = stage(
        *trade_z(first_slabs), grad_tokens, result, two_sum, grad_gate_w, grad_up_w, grad_down_w
    )
    first_quarter = added(first_got).astype(BF)
    quarters = [first_quarter] + [send(first_quarter, p) for p in (OVER_C, OVER_Y, OVER_YC)]
    attn_home = transpose(after(attn_sum, first_quarter), stays)
    *quarters, attn_home = stage(*quarters, attn_home)
    attn_home = attn_home.astype(F32)
    grad_up_q, grad_out_w = attn_home[:upq_rows], attn_home[upq_rows:]
    q_sum = jnp.sum(up_q.astype(F32) * grad_up_q, axis=1)
    small = jnp.concatenate([two_sum, q_sum]).reshape(3, -1)
    small = small + send(small, OVER_C) + send(small, OVER_Y) + send(small, OVER_YC)
    small = small.reshape(-1)
    grad_down_q, grad_key_w, grad_value_w, grad_gain_one = first_finish(
        numbers, quarters, first_w, own_one, latent_width
    )
    grad_gain_two = small[:block] / own_two
    grad_gain_q = small[block:] / own_q

    return (
        result,
        grad_tokens,
        grad_gain_one,
        grad_down_q,
        grad_gain_q,
        grad_up_q,
        grad_key_w,
        grad_value_w,
        grad_out_w,
        grad_gain_two,
        grad_gate_w,
        grad_up_w,
        grad_down_w,
    )


def rows_at(array, start, count):
    return lax.dynamic_slice_in_dim(array, start, count, axis=0)


def rotate(array, places):
    half = array.shape[-1] // 2
    freqs = 10000.0 ** (-jnp.arange(half, dtype=jnp.float32) / half)
    angles = places[:, None] * freqs[None, :]
    cosine = jnp.cos(angles)
    sine = jnp.sin(angles)
    first = array[..., :half]
    latter = array[..., half:]
    return jnp.concatenate(
        [first * cosine - latter * sine, latter * cosine + first * sine], axis=-1
    )


def forward(token_rows, attention_w, ffn_w, gains, own_pos, allowed):
    gain_one, gain_q, gain_two = gains
    down_q, up_q, key_w, value_w, out_w = attention_w
    gate_w, up_w, down_w = ffn_w
    row_count = token_rows.shape[0]
    heads = up_q.shape[1] // HD
    scale = HD ** (-0.5)
    plain_one, inverse_one = rms_parts(token_rows)
    normed = (plain_one * gain_one).astype(jnp.bfloat16)
    latent = jnp.dot(normed, down_q, preferred_element_type=jnp.float32)
    plain_q, inverse_q = rms_parts(latent)
    query_in = (plain_q * gain_q).astype(jnp.bfloat16)
    query_pre = jnp.dot(query_in, up_q, preferred_element_type=jnp.float32)
    query = rotate(query_pre.reshape(row_count, heads, HD).transpose(1, 0, 2), own_pos).astype(
        jnp.bfloat16
    )
    keys = rotate(jnp.dot(normed, key_w, preferred_element_type=jnp.float32), own_pos).astype(
        jnp.bfloat16
    )
    values = jnp.dot(normed, value_w, preferred_element_type=jnp.float32).astype(jnp.bfloat16)
    keys_all, values_all = (
        lax.all_gather(keys, "ctx", axis=0, tiled=True),
        lax.all_gather(values, "ctx", axis=0, tiled=True),
    )

    def one_head(q_head):
        scores = jnp.where(allowed, times_trans(q_head, keys_all) * scale, -1e30)
        largest = jnp.max(scores, axis=-1, keepdims=True)
        exponent = jnp.exp(scores - largest)
        totals = jnp.sum(exponent, axis=-1, keepdims=True)
        soft = (exponent / totals).astype(jnp.bfloat16)
        return (
            jnp.dot(soft, values_all, preferred_element_type=jnp.float32),
            (largest + jnp.log(totals))[:, 0],
        )

    mixed_heads, log_totals = lax.map(one_head, query)
    attended = mixed_heads.transpose(1, 0, 2).reshape(row_count, heads * HD).astype(jnp.bfloat16)
    branch = lax.psum(times_trans(attended, out_w), "tensor")
    middle = token_rows + branch
    plain_two, inverse_two = rms_parts(middle)
    normed_two = (plain_two * gain_two).astype(jnp.bfloat16)
    gate_pre = jnp.dot(normed_two, gate_w, preferred_element_type=jnp.float32)
    up_pre = jnp.dot(normed_two, up_w, preferred_element_type=jnp.float32)
    hidden = (jax.nn.silu(gate_pre) * up_pre).astype(jnp.bfloat16)
    result = middle + lax.psum(times_trans(hidden, down_w).astype(jnp.bfloat16), "tensor").astype(
        jnp.float32
    )
    kept_values = (
        plain_one,
        inverse_one,
        normed,
        plain_q,
        inverse_q,
        query_in,
        query,
        keys_all,
        values_all,
        log_totals,
        attended,
        plain_two,
        inverse_two,
        normed_two,
        gate_pre,
        up_pre,
        hidden,
    )
    return (result, kept_values)


def backward(cotangent, attention_w, ffn_w, gains, own_pos, allowed, kept_values):
    gain_one, gain_q, gain_two = gains
    down_q, up_q, key_w, value_w, out_w = attention_w
    gate_w, up_w, down_w = ffn_w
    (
        plain_one,
        inverse_one,
        normed,
        plain_q,
        inverse_q,
        query_in,
        query,
        keys_all,
        values_all,
        log_totals,
        attended,
        plain_two,
        inverse_two,
        normed_two,
        gate_pre,
        up_pre,
        hidden,
    ) = kept_values
    row_count = cotangent.shape[0]
    heads = query.shape[0]
    scale = HD ** (-0.5)
    grad_down = trans_times(cotangent, hidden)
    grad_hidden = jnp.dot(cotangent, down_w, preferred_element_type=jnp.float32)
    sigma = jax.nn.sigmoid(gate_pre)
    grad_gate = (grad_hidden * up_pre * sigma * (1.0 + gate_pre * (1.0 - sigma))).astype(
        jnp.bfloat16
    )
    grad_up = (grad_hidden * gate_pre * sigma).astype(jnp.bfloat16)
    grad_gate_w = trans_times(normed_two, grad_gate)
    grad_up_w = trans_times(normed_two, grad_up)
    grad_norm_two = lax.psum(times_trans(grad_gate, gate_w) + times_trans(grad_up, up_w), "tensor")
    grad_mid_part, grad_gain_two = rms_back(grad_norm_two, plain_two, inverse_two, gain_two)
    ffn_grads = (
        lax.psum_scatter(grad_gate_w, ("dp", "ctx"), scatter_dimension=0, tiled=True),
        lax.psum_scatter(grad_up_w, ("dp", "ctx"), scatter_dimension=0, tiled=True),
        lax.psum_scatter(grad_down, ("dp", "ctx"), scatter_dimension=0, tiled=True),
        lax.psum_scatter(grad_gain_two, ("dp", "ctx"), scatter_dimension=0, tiled=True),
    )
    grad_middle = cotangent.astype(jnp.float32) + grad_mid_part
    grad_branch = grad_middle.astype(jnp.bfloat16)
    grad_out_w = trans_times(grad_branch, attended)
    grad_attended = jnp.dot(grad_branch, out_w, preferred_element_type=jnp.float32).astype(
        jnp.bfloat16
    )
    grad_heads = grad_attended.reshape(row_count, heads, HD).transpose(1, 0, 2)

    def head_back(carry, item):
        key_acc, value_acc = carry
        q_head, grad_head, lse_head = item
        scores = jnp.where(allowed, times_trans(q_head, keys_all) * scale, -1e30)
        soft = jnp.exp(scores - lse_head[:, None])
        grad_soft = times_trans(grad_head, values_all)
        inner = jnp.sum(soft * grad_soft, axis=-1, keepdims=True)
        grad_scores = (soft * (grad_soft - inner)).astype(jnp.bfloat16)
        grad_q = jnp.dot(grad_scores, keys_all, preferred_element_type=jnp.float32) * scale
        key_acc = key_acc + trans_times(grad_scores, q_head) * scale
        value_acc = value_acc + trans_times(soft.astype(jnp.bfloat16), grad_head)
        return ((key_acc, value_acc), grad_q)

    empty = jnp.zeros(keys_all.shape, jnp.float32)
    (key_total, value_total), grad_query = lax.scan(
        head_back, (empty, empty), (query, grad_heads, log_totals)
    )
    key_own, value_own = (
        lax.psum_scatter(key_total, "ctx", scatter_dimension=0, tiled=True),
        lax.psum_scatter(value_total, "ctx", scatter_dimension=0, tiled=True),
    )
    grad_query_pre = (
        rotate(grad_query, -own_pos)
        .transpose(1, 0, 2)
        .reshape(row_count, heads * HD)
        .astype(jnp.bfloat16)
    )
    grad_up_q = trans_times(query_in, grad_query_pre)
    grad_qin_part = times_trans(grad_query_pre, up_q)
    grad_qin, grad_keys_rot, grad_values = lax.psum((grad_qin_part, key_own, value_own), "tensor")
    grad_key_pre = rotate(grad_keys_rot, -own_pos).astype(jnp.bfloat16)
    grad_value_low = grad_values.astype(jnp.bfloat16)
    grad_latent, grad_gain_q = rms_back(grad_qin, plain_q, inverse_q, gain_q)
    grad_latent_low = grad_latent.astype(jnp.bfloat16)
    grad_down_q = trans_times(normed, grad_latent_low)
    grad_key_w = trans_times(normed, grad_key_pre)
    grad_value_w = trans_times(normed, grad_value_low)
    grad_norm_one = (
        times_trans(grad_latent_low, down_q)
        + times_trans(grad_key_pre, key_w)
        + times_trans(grad_value_low, value_w)
    )
    grad_in_part, grad_gain_one = rms_back(grad_norm_one, plain_one, inverse_one, gain_one)
    grad_tokens = grad_middle + grad_in_part
    attention_grads = (
        lax.psum_scatter(grad_gain_one, ("dp", "ctx"), scatter_dimension=0, tiled=True),
        lax.psum_scatter(grad_down_q, ("dp", "ctx"), scatter_dimension=0, tiled=True),
        lax.psum_scatter(grad_gain_q, ("dp", "ctx"), scatter_dimension=0, tiled=True),
        lax.psum_scatter(grad_up_q, ("dp", "ctx"), scatter_dimension=0, tiled=True),
        lax.psum_scatter(grad_key_w, ("dp", "ctx"), scatter_dimension=0, tiled=True),
        lax.psum_scatter(grad_value_w, ("dp", "ctx"), scatter_dimension=0, tiled=True),
        lax.psum_scatter(grad_out_w, ("dp", "ctx"), scatter_dimension=0, tiled=True),
    )
    return (grad_tokens, attention_grads, ffn_grads)


def per_device(
    tokens_in,
    cotangent,
    seq_lengths,
    block_order,
    gain_one,
    down_q,
    gain_q,
    up_q,
    key_w,
    value_w,
    out_w,
    gain_two,
    gate_w,
    up_w,
    down_w,
):
    token_rows = tokens_in.astype(jnp.float32)
    row_count = tokens_in.shape[0]
    block_rows = row_count // 2
    places = (
        block_order[0][:, :, None] * block_rows
        + jnp.arange(block_rows, dtype=jnp.int32)[None, None, :]
    ).reshape(-1)
    second = (places >= seq_lengths[0, 0]).astype(jnp.int32)
    in_sequence = places - second * seq_lengths[0, 0]
    start = lax.axis_index("ctx") * row_count
    own_places = lax.dynamic_slice_in_dim(places, start, row_count)
    own_second = lax.dynamic_slice_in_dim(second, start, row_count)
    own_pos = lax.dynamic_slice_in_dim(in_sequence, start, row_count).astype(jnp.float32)
    allowed = (own_second[:, None] == second[None, :]) & (places[None, :] <= own_places[:, None])
    gains = (gain_one, gain_q, gain_two)
    attention_w = (
        lax.all_gather(down_q, ("dp", "ctx"), axis=0, tiled=True),
        lax.all_gather(up_q, ("dp", "ctx"), axis=0, tiled=True),
        lax.all_gather(key_w, ("dp", "ctx"), axis=0, tiled=True),
        lax.all_gather(value_w, ("dp", "ctx"), axis=0, tiled=True),
        lax.all_gather(out_w, ("dp", "ctx"), axis=0, tiled=True),
    )
    ffn_w = (
        lax.all_gather(gate_w, ("dp", "ctx"), axis=0, tiled=True),
        lax.all_gather(up_w, ("dp", "ctx"), axis=0, tiled=True),
        lax.all_gather(down_w, ("dp", "ctx"), axis=0, tiled=True),
    )
    result, kept_values = forward(token_rows, attention_w, ffn_w, gains, own_pos, allowed)
    attention_w = (
        lax.all_gather(down_q, ("dp", "ctx"), axis=0, tiled=True),
        lax.all_gather(up_q, ("dp", "ctx"), axis=0, tiled=True),
        lax.all_gather(key_w, ("dp", "ctx"), axis=0, tiled=True),
        lax.all_gather(value_w, ("dp", "ctx"), axis=0, tiled=True),
        lax.all_gather(out_w, ("dp", "ctx"), axis=0, tiled=True),
    )
    ffn_w = (
        lax.all_gather(gate_w, ("dp", "ctx"), axis=0, tiled=True),
        lax.all_gather(up_w, ("dp", "ctx"), axis=0, tiled=True),
        lax.all_gather(down_w, ("dp", "ctx"), axis=0, tiled=True),
    )
    unused, kept_values = forward(token_rows, attention_w, ffn_w, gains, own_pos, allowed)
    grad_tokens, attention_grads, ffn_grads = backward(
        cotangent, attention_w, ffn_w, gains, own_pos, allowed, kept_values
    )
    grad_gain_one, grad_down_q, grad_gain_q, grad_up_q, grad_key_w, grad_value_w, grad_out_w = (
        attention_grads
    )
    grad_gate_w, grad_up_w, grad_down_w, grad_gain_two = ffn_grads
    return (
        result.astype(jnp.bfloat16),
        grad_tokens,
        grad_gain_one,
        grad_down_q,
        grad_gain_q,
        grad_up_q,
        grad_key_w,
        grad_value_w,
        grad_out_w,
        grad_gain_two,
        grad_gate_w,
        grad_up_w,
        grad_down_w,
    )


def solution(mesh):
    fast = dict(mesh.shape) == {"dp": 4, "ctx": 2, "tensor": 4}
    return jax.shard_map(
        fast_device if fast else per_device,
        mesh=mesh,
        in_specs=(
            P(("dp", "ctx"), None),
            P(("dp", "ctx"), None),
            P("dp", None),
            P("dp", None, None),
            P(),
            P(("dp", "ctx"), None),
            P(),
            P(("dp", "ctx"), "tensor"),
            P(("dp", "ctx"), None),
            P(("dp", "ctx"), None),
            P(("dp", "ctx"), "tensor"),
            P(),
            P(("dp", "ctx"), "tensor"),
            P(("dp", "ctx"), "tensor"),
            P(("dp", "ctx"), "tensor"),
        ),
        out_specs=(
            P(("dp", "ctx"), None),
            P(("dp", "ctx"), None),
            P(("dp", "ctx")),
            P(("dp", "ctx"), None),
            P(("dp", "ctx")),
            P(("dp", "ctx"), "tensor"),
            P(("dp", "ctx"), None),
            P(("dp", "ctx"), None),
            P(("dp", "ctx"), "tensor"),
            P(("dp", "ctx")),
            P(("dp", "ctx"), "tensor"),
            P(("dp", "ctx"), "tensor"),
            P(("dp", "ctx"), "tensor"),
        ),
        check_vma=False,
    )
```
